32 devices in a mesh: rows: 4 (over z), cols: 8 (over y, x, core).
Axes of the slice: x: 2, y: 2, z: 4, core: 2. Of those that a mesh axis runs over, the one named last changes fastest.
Arguments:
- tokens: bfloat16 [32, 1024, 768], P('rows', 'cols'), may hold values from -6 to 6
- segment_ids: int32 [32, 1024], P('rows'), may hold values from 0 to 3, never falling along the last dimension, each value on 1 to 768 neighbouring positions
- cotangent: bfloat16 [32, 1024, 768], P('rows', 'cols'), may hold values from -6 to 6
- w_qkv: bfloat16 [768, 2304], replicated, may hold values from -0.21875 to 0.21875
- q_bias: float32 [768], replicated, may hold values from -1.2 to 1.2
- v_bias: float32 [768], replicated, may hold values from -1.2 to 1.2
- w_out: bfloat16 [768, 768], replicated, may hold values from -1.75 to 1.75
- out_bias: float32 [768], replicated, may hold values from -1.2 to 1.2
- attn_gain: float32 [768], replicated, may hold values from 0.5 to 1.5
- attn_shift: float32 [768], replicated, may hold values from -1.2 to 1.2
- mlp_gain: float32 [768], replicated, may hold values from 0.5 to 1.5
- mlp_shift: float32 [768], replicated, may hold values from -1.2 to 1.2
- w_up: bfloat16 [768, 3072], replicated, may hold values from -0.21875 to 0.21875
- up_bias: float32 [3072], replicated, may hold values from -1.2 to 1.2
- w_down: bfloat16 [3072, 768], replicated, may hold values from -0.109375 to 0.109375
- down_bias: float32 [768], replicated, may hold values from -1.2 to 1.2
Outputs:
- output: bfloat16 [32, 1024, 768], P('rows', 'cols')
- grad_tokens: float32 [32, 1024, 768], P('rows', 'cols')
- grad_w_qkv: float32 [768, 2304], replicated
- grad_q_bias: float32 [768], replicated
- grad_v_bias: float32 [768], replicated
- grad_w_out: float32 [768, 768], replicated
- grad_out_bias: float32 [768], replicated
- grad_attn_gain: float32 [768], replicated
- grad_attn_shift: float32 [768], replicated
- grad_mlp_gain: float32 [768], replicated
- grad_mlp_shift: float32 [768], replicated
- grad_w_up: float32 [768, 3072], replicated
- grad_up_bias: float32 [3072], replicated
- grad_w_down: float32 [3072, 768], replicated
- grad_down_bias: float32 [768], replicated
The draws below stay inside these ranges and needn't reach their ends.
Inputs may be any that keep to these rules, and one draw needn't show every extreme that they name: `segment_ids`: along each stored sequence the ids never fall; each document is a run of slots.
All inputs are finite; a program needn't handle non-finite values.
Results may differ from the reference program's by a relative error of at most 0.012.
Values may be sent and summed in bfloat16 or wider, within the bound.
A program may use at most 384 MiB of HBM per device.

```python
import math
from functools import partial
import jax
import jax.numpy as jnp
import numpy as np
from jax import lax

D = 768
HEADS = 12
HDIM = 64
FF = 3072
LEN = 1024
DOCS = 4
SEQS = 32


def steps_of(stream_key, extent, cuts, low, top_value):
    gain, own = 1.0, jax.random.fold_in(stream_key, 6)
    for position, parts in cuts:
        steps = jnp.exp(jax.random.uniform(jax.random.fold_in(own, position), (parts,), jnp.float32, low / len(cuts), top_value / len(cuts)))
        gain = gain * jnp.repeat(steps, extent[position] // parts).reshape([-1 if axis == position else 1 for axis in range(len(extent))])
    return gain


def split_up(count, total, most, lean):
    weights = [(1 << 20) // math.isqrt(standing ** lean) + 1 for standing in range(2, count + 1)]
    surplus, holding = total - most - (count - 1), [1] * (count - 1)
    while surplus > 0:
        candidates = [i for i in range(count - 1) if holding[i] < most]
        pool, left = sum([weights[i] for i in candidates]), surplus
        for i in candidates:
            extra = min(most - holding[i], max(1, left * weights[i] // pool), surplus)
            holding[i] = holding[i] + extra
            surplus = surplus - extra
    return np.array([most] + holding)


def uneven(rng, count, total, bound, lean):
    if count == 2:
        one = jax.random.randint(rng, (), max(1, total - bound), min(bound, total - 1) + 1)
        return jnp.stack([one, total - one])
    lengths = jnp.asarray(split_up(count, total, bound, lean), jnp.int32)
    pairs = (count - 1) // 2
    giver, sink = lengths[1:1 + 2 * pairs:2], lengths[2:2 + 2 * pairs:2]
    room = jnp.minimum(giver - 1, bound - sink)
    shifted = jax.random.randint(jax.random.fold_in(rng, 1), (pairs,), 0, 1 << 20) % (room + 1)
    lengths = lengths.at[1:1 + 2 * pairs:2].set(giver - shifted).at[2:2 + 2 * pairs:2].set(sink + shifted)
    return lengths[jax.random.permutation(jax.random.fold_in(rng, 2), count)]


def centred(rng, dims, deviation, reach, shards=(), kind=jnp.bfloat16):
    entries = deviation * jax.random.normal(rng, dims, jnp.float32)
    if shards:
        entries = entries * steps_of(rng, dims, shards, -0.22, 0.18)
    return jnp.clip(entries, -reach, reach).astype(kind)


def setup_inputs(seed: int = 0) -> dict:
    seeds = jax.random.split(jax.random.key(seed), 17)
    tokens = centred(seeds[0], (SEQS, LEN, D), 1.0, 6.0, ((0, 4), (1, 8)))
    segment_ids = jax.vmap(lambda own: jnp.searchsorted(jnp.cumsum(uneven(own, DOCS, LEN, 3 * LEN // 4, 2)), jnp.arange(LEN), side="right"))(jax.random.split(seeds[1], SEQS)).reshape((SEQS, LEN)).astype(jnp.int32)
    cotangent = centred(seeds[2], (SEQS, LEN, D), 1.0, 6.0, ((0, 4), (1, 8)))
    w_qkv = centred(seeds[3], (D, 3 * D), D ** -0.5, 0.21875)
    q_bias = centred(seeds[4], (D,), 0.2, 1.2, (), jnp.float32)
    v_bias = centred(seeds[5], (D,), 0.2, 1.2, (), jnp.float32)
    w_out = centred(seeds[6], (D, D), (D // 64) ** -0.5, 1.75)
    out_bias = centred(seeds[7], (D,), 0.2, 1.2, (), jnp.float32)
    attn_gain = jnp.clip(1.0 + 0.1 * jax.random.normal(seeds[8], (D,), jnp.float32), 0.5, 1.5)
    attn_shift = centred(seeds[9], (D,), 0.2, 1.2, (), jnp.float32)
    mlp_gain = jnp.clip(1.0 + 0.1 * jax.random.normal(seeds[10], (D,), jnp.float32), 0.5, 1.5)
    mlp_shift = centred(seeds[11], (D,), 0.2, 1.2, (), jnp.float32)
    w_up = centred(seeds[12], (D, FF), D ** -0.5, 0.21875)
    up_bias = centred(seeds[13], (FF,), 0.2, 1.2, (), jnp.float32)
    w_down = centred(seeds[14], (FF, D), FF ** -0.5, 0.109375)
    down_bias = centred(seeds[15], (D,), 0.2, 1.2, (), jnp.float32)
    return dict(tokens=tokens, segment_ids=segment_ids, cotangent=cotangent, w_qkv=w_qkv, q_bias=q_bias, v_bias=v_bias, w_out=w_out, out_bias=out_bias, attn_gain=attn_gain, attn_shift=attn_shift, mlp_gain=mlp_gain, mlp_shift=mlp_shift, w_up=w_up, up_bias=up_bias, w_down=w_down, down_bias=down_bias)


@jax.custom_vjp
def low(v):
    return lax.optimization_barrier(v.astype(jnp.bfloat16)).astype(jnp.float32)

@jax.custom_vjp
def low_back(v):
    return v

def low_keep(v):
    return (low(v), None)

def low_pass(kept, grad):
    return (grad,)

def back_keep(v):
    return (v, None)

def back_low(kept, grad):
    return (low(grad),)
low.defvjp(low_keep, low_pass)
low_back.defvjp(back_keep, back_low)

def matmul(left_side, right_side):
    return jnp.matmul(left_side, right_side, precision=lax.Precision.HIGHEST)

def norm_rows(values, gain_vec, shift_vec):
    average = lax.optimization_barrier(jnp.mean(values, axis=-1, keepdims=True))
    centered = values - average
    variance = lax.optimization_barrier(jnp.mean(centered * centered, axis=-1, keepdims=True))
    return centered * lax.rsqrt(variance + 1e-05) * gain_vec + shift_vec

def score_block(query_row, key_row, value_row, segment_row):
    length = query_row.shape[0]
    query_heads = query_row.reshape(length, HEADS, HDIM)
    key_heads = key_row.reshape(length, HEADS, HDIM)
    value_heads = value_row.reshape(length, HEADS, HDIM)
    scores = jnp.einsum('ihd,jhd->hij', query_heads, key_heads, precision=lax.Precision.HIGHEST) * HDIM ** (-0.5)
    scores = low_back(scores)
    positions = jnp.arange(length, dtype=jnp.int32)
    same_doc = segment_row[:, None] == segment_row[None, :]
    allowed = same_doc & (positions[:, None] <= positions[None, :])
    doc_starts = jnp.concatenate([segment_row[:-1] != segment_row[1:], jnp.ones((1,), dtype=bool)])
    picked = same_doc & (positions[:, None] < positions[None, :]) & jnp.logical_not(doc_starts)[None, :]
    selected = jnp.where(picked, jax.nn.relu(scores[0]), 0.0)
    carried = lax.cumsum(selected, axis=0, reverse=True) - selected
    logits = jnp.where(allowed[None], scores - 8.0 / LEN * carried[None], -1e+30)
    row_peak = lax.optimization_barrier(jnp.max(logits, axis=2, keepdims=True))
    expon = jnp.where(allowed[None], jnp.exp(logits - row_peak), 0.0)
    probs = low(expon / lax.optimization_barrier(jnp.sum(expon, axis=2, keepdims=True)))
    mixed = jnp.einsum('hij,jhd->ihd', probs, value_heads, precision=lax.Precision.HIGHEST)
    return mixed.reshape(length, HEADS * HDIM)

def attend_item(item_tuple):
    return jax.checkpoint(score_block)(item_tuple[0], item_tuple[1], item_tuple[2], item_tuple[3])

def layer(segment_ids, tokens, w_qkv, q_bias, v_bias, w_out, out_bias, attn_gain, attn_shift, mlp_gain, mlp_shift, w_up, up_bias, w_down, down_bias):
    model_width = tokens.shape[-1]
    normed = low(norm_rows(tokens, attn_gain, attn_shift))
    projected = matmul(normed, w_qkv)
    queries = low(low_back(projected[..., :model_width] + q_bias))
    keys_all = low(low_back(projected[..., model_width:2 * model_width]))
    values_all = low(low_back(projected[..., 2 * model_width:] + v_bias))
    attended = lax.map(attend_item, (queries, keys_all, values_all, segment_ids))
    attended = low(low_back(attended))
    residual = tokens + low_back(matmul(attended, w_out) + out_bias)
    normed_two = low(norm_rows(residual, mlp_gain, mlp_shift))
    upper = low_back(matmul(normed_two, w_up) + up_bias)
    activated = low(jax.nn.gelu(upper, approximate=True))
    return residual + low_back(matmul(activated, w_down) + down_bias)

def reference(tokens, segment_ids, cotangent, w_qkv, q_bias, v_bias, w_out, out_bias, attn_gain, attn_shift, mlp_gain, mlp_shift, w_up, up_bias, w_down, down_bias):
    floats = [array_item.astype(jnp.float32) for array_item in (tokens, w_qkv, q_bias, v_bias, w_out, out_bias, attn_gain, attn_shift, mlp_gain, mlp_shift, w_up, up_bias, w_down, down_bias)]
    result, pullback = jax.vjp(partial(layer, segment_ids), *floats)
    grads = pullback(cotangent.astype(jnp.float32))
    return (result.astype(jnp.bfloat16), grads[0], grads[1], grads[2], grads[3], grads[4], grads[5], grads[6], grads[7], grads[8], grads[9], grads[10], grads[11], grads[12], grads[13])
```

```python
import jax
import jax.numpy as jnp
from jax import lax
from jax.sharding import PartitionSpec as P

HEADS = 12
HDIM = 64
BF = jnp.bfloat16
F32 = jnp.float32


def to_whole(value, copies):
    if copies > 1:
        value = jnp.repeat(value, copies, axis=0)
    return lax.all_to_all(value, "cols", 0, 1, tiled=True)


def to_parts(value, copies):
    parts = lax.all_to_all(value, "cols", 1, 0, tiled=True)
    return parts[::copies] if copies > 1 else parts


def dot(a, b, dims=((1,), (0,))):
    return lax.dot_general(a, b, (dims, ((), ())), preferred_element_type=F32)


def norm_parts(values):
    average = jnp.mean(values, axis=-1, keepdims=True)
    centered = values - average
    scale = lax.rsqrt(jnp.mean(centered * centered, axis=-1, keepdims=True) + 1e-05)
    return centered * scale, scale


def norm_back(grad, normal, scale, gain):
    weighted = grad * gain
    inner = jnp.mean(weighted * normal, axis=-1, keepdims=True)
    return scale * (weighted - jnp.mean(weighted, axis=-1, keepdims=True) - normal * inner)


def gelu_tanh(values):
    return jax.nn.gelu(values, approximate=True)


def heads_of(values):
    return values.reshape(values.shape[0], HEADS, HDIM)


def score_parts(queries, keys, segs):
    length = queries.shape[0]
    scores = jnp.einsum(
        "ihd,jhd->hij", heads_of(queries), heads_of(keys), preferred_element_type=F32
    ) * HDIM ** (-0.5)
    pos = jnp.arange(length, dtype=jnp.int32)
    starts = jnp.concatenate([segs[:-1] != segs[1:], jnp.ones((1,), dtype=bool)])
    same = segs[:, None] == segs[None, :]
    allowed = same & (pos[:, None] <= pos[None, :])
    picked = same & (pos[:, None] < pos[None, :]) & ~starts[None, :]
    selected = jnp.where(picked, jax.nn.relu(scores[0]), 0.0)
    carried = lax.cumsum(selected, axis=0, reverse=True) - selected
    logits = jnp.where(allowed[None], scores - 8.0 / length * carried[None], -1e30)
    return scores, logits, allowed, picked


def attend(queries, keys, values, segs):
    scores, logits, allowed, picked = score_parts(queries, keys, segs)
    peak = jnp.max(logits, axis=2, keepdims=True)
    expon = jnp.where(allowed[None], jnp.exp(logits - peak), 0.0)
    total = jnp.sum(expon, axis=2, keepdims=True)
    probs = (expon / total).astype(BF)
    mixed = jnp.einsum("hij,jhd->ihd", probs, heads_of(values), preferred_element_type=F32)
    return mixed.reshape(queries.shape), peak + jnp.log(total)


def attend_back(queries, keys, values, segs, stats, grad):
    length = queries.shape[0]
    scores, logits, allowed, picked = score_parts(queries, keys, segs)
    probs = jnp.where(allowed[None], jnp.exp(logits - stats), 0.0)
    grad_probs = jnp.einsum(
        "ihd,jhd->hij", heads_of(grad), heads_of(values), preferred_element_type=F32
    )
    delta = jnp.sum(probs * grad_probs, axis=2, keepdims=True)
    grad_logits = probs * (grad_probs - delta)
    grad_carried = -(8.0 / length) * jnp.sum(grad_logits, axis=0)
    grad_selected = lax.cumsum(grad_carried, axis=0) - grad_carried
    extra = jnp.where(picked & (scores[0] > 0), grad_selected, 0.0)
    grad_scores = jnp.concatenate([grad_logits[:1] + extra[None], grad_logits[1:]], 0).astype(BF)
    scale = HDIM ** (-0.5)
    dq = jnp.einsum("hij,jhd->ihd", grad_scores, heads_of(keys), preferred_element_type=F32)
    dk = jnp.einsum("hij,ihd->jhd", grad_scores, heads_of(queries), preferred_element_type=F32)
    dv = jnp.einsum("hij,ihd->jhd", probs.astype(BF), heads_of(grad), preferred_element_type=F32)
    shape = queries.shape
    return tuple(g.astype(BF).reshape(shape) for g in (dq * scale, dk * scale, dv))


def layer(tokens, segs, cotangent, weights):
    (w_qkv, q_bias, v_bias, w_out, out_bias, attn_gain, attn_shift, mlp_gain, mlp_shift,
     w_up, up_bias, w_down, down_bias) = weights
    width = tokens.shape[1]
    inputs = tokens.astype(F32)
    normal_one, scale_one = norm_parts(inputs)
    normed = (normal_one * attn_gain + attn_shift).astype(BF)
    projected = dot(normed, w_qkv)
    queries = (projected[:, :width] + q_bias).astype(BF)
    keys = projected[:, width : 2 * width].astype(BF)
    values = (projected[:, 2 * width :] + v_bias).astype(BF)
    mixed, stats = attend(queries, keys, values, segs)
    attended = mixed.astype(BF)
    residual = inputs + dot(attended, w_out) + out_bias
    normal_two, scale_two = norm_parts(residual)
    normed_two = (normal_two * mlp_gain + mlp_shift).astype(BF)
    upper = dot(normed_two, w_up) + up_bias
    act, gelu_back = jax.vjp(gelu_tanh, upper)
    act = act.astype(BF)
    output = (residual + dot(act, w_down) + down_bias).astype(BF)
    grad_top = cotangent.astype(F32)
    g_down_bias = jnp.sum(grad_top, axis=0)
    g_w_down = dot(act, cotangent, ((0,), (0,)))
    grad_upper = gelu_back(dot(cotangent, w_down, ((1,), (1,))))[0].astype(BF)
    g_up_bias = jnp.sum(grad_upper.astype(F32), axis=0)
    g_w_up = dot(normed_two, grad_upper, ((0,), (0,)))
    grad_two = dot(grad_upper, w_up, ((1,), (1,)))
    g_mlp_gain = jnp.sum(grad_two * normal_two, axis=0)
    g_mlp_shift = jnp.sum(grad_two, axis=0)
    grad_residual = grad_top + norm_back(grad_two, normal_two, scale_two, mlp_gain)
    grad_branch = grad_residual.astype(BF)
    g_out_bias = jnp.sum(grad_branch.astype(F32), axis=0)
    g_w_out = dot(attended, grad_branch, ((0,), (0,)))
    grad_attended = dot(grad_branch, w_out, ((1,), (1,))).astype(BF)
    dq, dk, dv = attend_back(queries, keys, values, segs, stats, grad_attended)
    g_q_bias = jnp.sum(dq.astype(F32), axis=0)
    g_v_bias = jnp.sum(dv.astype(F32), axis=0)
    grad_proj = jnp.concatenate([dq, dk, dv], axis=1)
    g_w_qkv = dot(normed, grad_proj, ((0,), (0,)))
    grad_one = dot(grad_proj, w_qkv, ((1,), (1,)))
    g_attn_gain = jnp.sum(grad_one * normal_one, axis=0)
    g_attn_shift = jnp.sum(grad_one, axis=0)
    grad_tokens = grad_residual + norm_back(grad_one, normal_one, scale_one, attn_gain)
    return output, grad_tokens, (
        g_w_qkv, g_q_bias, g_v_bias, g_w_out, g_out_bias, g_attn_gain, g_attn_shift,
        g_mlp_gain, g_mlp_shift, g_w_up, g_up_bias, g_w_down, g_down_bias)


def summed_grads(grads, copies):
    grads = [g / copies for g in grads] if copies > 1 else list(grads)
    matrices = [i for i, g in enumerate(grads) if g.ndim == 2]
    vectors = [i for i, g in enumerate(grads) if g.ndim == 1]
    big = lax.psum([grads[i].astype(BF) for i in matrices], ("rows", "cols"))
    small = lax.psum(jnp.concatenate([grads[i] for i in vectors]), ("rows", "cols"))
    out = [None] * len(grads)
    for i, g in zip(matrices, big):
        out[i] = g.astype(F32)
    at = 0
    for i in vectors:
        out[i] = small[at : at + grads[i].shape[0]]
        at += grads[i].shape[0]
    return out


def per_device(tokens, segment_ids, cotangent, *weights):
    seqs = tokens.shape[0]
    cols = lax.axis_size("cols")
    copies = max(1, cols // seqs)
    held = max(1, seqs // cols)
    tokens_whole = to_whole(tokens, copies)
    cotangent_whole = to_whole(cotangent, copies)
    first = (lax.axis_index("cols") // copies) * held
    segs = lax.dynamic_slice_in_dim(segment_ids, first, held, 0)
    results = [
        layer(tokens_whole[s], segs[s], cotangent_whole[s], weights) for s in range(held)
    ]
    output = jnp.stack([r[0] for r in results])
    grad_tokens = jnp.stack([r[1] for r in results])
    grads = [sum(parts[1:], parts[0]) for parts in zip(*[r[2] for r in results])]
    return (
        to_parts(output, copies),
        to_parts(grad_tokens.astype(BF), copies).astype(F32),
        *summed_grads(grads, copies),
    )


def solution(mesh):
    placed = (P("rows", "cols", None), P("rows", None), P("rows", "cols", None)) + (P(),) * 13
    return jax.shard_map(
        per_device,
        mesh=mesh,
        in_specs=placed,
        out_specs=(P("rows", "cols", None), P("rows", "cols", None)) + (P(),) * 13,
        check_vma=False,
    )
```

```python
import jax
import jax.numpy as jnp
from jax import lax
from jax.experimental import pallas as pl
from jax.experimental.pallas import tpu as pltpu
from jax.sharding import PartitionSpec as P

HEADS = 12
HDIM = 64
BF = jnp.bfloat16
F32 = jnp.float32
LOG2E = 1.4426950408889634
BIG = 1e30
BLOCK = 256


def to_whole(value, copies):
    if copies > 1:
        value = jnp.repeat(value, copies, axis=0)
    return lax.all_to_all(value, "cols", 0, 1, tiled=True)


def to_parts(value, copies):
    parts = lax.all_to_all(value, "cols", 1, 0, tiled=True)
    return parts[::copies] if copies > 1 else parts


def dot(a, b, dims=((1,), (0,))):
    return lax.dot_general(a, b, (dims, ((), ())), preferred_element_type=F32)


def norm_parts(values):
    average = jnp.mean(values, axis=-1, keepdims=True)
    centered = values - average
    scale = lax.rsqrt(jnp.mean(centered * centered, axis=-1, keepdims=True) + 1e-05)
    return centered * scale, scale


def norm_back(grad, normal, scale, gain):
    weighted = grad * gain
    inner = jnp.mean(weighted * normal, axis=-1, keepdims=True)
    return scale * (weighted - jnp.mean(weighted, axis=-1, keepdims=True) - normal * inner)


def gelu_tanh(values):
    return jax.nn.gelu(values, approximate=True)


NT=((1,),(1,))

def tri(size, upper):
    r=lax.broadcasted_iota(jnp.int32,(size,size),0); c=lax.broadcasted_iota(jnp.int32,(size,size),1)
    return jnp.where(c>r if upper else c<r, 1.0, 0.0).astype(BF)

def split_sum(mask, x):
    hi=x.astype(BF)
    lo=(x-hi.astype(F32)).astype(BF)
    return dot(mask,hi)+dot(mask,lo)

def lane_low(shape):
    return lax.broadcasted_iota(jnp.int32,shape,1) < HDIM

def attn_fwd_kernel(q_ref,k_ref,v_ref,segc_ref,segr_ref,startr_ref,o_ref,lse_ref,pen_ref):
    L=q_ref.shape[0]; nb=L//BLOCK
    scale=HDIM**-0.5
    pairs=HEADS//2
    upper=tri(BLOCK,True)
    carry=jnp.zeros((1,L),F32)
    for b in range(nb-1,-1,-1):
        i0=b*BLOCK; n=L-i0
        q0=q_ref[i0:i0+BLOCK,0:128]
        q0=jnp.where(lane_low(q0.shape),q0,jnp.zeros_like(q0))
        s=dot(q0,k_ref[i0:L,0:128],NT)*scale
        rows=i0+lax.broadcasted_iota(jnp.int32,(BLOCK,n),0)
        cols=i0+lax.broadcasted_iota(jnp.int32,(BLOCK,n),1)
        same=segc_ref[i0:i0+BLOCK,0:1]==segr_ref[0:1,i0:L]
        picked=same&(cols>rows)&(startr_ref[0:1,i0:L]==0)
        sel=jnp.where(picked,jnp.maximum(s,0.0),0.0)
        if b==nb-1: cin=jnp.zeros((1,n),F32)
        else: cin=jnp.concatenate([jnp.zeros((1,BLOCK),F32),carry],axis=1)
        carried=split_sum(upper,sel)+cin
        pen_ref[i0:i0+BLOCK,i0:L]=jnp.where(same&(cols>=rows),carried*(8.0/L*LOG2E),BIG)
        carry=cin+jnp.sum(sel,axis=0,keepdims=True)
    c=scale*LOG2E
    for b in range(nb):
        i0=b*BLOCK; n=L-i0
        def pair(p,stats,i0=i0,n=n):
            off=pl.multiple_of(p*128,128)
            q=q_ref[i0:i0+BLOCK,pl.ds(off,128)]
            k=k_ref[i0:L,pl.ds(off,128)]
            v=v_ref[i0:L,pl.ds(off,128)]
            low=lane_low(q.shape)
            outs=[]
            lane=lax.broadcasted_iota(jnp.int32,(BLOCK,128),1)
            for h in range(2):
                mine=low if h==0 else jnp.logical_not(low)
                qm=jnp.where(mine,q,jnp.zeros_like(q))
                s=dot(qm,k,NT)*c-pen_ref[i0:i0+BLOCK,i0:L]
                m=jnp.max(s,axis=1,keepdims=True)
                e=jnp.exp2(s-m).astype(BF)
                lowv=lane_low(v.shape)
                vm=jnp.where(lowv if h==0 else jnp.logical_not(lowv),v,jnp.ones_like(v))
                o=dot(e,vm)
                tot=pltpu.roll(o,HDIM,1)
                outs.append(o/tot)
                full=jnp.where(mine,tot,o)
                stats=jnp.where(lane==2*p+h,m+jnp.log2(full),stats)
            o_ref[i0:i0+BLOCK,pl.ds(off,128)]=jnp.where(low,outs[0],outs[1]).astype(BF)
            return stats
        lse_ref[i0:i0+BLOCK,:]=lax.fori_loop(0,pairs,pair,jnp.zeros((BLOCK,128),F32))

def attn_fwd(q,k,v,seg):
    L,D=q.shape
    start=jnp.concatenate([(seg[:-1]!=seg[1:]).astype(jnp.int32),jnp.ones((1,),jnp.int32)])
    vm=pl.BlockSpec(memory_space=pltpu.VMEM)
    return pl.pallas_call(attn_fwd_kernel,
        out_shape=(jax.ShapeDtypeStruct((L,D),BF),jax.ShapeDtypeStruct((L,128),F32),jax.ShapeDtypeStruct((L,L),F32)),
        in_specs=[vm]*6,out_specs=(vm,)*3,
        compiler_params=pltpu.CompilerParams(vmem_limit_bytes=60*2**20),name="attn_fwd")(q,k,v,seg[:,None],seg[None,:],start[None,:])

def attn_bwd_kernel(q_ref,k_ref,v_ref,g_ref,o_ref,lse_ref,pen_ref,startr_ref,out_ref,qt,gt,dkt,dvt,dsum):
    L,D=q_ref.shape; nb=L//BLOCK
    scale=HDIM**-0.5; c=scale*LOG2E
    pairs=HEADS//2
    lower=tri(BLOCK,False)
    for p in range(pairs):
        qt[p*128:(p+1)*128,:]=q_ref[:,p*128:(p+1)*128].T
        gt[p*128:(p+1)*128,:]=g_ref[:,p*128:(p+1)*128].T
    dkt[...]=jnp.zeros_like(dkt); dvt[...]=jnp.zeros_like(dvt)
    carry=jnp.zeros((1,L),F32)
    for b in range(nb):
        i0=b*BLOCK; n=L-i0
        rowsl=slice(i0,i0+BLOCK)
        carry=carry[:,-n:]
        def head(p,h,i0=i0,n=n,rowsl=rowsl):
            static=isinstance(p,int)
            off=p*128 if static else pl.multiple_of(p*128,128)
            q=q_ref[rowsl,pl.ds(off,128)]; g=g_ref[rowsl,pl.ds(off,128)]; o=o_ref[rowsl,pl.ds(off,128)]
            k=k_ref[i0:L,pl.ds(off,128)]; v=v_ref[i0:L,pl.ds(off,128)]
            low=lane_low(q.shape); mine=low if h==0 else jnp.logical_not(low)
            qm=jnp.where(mine,q,jnp.zeros_like(q)); gm=jnp.where(mine,g,jnp.zeros_like(g))
            lane=lax.broadcasted_iota(jnp.int32,(BLOCK,128),1)
            lse=jnp.sum(jnp.where(lane==2*p+h,lse_ref[rowsl,:],0.0),axis=1,keepdims=True)
            delta=jnp.sum(gm.astype(F32)*o.astype(F32),axis=1,keepdims=True)
            s=dot(qm,k,NT)
            pr=jnp.exp2(s*c-pen_ref[rowsl,i0:L]-lse)
            dp=dot(gm,v,NT)
            ds=pr*(dp-delta)
            return s,pr,ds,off,k
        def finish(p,h,pr,ds,off,k,i0=i0,rowsl=rowsl):
            base=p*128+h*HDIM
            if not isinstance(p,int): base=pl.multiple_of(base,64)
            dsb=ds.astype(BF); prb=pr.astype(BF)
            dvt[pl.ds(base,HDIM),i0:L]+=dot(gt[pl.ds(base,HDIM),rowsl],prb)
            dkt[pl.ds(base,HDIM),i0:L]+=dot(qt[pl.ds(base,HDIM),rowsl],dsb)
            return dot(dsb,k)
        dsum[:,i0:L]=jnp.zeros((BLOCK,n),F32)
        def pair(p,carry_):
            dq=[]
            for h in range(2):
                s,pr,ds,off,k=head(p,h)
                dsum[:,i0:L]+=ds
                dq.append(finish(p,h,pr,ds,off,k))
            out_ref[rowsl,pl.ds(off,128)]=(jnp.where(lane_low(dq[0].shape),dq[0],dq[1])*scale).astype(BF)
            return carry_
        lax.fori_loop(1,pairs,pair,0)
        s,pr,ds,off,k=head(0,1)
        dsum[:,i0:L]+=ds
        dq1=finish(0,1,pr,ds,off,k)
        s,pr,ds,off,k=head(0,0)
        total=dsum[:,i0:L]+ds
        rows=i0+lax.broadcasted_iota(jnp.int32,(BLOCK,n),0)
        cols=i0+lax.broadcasted_iota(jnp.int32,(BLOCK,n),1)
        picked=(pen_ref[rowsl,i0:L]<1e29)&(cols>rows)&(startr_ref[0:1,i0:L]==0)&(s>0)
        gsel=(split_sum(lower,total)+carry)*(-8.0/L)
        carry=carry+jnp.sum(total,axis=0,keepdims=True)
        ds=ds+jnp.where(picked,gsel,0.0)
        dq0=finish(0,0,pr,ds,off,k)
        out_ref[rowsl,0:128]=(jnp.where(lane_low(dq0.shape),dq0,dq1)*scale).astype(BF)
    for p in range(pairs):
        sl=slice(p*128,(p+1)*128)
        out_ref[:,D+p*128:D+(p+1)*128]=(dkt[sl,:]*scale).T.astype(BF)
        out_ref[:,2*D+p*128:2*D+(p+1)*128]=dvt[sl,:].T.astype(BF)

def attn_bwd(q,k,v,g,o,lse,pen,seg):
    L,D=q.shape
    start=jnp.concatenate([(seg[:-1]!=seg[1:]).astype(jnp.int32),jnp.ones((1,),jnp.int32)])
    vm=pl.BlockSpec(memory_space=pltpu.VMEM)
    return pl.pallas_call(attn_bwd_kernel,
        out_shape=jax.ShapeDtypeStruct((L,3*D),BF),
        in_specs=[vm]*8,out_specs=vm,
        scratch_shapes=[pltpu.VMEM((D,L),BF),pltpu.VMEM((D,L),BF),pltpu.VMEM((D,L),F32),pltpu.VMEM((D,L),F32),pltpu.VMEM((BLOCK,L),F32)],
        compiler_params=pltpu.CompilerParams(vmem_limit_bytes=60*2**20),name="attn_bwd")(q,k,v,g,o,lse,pen,start[None,:])


def layer(tokens, segs, cotangent, weights):
    (w_qkv, q_bias, v_bias, w_out, out_bias, attn_gain, attn_shift, mlp_gain, mlp_shift,
     w_up, up_bias, w_down, down_bias) = weights
    width = tokens.shape[1]
    inputs = tokens.astype(F32)
    normal_one, scale_one = norm_parts(inputs)
    normed = (normal_one * attn_gain + attn_shift).astype(BF)
    projected = dot(normed, w_qkv)
    queries = (projected[:, :width] + q_bias).astype(BF)
    keys = projected[:, width : 2 * width].astype(BF)
    values = (projected[:, 2 * width :] + v_bias).astype(BF)
    attended, stats, penalty = attn_fwd(queries, keys, values, segs)
    residual = inputs + dot(attended, w_out) + out_bias
    normal_two, scale_two = norm_parts(residual)
    normed_two = (normal_two * mlp_gain + mlp_shift).astype(BF)
    upper = dot(normed_two, w_up) + up_bias
    act, gelu_back = jax.vjp(gelu_tanh, upper)
    act = act.astype(BF)
    output = (residual + dot(act, w_down) + down_bias).astype(BF)
    grad_top = cotangent.astype(F32)
    g_down_bias = jnp.sum(grad_top, axis=0)
    g_w_down = dot(act, cotangent, ((0,), (0,)))
    grad_upper = gelu_back(dot(cotangent, w_down, ((1,), (1,))))[0].astype(BF)
    g_up_bias = jnp.sum(grad_upper.astype(F32), axis=0)
    g_w_up = dot(normed_two, grad_upper, ((0,), (0,)))
    grad_two = dot(grad_upper, w_up, ((1,), (1,)))
    g_mlp_gain = jnp.sum(grad_two * normal_two, axis=0)
    g_mlp_shift = jnp.sum(grad_two, axis=0)
    grad_residual = grad_top + norm_back(grad_two, normal_two, scale_two, mlp_gain)
    grad_branch = grad_residual.astype(BF)
    g_out_bias = jnp.sum(grad_branch.astype(F32), axis=0)
    g_w_out = dot(attended, grad_branch, ((0,), (0,)))
    grad_attended = dot(grad_branch, w_out, ((1,), (1,))).astype(BF)
    grad_proj = attn_bwd(queries, keys, values, grad_attended, attended, stats, penalty, segs)
    bias_sums = jnp.sum(grad_proj.astype(F32), axis=0)
    g_q_bias = bias_sums[:width]
    g_v_bias = bias_sums[2 * width :]
    g_w_qkv = dot(normed, grad_proj, ((0,), (0,)))
    grad_one = dot(grad_proj, w_qkv, ((1,), (1,)))
    g_attn_gain = jnp.sum(grad_one * normal_one, axis=0)
    g_attn_shift = jnp.sum(grad_one, axis=0)
    grad_tokens = grad_residual + norm_back(grad_one, normal_one, scale_one, attn_gain)
    return output, grad_tokens, (
        g_w_qkv, g_q_bias, g_v_bias, g_w_out, g_out_bias, g_attn_gain, g_attn_shift,
        g_mlp_gain, g_mlp_shift, g_w_up, g_up_bias, g_w_down, g_down_bias)


def summed_grads(grads, copies):
    grads = [g / copies for g in grads] if copies > 1 else list(grads)
    matrices = [i for i, g in enumerate(grads) if g.ndim == 2]
    vectors = [i for i, g in enumerate(grads) if g.ndim == 1]
    big = lax.psum([grads[i].astype(BF) for i in matrices], ("rows", "cols"))
    small = lax.psum(jnp.concatenate([grads[i] for i in vectors]), ("rows", "cols"))
    out = [None] * len(grads)
    for i, g in zip(matrices, big):
        out[i] = g.astype(F32)
    at = 0
    for i in vectors:
        out[i] = small[at : at + grads[i].shape[0]]
        at += grads[i].shape[0]
    return out


def per_device(tokens, segment_ids, cotangent, *weights):
    seqs = tokens.shape[0]
    cols = lax.axis_size("cols")
    copies = max(1, cols // seqs)
    held = max(1, seqs // cols)
    tokens_whole = to_whole(tokens, copies)
    cotangent_whole = to_whole(cotangent, copies)
    first = (lax.axis_index("cols") // copies) * held
    segs = lax.dynamic_slice_in_dim(segment_ids, first, held, 0)
    results = [
        layer(tokens_whole[s], segs[s], cotangent_whole[s], weights) for s in range(held)
    ]
    output = jnp.stack([r[0] for r in results])
    grad_tokens = jnp.stack([r[1] for r in results])
    grads = [sum(parts[1:], parts[0]) for parts in zip(*[r[2] for r in results])]
    return (
        to_parts(output, copies),
        to_parts(grad_tokens.astype(BF), copies).astype(F32),
        *summed_grads(grads, copies),
    )


def solution(mesh):
    placed = (P("rows", "cols", None), P("rows", None), P("rows", "cols", None)) + (P(),) * 13
    return jax.shard_map(
        per_device,
        mesh=mesh,
        in_specs=placed,
        out_specs=(P("rows", "cols", None), P("rows", "cols", None)) + (P(),) * 13,
        check_vma=False,
    )
```

```python
import functools

import jax
import jax.numpy as jnp
from jax import lax
from jax.experimental import pallas as pl
from jax.experimental.pallas import tpu as pltpu
from jax.sharding import PartitionSpec as P

HEADS = 12
HDIM = 64
BF = jnp.bfloat16
F32 = jnp.float32
LOG2E = 1.4426950408889634
BIG = 1e30
BLOCK = 256
MESH = pl.DeviceIdType.MESH
PANEL = 768
SPLIT = 2
STEP = 48


def to_whole(value, copies):
    if copies > 1:
        value = jnp.repeat(value, copies, axis=0)
    return lax.all_to_all(value, "cols", 0, 1, tiled=True)


def to_parts(value, copies):
    parts = lax.all_to_all(value, "cols", 1, 0, tiled=True)
    return parts[::copies] if copies > 1 else parts


def dot(a, b, dims=((1,), (0,))):
    return lax.dot_general(a, b, (dims, ((), ())), preferred_element_type=F32)


def norm_parts(values):
    average = jnp.mean(values, axis=-1, keepdims=True)
    centered = values - average
    scale = lax.rsqrt(jnp.mean(centered * centered, axis=-1, keepdims=True) + 1e-05)
    return centered * scale, scale


def norm_back(grad, normal, scale, gain):
    weighted = grad * gain
    inner = jnp.mean(weighted * normal, axis=-1, keepdims=True)
    return scale * (weighted - jnp.mean(weighted, axis=-1, keepdims=True) - normal * inner)


def gelu_tanh(values):
    return jax.nn.gelu(values, approximate=True)


NT=((1,),(1,))

def tri(size, upper):
    r=lax.broadcasted_iota(jnp.int32,(size,size),0); c=lax.broadcasted_iota(jnp.int32,(size,size),1)
    return jnp.where(c>r if upper else c<r, 1.0, 0.0).astype(BF)

def split_sum(mask, x):
    hi=x.astype(BF)
    lo=(x-hi.astype(F32)).astype(BF)
    return dot(mask,hi)+dot(mask,lo)

def lane_low(shape):
    return lax.broadcasted_iota(jnp.int32,shape,1) < HDIM

def attn_fwd_kernel(q_ref,k_ref,v_ref,segc_ref,segr_ref,startr_ref,o_ref,lse_ref,pen_ref):
    L=q_ref.shape[0]; nb=L//BLOCK
    scale=HDIM**-0.5
    pairs=HEADS//2
    upper=tri(BLOCK,True)
    carry=jnp.zeros((1,L),F32)
    for b in range(nb-1,-1,-1):
        i0=b*BLOCK; n=L-i0
        q0=q_ref[i0:i0+BLOCK,0:128]
        q0=jnp.where(lane_low(q0.shape),q0,jnp.zeros_like(q0))
        s=dot(q0,k_ref[i0:L,0:128],NT)*scale
        rows=i0+lax.broadcasted_iota(jnp.int32,(BLOCK,n),0)
        cols=i0+lax.broadcasted_iota(jnp.int32,(BLOCK,n),1)
        same=segc_ref[i0:i0+BLOCK,0:1]==segr_ref[0:1,i0:L]
        picked=same&(cols>rows)&(startr_ref[0:1,i0:L]==0)
        sel=jnp.where(picked,jnp.maximum(s,0.0),0.0)
        if b==nb-1: cin=jnp.zeros((1,n),F32)
        else: cin=jnp.concatenate([jnp.zeros((1,BLOCK),F32),carry],axis=1)
        carried=split_sum(upper,sel)+cin
        pen_ref[i0:i0+BLOCK,i0:L]=jnp.where(same&(cols>=rows),carried*(8.0/L*LOG2E),BIG)
        carry=cin+jnp.sum(sel,axis=0,keepdims=True)
    c=scale*LOG2E
    for b in range(nb):
        i0=b*BLOCK; n=L-i0
        def pair(p,stats,i0=i0,n=n):
            off=pl.multiple_of(p*128,128)
            q=q_ref[i0:i0+BLOCK,pl.ds(off,128)]
            k=k_ref[i0:L,pl.ds(off,128)]
            v=v_ref[i0:L,pl.ds(off,128)]
            low=lane_low(q.shape)
            outs=[]
            lane=lax.broadcasted_iota(jnp.int32,(BLOCK,128),1)
            for h in range(2):
                mine=low if h==0 else jnp.logical_not(low)
                qm=jnp.where(mine,q,jnp.zeros_like(q))
                s=dot(qm,k,NT)*c-pen_ref[i0:i0+BLOCK,i0:L]
                m=jnp.max(s,axis=1,keepdims=True)
                e=jnp.exp2(s-m).astype(BF)
                lowv=lane_low(v.shape)
                vm=jnp.where(lowv if h==0 else jnp.logical_not(lowv),v,jnp.ones_like(v))
                o=dot(e,vm)
                tot=pltpu.roll(o,HDIM,1)
                outs.append(o/tot)
                full=jnp.where(mine,tot,o)
                stats=jnp.where(lane==2*p+h,m+jnp.log2(full),stats)
            o_ref[i0:i0+BLOCK,pl.ds(off,128)]=jnp.where(low,outs[0],outs[1]).astype(BF)
            return stats
        lse_ref[i0:i0+BLOCK,:]=lax.fori_loop(0,pairs,pair,jnp.zeros((BLOCK,128),F32))

def attn_fwd(q,k,v,seg):
    L,D=q.shape
    start=jnp.concatenate([(seg[:-1]!=seg[1:]).astype(jnp.int32),jnp.ones((1,),jnp.int32)])
    vm=pl.BlockSpec(memory_space=pltpu.VMEM)
    return pl.pallas_call(attn_fwd_kernel,
        out_shape=(jax.ShapeDtypeStruct((L,D),BF),jax.ShapeDtypeStruct((L,128),F32),jax.ShapeDtypeStruct((L,L),F32)),
        in_specs=[vm]*6,out_specs=(vm,)*3,
        compiler_params=pltpu.CompilerParams(vmem_limit_bytes=60*2**20),name="attn_fwd")(q,k,v,seg[:,None],seg[None,:],start[None,:])

def attn_bwd_kernel(q_ref,k_ref,v_ref,g_ref,o_ref,lse_ref,pen_ref,startr_ref,out_ref,qt,gt,dkt,dvt,dsum):
    L,D=q_ref.shape; nb=L//BLOCK
    scale=HDIM**-0.5; c=scale*LOG2E
    pairs=HEADS//2
    lower=tri(BLOCK,False)
    for p in range(pairs):
        qt[p*128:(p+1)*128,:]=q_ref[:,p*128:(p+1)*128].T
        gt[p*128:(p+1)*128,:]=g_ref[:,p*128:(p+1)*128].T
    dkt[...]=jnp.zeros_like(dkt); dvt[...]=jnp.zeros_like(dvt)
    carry=jnp.zeros((1,L),F32)
    for b in range(nb):
        i0=b*BLOCK; n=L-i0
        rowsl=slice(i0,i0+BLOCK)
        carry=carry[:,-n:]
        def head(p,h,i0=i0,n=n,rowsl=rowsl):
            static=isinstance(p,int)
            off=p*128 if static else pl.multiple_of(p*128,128)
            q=q_ref[rowsl,pl.ds(off,128)]; g=g_ref[rowsl,pl.ds(off,128)]; o=o_ref[rowsl,pl.ds(off,128)]
            k=k_ref[i0:L,pl.ds(off,128)]; v=v_ref[i0:L,pl.ds(off,128)]
            low=lane_low(q.shape); mine=low if h==0 else jnp.logical_not(low)
            qm=jnp.where(mine,q,jnp.zeros_like(q)); gm=jnp.where(mine,g,jnp.zeros_like(g))
            lane=lax.broadcasted_iota(jnp.int32,(BLOCK,128),1)
            lse=jnp.sum(jnp.where(lane==2*p+h,lse_ref[rowsl,:],0.0),axis=1,keepdims=True)
            delta=jnp.sum(gm.astype(F32)*o.astype(F32),axis=1,keepdims=True)
            s=dot(qm,k,NT)
            pr=jnp.exp2(s*c-pen_ref[rowsl,i0:L]-lse)
            dp=dot(gm,v,NT)
            ds=pr*(dp-delta)
            return s,pr,ds,off,k
        def finish(p,h,pr,ds,off,k,i0=i0,rowsl=rowsl):
            base=p*128+h*HDIM
            if not isinstance(p,int): base=pl.multiple_of(base,64)
            dsb=ds.astype(BF); prb=pr.astype(BF)
            dvt[pl.ds(base,HDIM),i0:L]+=dot(gt[pl.ds(base,HDIM),rowsl],prb)
            dkt[pl.ds(base,HDIM),i0:L]+=dot(qt[pl.ds(base,HDIM),rowsl],dsb)
            return dot(dsb,k)
        dsum[:,i0:L]=jnp.zeros((BLOCK,n),F32)
        def pair(p,carry_):
            dq=[]
            for h in range(2):
                s,pr,ds,off,k=head(p,h)
                dsum[:,i0:L]+=ds
                dq.append(finish(p,h,pr,ds,off,k))
            out_ref[rowsl,pl.ds(off,128)]=(jnp.where(lane_low(dq[0].shape),dq[0],dq[1])*scale).astype(BF)
            return carry_
        lax.fori_loop(1,pairs,pair,0)
        s,pr,ds,off,k=head(0,1)
        dsum[:,i0:L]+=ds
        dq1=finish(0,1,pr,ds,off,k)
        s,pr,ds,off,k=head(0,0)
        total=dsum[:,i0:L]+ds
        rows=i0+lax.broadcasted_iota(jnp.int32,(BLOCK,n),0)
        cols=i0+lax.broadcasted_iota(jnp.int32,(BLOCK,n),1)
        picked=(pen_ref[rowsl,i0:L]<1e29)&(cols>rows)&(startr_ref[0:1,i0:L]==0)&(s>0)
        gsel=(split_sum(lower,total)+carry)*(-8.0/L)
        carry=carry+jnp.sum(total,axis=0,keepdims=True)
        ds=ds+jnp.where(picked,gsel,0.0)
        dq0=finish(0,0,pr,ds,off,k)
        out_ref[rowsl,0:128]=(jnp.where(lane_low(dq0.shape),dq0,dq1)*scale).astype(BF)
    for p in range(pairs):
        sl=slice(p*128,(p+1)*128)
        out_ref[:,D+p*128:D+(p+1)*128]=(dkt[sl,:]*scale).T.astype(BF)
        out_ref[:,2*D+p*128:2*D+(p+1)*128]=dvt[sl,:].T.astype(BF)

def attn_bwd(q,k,v,g,o,lse,pen,seg):
    L,D=q.shape
    start=jnp.concatenate([(seg[:-1]!=seg[1:]).astype(jnp.int32),jnp.ones((1,),jnp.int32)])
    vm=pl.BlockSpec(memory_space=pltpu.VMEM)
    return pl.pallas_call(attn_bwd_kernel,
        out_shape=jax.ShapeDtypeStruct((L,3*D),BF),
        in_specs=[vm]*8,out_specs=vm,
        scratch_shapes=[pltpu.VMEM((D,L),BF),pltpu.VMEM((D,L),BF),pltpu.VMEM((D,L),F32),pltpu.VMEM((D,L),F32),pltpu.VMEM((BLOCK,L),F32)],
        compiler_params=pltpu.CompilerParams(vmem_limit_bytes=60*2**20),name="attn_bwd")(q,k,v,g,o,lse,pen,start[None,:])


def layer(tokens, segs, cotangent, weights):
    (w_qkv, q_bias, v_bias, w_out, out_bias, attn_gain, attn_shift, mlp_gain, mlp_shift,
     w_up, up_bias, w_down, down_bias) = weights
    width = tokens.shape[1]
    inputs = tokens.astype(F32)
    normal_one, scale_one = norm_parts(inputs)
    normed = (normal_one * attn_gain + attn_shift).astype(BF)
    projected = dot(normed, w_qkv)
    queries = (projected[:, :width] + q_bias).astype(BF)
    keys = projected[:, width : 2 * width].astype(BF)
    values = (projected[:, 2 * width :] + v_bias).astype(BF)
    attended, stats, penalty = attn_fwd(queries, keys, values, segs)
    residual = inputs + dot(attended, w_out) + out_bias
    normal_two, scale_two = norm_parts(residual)
    normed_two = (normal_two * mlp_gain + mlp_shift).astype(BF)
    upper = dot(normed_two, w_up) + up_bias
    act, gelu_back = jax.vjp(gelu_tanh, upper)
    act = act.astype(BF)
    output = (residual + dot(act, w_down) + down_bias).astype(BF)
    grad_top = cotangent.astype(F32)
    g_down_bias = jnp.sum(grad_top, axis=0)
    g_w_down = dot(act, cotangent, ((0,), (0,)))
    grad_upper = gelu_back(dot(cotangent, w_down, ((1,), (1,))))[0].astype(BF)
    g_up_bias = jnp.sum(grad_upper.astype(F32), axis=0)
    g_w_up = dot(normed_two, grad_upper, ((0,), (0,)))
    grad_two = dot(grad_upper, w_up, ((1,), (1,)))
    g_mlp_gain = jnp.sum(grad_two * normal_two, axis=0)
    g_mlp_shift = jnp.sum(grad_two, axis=0)
    grad_residual = grad_top + norm_back(grad_two, normal_two, scale_two, mlp_gain)
    grad_branch = grad_residual.astype(BF)
    g_out_bias = jnp.sum(grad_branch.astype(F32), axis=0)
    g_w_out = dot(attended, grad_branch, ((0,), (0,)))
    grad_attended = dot(grad_branch, w_out, ((1,), (1,))).astype(BF)
    grad_proj = attn_bwd(queries, keys, values, grad_attended, attended, stats, penalty, segs)
    bias_sums = jnp.sum(grad_proj.astype(F32), axis=0)
    g_q_bias = bias_sums[:width]
    g_v_bias = bias_sums[2 * width :]
    g_w_qkv = dot(normed, grad_proj, ((0,), (0,)))
    grad_one = dot(grad_proj, w_qkv, ((1,), (1,)))
    g_attn_gain = jnp.sum(grad_one * normal_one, axis=0)
    g_attn_shift = jnp.sum(grad_one, axis=0)
    grad_tokens = grad_residual + norm_back(grad_one, normal_one, scale_one, attn_gain)
    return output, grad_tokens, (
        g_w_qkv, g_q_bias, g_v_bias, g_w_out, g_out_bias, g_attn_gain, g_attn_shift,
        g_mlp_gain, g_mlp_shift, g_w_up, g_up_bias, g_w_down, g_down_bias)


def view(ref, tall, panel, row, rows, col, cols):
    if tall:
        return ref.at[pl.ds(pl.multiple_of(panel*PANEL+row,16),rows),pl.ds(col,cols)]
    return ref.at[pl.ds(pl.multiple_of(row,16),rows),pl.ds(pl.multiple_of(panel*PANEL+col,128),cols)]

def add_into(dst, row, rows, parts, step=STEP):
    def turn(i, _):
        at=pl.multiple_of(i*step,16)
        here=pl.ds(pl.multiple_of(row+at,16),step)
        total=dst[here,:].astype(F32)
        for part in parts:
            total=total+part[pl.ds(at,step),:].astype(F32)
        dst[here,:]=total.astype(BF)
        return 0
    lax.fori_loop(0,rows//step,turn,0)

def reduce_kernel(n_tall, *refs):
    it=iter(refs)
    ins=[next(it) for _ in range(3)]
    tok_ref=next(it); small_ref=next(it)
    outs=[next(it) for _ in range(3)]
    tok_out=next(it); small_out=next(it)
    own,rc,r1,r2,rz,sm_acc,sm_rec=[next(it) for _ in range(7)]
    ssem,rsem,lsem,tss,trs,tls,sms,smr=[next(it) for _ in range(8)]
    z=lax.axis_index("rows"); col=lax.axis_index("cols")
    y=col//4; x=(col//2)%2; c=col%2
    core=(z,y*4+x*2+(1-c)); xd=(z,y*4+(1-x)*2+c); yd=(z,(1-y)*4+x*2+c)
    zd=[(lax.rem(z+d,4),col) for d in range(1,4)]
    cd=[(z,lax.rem(col+d,8)) for d in range(1,8)]
    barrier=pltpu.get_barrier_semaphore()
    for dev in cd+zd:
        pl.semaphore_signal(barrier,inc=1,device_id=dev,device_id_type=MESH)
    pl.semaphore_wait(barrier,10)
    W=PANEL//SPLIT
    chunks=[(g,j) for g in range(3) for j in range(SPLIT)]
    def remote(src,dst,s,r,dev):
        return pltpu.make_async_remote_copy(src_ref=src,dst_ref=dst,send_sem=s,recv_sem=r,device_id=dev,device_id_type=MESH)
    part=tok_ref.shape[0]//8
    def rows_of(d): return pl.ds(pl.multiple_of(d*part,16),part)
    toks=[remote(tok_ref.at[rows_of(cd[i][1]),:],tok_out.at[col],tss.at[i],trs.at[i],cd[i]) for i in range(7)]
    tok_own=pltpu.make_async_copy(tok_ref.at[rows_of(col),:],tok_out.at[col],tls)
    small_devs=[core,xd,yd,(z+1-2*(z%2),col),(lax.rem(z+2,4),col)]
    smalls=[remote(sm_acc.at[i],sm_rec.at[i],sms.at[i],smr.at[i],small_devs[i]) for i in range(5)]
    class C: pass
    work=[]
    for n,(g,j) in enumerate(chunks):
        w=C(); tall=g<n_tall; co=j*W
        def src(panel,row,rows): return view(ins[g],tall,panel,row,rows,co,W)
        def out(panel,row,rows,g=g,tall=tall,co=co): return view(outs[g],tall,panel,row,rows,co,W)
        S=lambda k,n=n: ssem.at[n,k]
        R=lambda k,n=n: rsem.at[n,k]
        w.own=[pltpu.make_async_copy(src(2*c+u,0,PANEL),own.at[n,u],lsem.at[n,u]) for u in range(2)]
        w.c=[remote(src(2*(1-c)+u,0,PANEL),rc.at[n,u],S(u),R(u),core) for u in range(2)]
        h=[x,y]; q=[y,x]
        w.keep1=[h[u]*384 for u in range(2)]; w.send1=[(1-h[u])*384 for u in range(2)]
        w.one=[remote(own.at[n,u,pl.ds(pl.multiple_of(w.send1[u],16),384),:],r1.at[n,u],S(2+u),R(2+u),(xd,yd)[u]) for u in range(2)]
        w.keep2=[w.keep1[u]+q[u]*192 for u in range(2)]; w.send2=[w.keep1[u]+(1-q[u])*192 for u in range(2)]
        w.two=[remote(own.at[n,u,pl.ds(pl.multiple_of(w.send2[u],16),192),:],r2.at[n,u],S(4+u),R(4+u),(yd,xd)[u]) for u in range(2)]
        w.z=[remote(own.at[n,u,pl.ds(pl.multiple_of(w.keep2[u]+zd[d][0]*48,16),48),:],rz.at[n,u,d],S(6+3*u+d),R(6+3*u+d),zd[d]) for u in range(2) for d in range(3)]
        w.final=[w.keep2[u]+z*48 for u in range(2)]
        def fin(u,n=n,w=w): return own.at[n,u,pl.ds(pl.multiple_of(w.final[u],16),48),:]
        w.fin=[pltpu.make_async_copy(fin(u),out(2*c+u,w.final[u],48),lsem.at[n,2+u]) for u in range(2)]
        w.zz=[remote(fin(u),out(2*c+u,w.final[u],48),S(12+3*u+d),R(12+3*u+d),zd[d]) for u in range(2) for d in range(3)]
        w.two_b=[remote(out(2*c+u,w.keep2[u],192),out(2*c+u,w.keep2[u],192),S(18+u),R(18+u),(yd,xd)[u]) for u in range(2)]
        w.one_b=[remote(out(2*c+u,w.keep1[u],384),out(2*c+u,w.keep1[u],384),S(20+u),R(20+u),(xd,yd)[u]) for u in range(2)]
        w.c_b=[remote(out(2*c+u,0,PANEL),out(2*c+u,0,PANEL),S(22+u),R(22+u),core) for u in range(2)]
        work.append(w)
    def start(copies):
        for d in copies: d.start()
    def begin(n):
        w=work[n]; start(w.c); start(w.own)
    def s0(n):
        w=work[n]
        for u in range(2):
            w.own[u].wait(); w.c[u].wait_recv()
            add_into(own.at[n,u],w.send1[u],384,[rc.at[n,u,pl.ds(pl.multiple_of(w.send1[u],16),384),:]])
            w.one[u].start()
        for u in range(2):
            add_into(own.at[n,u],w.keep1[u],384,[rc.at[n,u,pl.ds(pl.multiple_of(w.keep1[u],16),384),:]])
    def s1(n):
        w=work[n]
        for u in range(2):
            w.one[u].wait_recv()
            add_into(own.at[n,u],w.send2[u],192,[r1.at[n,u,pl.ds(pl.multiple_of(w.send2[u]-w.keep1[u],16),192),:]])
            w.two[u].start()
            add_into(own.at[n,u],w.keep2[u],192,[r1.at[n,u,pl.ds(pl.multiple_of(w.keep2[u]-w.keep1[u],16),192),:]])
    def s2(n):
        w=work[n]
        for u in range(2):
            w.two[u].wait_recv()
            add_into(own.at[n,u],w.keep2[u],192,[r2.at[n,u]])
            start(w.z[3*u:3*u+3])
    def s3(n):
        w=work[n]
        for u in range(2):
            for d in w.z[3*u:3*u+3]: d.wait_recv()
            add_into(own.at[n,u],w.final[u],48,[rz.at[n,u,d] for d in range(3)])
            start(w.zz[3*u:3*u+3]); w.fin[u].start()
    def s4(n):
        w=work[n]
        for u in range(2):
            for d in w.zz[3*u:3*u+3]: d.wait_recv()
            w.fin[u].wait(); w.two_b[u].start()
    def s5(n):
        w=work[n]
        for u in range(2):
            w.two_b[u].wait_recv(); w.one_b[u].start()
    def s6(n):
        w=work[n]
        for u in range(2):
            w.one_b[u].wait_recv(); w.c_b[u].start()
    def s7(n):
        w=work[n]
        for u in range(2): w.c_b[u].wait_recv()
        for d in w.c+w.one+w.two+w.z+w.zz+w.two_b+w.one_b+w.c_b: d.wait_send()
    stages=[s0,s1,s2,s3,s4,s5,s6,s7]
    sm_acc[0]=small_ref[...]
    smalls[0].start();
    begin(0)
    start(toks); tok_own.start()
    N=len(chunks)
    for t in range(N+len(stages)-1):
        if t+1<N: begin(t+1)
        for n in range(N):
            if 0<=t-n<len(stages): stages[t-n](n)
        if t<5:
            smalls[t].wait_recv()
            nxt=sm_acc[t]+sm_rec[t]
            if t<4:
                sm_acc[t+1]=nxt; smalls[t+1].start()
            else: small_out[...]=nxt
    for d in smalls: d.wait_send()
    for d in toks: d.wait()
    tok_own.wait()

def reduce_all(down,up,qo,tokens,small):
    N=3*SPLIT; W=PANEL//SPLIT
    any_=pl.BlockSpec(memory_space=pl.ANY); vm=pl.BlockSpec(memory_space=pltpu.VMEM)
    DMA=pltpu.SemaphoreType.DMA
    L,D=tokens.shape
    return pl.pallas_call(functools.partial(reduce_kernel,1),
        out_shape=(jax.ShapeDtypeStruct(down.shape,BF),jax.ShapeDtypeStruct(up.shape,BF),jax.ShapeDtypeStruct(qo.shape,BF),
                   jax.ShapeDtypeStruct((8,L//8,D),BF),jax.ShapeDtypeStruct(small.shape,F32)),
        in_specs=[any_]*4+[vm],out_specs=(any_,)*4+(vm,),
        scratch_shapes=[pltpu.VMEM((N,2,PANEL,W),BF),pltpu.VMEM((N,2,PANEL,W),BF),pltpu.VMEM((N,2,384,W),BF),pltpu.VMEM((N,2,192,W),BF),
                        pltpu.VMEM((N,2,3,48,W),BF),pltpu.VMEM((5,)+small.shape,F32),pltpu.VMEM((5,)+small.shape,F32),
                        DMA((N,24)),DMA((N,24)),DMA((N,4)),DMA((7,)),DMA((7,)),DMA,DMA((5,)),DMA((5,))],
        compiler_params=pltpu.CompilerParams(vmem_limit_bytes=60*2**20,collective_id=1,has_side_effects=True),name="reduce_all")(down,up,qo,tokens,small)


def summed_grads(grads, copies):
    grads = [g / copies for g in grads]
    matrices = [i for i, g in enumerate(grads) if g.ndim == 2]
    vectors = [i for i, g in enumerate(grads) if g.ndim == 1]
    big = lax.psum([grads[i].astype(BF) for i in matrices], ("rows", "cols"))
    small = lax.psum(jnp.concatenate([grads[i] for i in vectors]), ("rows", "cols"))
    out = [None] * len(grads)
    for i, g in zip(matrices, big):
        out[i] = g.astype(F32)
    at = 0
    for i in vectors:
        out[i] = small[at : at + grads[i].shape[0]]
        at += grads[i].shape[0]
    return out


def whole_by_permutes(value):
    parts, cols = value.shape[0], lax.axis_size("cols")
    me = lax.axis_index("cols")
    whole = jnp.zeros_like(value)
    own = lax.dynamic_slice_in_dim(value, me, 1, 0)
    whole = lax.dynamic_update_slice_in_dim(whole, own, me, 0)
    for step in range(1, cols):
        block = lax.dynamic_slice_in_dim(value, lax.rem(me + step, cols), 1, 0)
        block = lax.ppermute(block, "cols", [(i, (i + step) % cols) for i in range(cols)])
        whole = lax.dynamic_update_slice_in_dim(whole, block, lax.rem(me - step + cols, cols), 0)
    return whole


def per_device(tokens, segment_ids, cotangent, *weights):
    seqs, part, width = tokens.shape
    cols = lax.axis_size("cols")
    fitting = (lax.axis_size("rows"), cols, seqs) == (4, 8, 8)
    copies = max(1, cols // seqs)
    held = max(1, seqs // cols)
    first = (lax.axis_index("cols") // copies) * held
    segs = lax.dynamic_slice_in_dim(segment_ids, first, held, 0)
    tokens_whole = to_whole(tokens, copies)
    if fitting:
        cotangent_whole = whole_by_permutes(cotangent).reshape(1, -1, width)
    else:
        cotangent_whole = to_whole(cotangent, copies)
    results = [
        layer(tokens_whole[s], segs[s], cotangent_whole[s], weights) for s in range(held)
    ]
    if fitting:
        output, grad_tokens, grads = results[0]
        output = whole_by_permutes(output.reshape(cols, part, width))
        (g_w_qkv, g_q_bias, g_v_bias, g_w_out, g_out_bias, g_attn_gain, g_attn_shift,
         g_mlp_gain, g_mlp_shift, g_w_up, g_up_bias, g_w_down, g_down_bias) = grads
        side = jnp.concatenate([g_w_qkv.astype(BF), g_w_out.astype(BF)], axis=1)
        small = jnp.concatenate([
            g_q_bias, g_v_bias, g_out_bias, g_attn_gain, g_attn_shift, g_mlp_gain, g_mlp_shift,
            g_down_bias, g_up_bias]).reshape(-1, width)
        small = jnp.pad(small, ((0, 16 - small.shape[0]), (0, 0)))
        down, up, side, grad_tokens, small = reduce_all(
            g_w_down.astype(BF), g_w_up.astype(BF), side, grad_tokens.astype(BF), small)
        up_bias = small[8:12].reshape(-1)
        return (
            output, grad_tokens.astype(F32), side[:, : 3 * width].astype(F32), small[0], small[1],
            side[:, 3 * width :].astype(F32), small[2], small[3], small[4], small[5], small[6],
            up.astype(F32), up_bias, down.astype(F32), small[7])
    output = jnp.stack([r[0] for r in results])
    grad_tokens = jnp.stack([r[1] for r in results])
    grads = [sum(parts[1:], parts[0]) for parts in zip(*[r[2] for r in results])]
    return (
        to_parts(output, copies),
        to_parts(grad_tokens.astype(BF), copies).astype(F32),
        *summed_grads(grads, copies),
    )


def solution(mesh):
    placed = (P("rows", "cols", None), P("rows", None), P("rows", "cols", None)) + (P(),) * 13
    return jax.shard_map(
        per_device,
        mesh=mesh,
        in_specs=placed,
        out_specs=(P("rows", "cols", None), P("rows", "cols", None)) + (P(),) * 13,
        check_vma=False,
    )
```

```python
import functools

import jax
import jax.numpy as jnp
from jax import lax
from jax.experimental import pallas as pl
from jax.experimental.pallas import tpu as pltpu
from jax.sharding import PartitionSpec as P

HEADS = 12
HDIM = 64
BF = jnp.bfloat16
F32 = jnp.float32
LOG2E = 1.4426950408889634
BIG = 1e30
BLOCK = 256
MESH = pl.DeviceIdType.MESH
PANEL = 768
SPLIT = 2
STEP = 48
VMEM_LIMIT = 62 * 2**20


def to_whole(value, copies):
    if copies > 1:
        value = jnp.repeat(value, copies, axis=0)
    return lax.all_to_all(value, "cols", 0, 1, tiled=True)


def to_parts(value, copies):
    parts = lax.all_to_all(value, "cols", 1, 0, tiled=True)
    return parts[::copies] if copies > 1 else parts


def dot(a, b, dims=((1,), (0,))):
    return lax.dot_general(a, b, (dims, ((), ())), preferred_element_type=F32)


def norm_parts(values):
    average = jnp.mean(values, axis=-1, keepdims=True)
    centered = values - average
    scale = lax.rsqrt(jnp.mean(centered * centered, axis=-1, keepdims=True) + 1e-05)
    return centered * scale, scale


def norm_back(grad, normal, scale, gain):
    weighted = grad * gain
    inner = jnp.mean(weighted * normal, axis=-1, keepdims=True)
    return scale * (weighted - jnp.mean(weighted, axis=-1, keepdims=True) - normal * inner)


def gelu_tanh(values):
    return jax.nn.gelu(values, approximate=True)


NT=((1,),(1,))

def tri(size, upper):
    r=lax.broadcasted_iota(jnp.int32,(size,size),0); c=lax.broadcasted_iota(jnp.int32,(size,size),1)
    return jnp.where(c>r if upper else c<r, 1.0, 0.0).astype(BF)

def split_sum(mask, x):
    hi=x.astype(BF)
    lo=(x-hi.astype(F32)).astype(BF)
    return dot(mask,hi)+dot(mask,lo)

def lane_low(shape):
    return lax.broadcasted_iota(jnp.int32,shape,1) < HDIM

def attn_fwd_kernel(q_ref,k_ref,v_ref,segc_ref,segr_ref,startr_ref,o_ref,lse_ref,pen_ref):
    L=q_ref.shape[0]; nb=L//BLOCK
    scale=HDIM**-0.5
    pairs=HEADS//2
    upper=tri(BLOCK,True)
    carry=jnp.zeros((1,L),F32)
    for b in range(nb-1,-1,-1):
        i0=b*BLOCK; n=L-i0
        q0=q_ref[i0:i0+BLOCK,0:128]
        q0=jnp.where(lane_low(q0.shape),q0,jnp.zeros_like(q0))
        s=dot(q0,k_ref[i0:L,0:128],NT)*scale
        rows=i0+lax.broadcasted_iota(jnp.int32,(BLOCK,n),0)
        cols=i0+lax.broadcasted_iota(jnp.int32,(BLOCK,n),1)
        same=segc_ref[i0:i0+BLOCK,0:1]==segr_ref[0:1,i0:L]
        picked=same&(cols>rows)&(startr_ref[0:1,i0:L]==0)
        sel=jnp.where(picked,jnp.maximum(s,0.0),0.0)
        if b==nb-1: cin=jnp.zeros((1,n),F32)
        else: cin=jnp.concatenate([jnp.zeros((1,BLOCK),F32),carry],axis=1)
        carried=split_sum(upper,sel)+cin
        pen_ref[i0:i0+BLOCK,i0:L]=jnp.where(same&(cols>=rows),carried*(8.0/L*LOG2E),BIG)
        carry=cin+jnp.sum(sel,axis=0,keepdims=True)
    c=scale*LOG2E
    for b in range(nb):
        i0=b*BLOCK; n=L-i0
        def pair(p,stats,i0=i0,n=n):
            off=pl.multiple_of(p*128,128)
            q=q_ref[i0:i0+BLOCK,pl.ds(off,128)]
            k=k_ref[i0:L,pl.ds(off,128)]
            v=v_ref[i0:L,pl.ds(off,128)]
            low=lane_low(q.shape)
            outs=[]
            lane=lax.broadcasted_iota(jnp.int32,(BLOCK,128),1)
            for h in range(2):
                mine=low if h==0 else jnp.logical_not(low)
                qm=jnp.where(mine,q,jnp.zeros_like(q))
                s=dot(qm,k,NT)*c-pen_ref[i0:i0+BLOCK,i0:L]
                m=jnp.max(s,axis=1,keepdims=True)
                e=jnp.exp2(s-m).astype(BF)
                lowv=lane_low(v.shape)
                vm=jnp.where(lowv if h==0 else jnp.logical_not(lowv),v,jnp.ones_like(v))
                o=dot(e,vm)
                tot=pltpu.roll(o,HDIM,1)
                outs.append(o/tot)
                full=jnp.where(mine,tot,o)
                stats=jnp.where(lane==2*p+h,m+jnp.log2(full),stats)
            o_ref[i0:i0+BLOCK,pl.ds(off,128)]=jnp.where(low,outs[0],outs[1]).astype(BF)
            return stats
        lse_ref[i0:i0+BLOCK,:]=lax.fori_loop(0,pairs,pair,jnp.zeros((BLOCK,128),F32))

def attn_fwd(q,k,v,seg):
    L,D=q.shape
    start=jnp.concatenate([(seg[:-1]!=seg[1:]).astype(jnp.int32),jnp.ones((1,),jnp.int32)])
    vm=pl.BlockSpec(memory_space=pltpu.VMEM)
    return pl.pallas_call(attn_fwd_kernel,
        out_shape=(jax.ShapeDtypeStruct((L,D),BF),jax.ShapeDtypeStruct((L,128),F32),jax.ShapeDtypeStruct((L,L),F32)),
        in_specs=[vm]*6,out_specs=(vm,)*3,
        compiler_params=pltpu.CompilerParams(vmem_limit_bytes=60*2**20),name="attn_fwd")(q,k,v,seg[:,None],seg[None,:],start[None,:])

def attn_bwd_kernel(q_ref,k_ref,v_ref,g_ref,o_ref,lse_ref,pen_ref,startr_ref,out_ref,qt,gt,dkt,dvt,dsum):
    L,D=q_ref.shape; nb=L//BLOCK
    scale=HDIM**-0.5; c=scale*LOG2E
    pairs=HEADS//2
    lower=tri(BLOCK,False)
    for p in range(pairs):
        qt[p*128:(p+1)*128,:]=q_ref[:,p*128:(p+1)*128].T
        gt[p*128:(p+1)*128,:]=g_ref[:,p*128:(p+1)*128].T
    dkt[...]=jnp.zeros_like(dkt); dvt[...]=jnp.zeros_like(dvt)
    carry=jnp.zeros((1,L),F32)
    for b in range(nb):
        i0=b*BLOCK; n=L-i0
        rowsl=slice(i0,i0+BLOCK)
        carry=carry[:,-n:]
        def head(p,h,i0=i0,n=n,rowsl=rowsl):
            static=isinstance(p,int)
            off=p*128 if static else pl.multiple_of(p*128,128)
            q=q_ref[rowsl,pl.ds(off,128)]; g=g_ref[rowsl,pl.ds(off,128)]; o=o_ref[rowsl,pl.ds(off,128)]
            k=k_ref[i0:L,pl.ds(off,128)]; v=v_ref[i0:L,pl.ds(off,128)]
            low=lane_low(q.shape); mine=low if h==0 else jnp.logical_not(low)
            qm=jnp.where(mine,q,jnp.zeros_like(q)); gm=jnp.where(mine,g,jnp.zeros_like(g))
            lane=lax.broadcasted_iota(jnp.int32,(BLOCK,128),1)
            lse=jnp.sum(jnp.where(lane==2*p+h,lse_ref[rowsl,:],0.0),axis=1,keepdims=True)
            delta=jnp.sum(gm.astype(F32)*o.astype(F32),axis=1,keepdims=True)
            s=dot(qm,k,NT)
            pr=jnp.exp2(s*c-pen_ref[rowsl,i0:L]-lse)
            dp=dot(gm,v,NT)
            ds=pr*(dp-delta)
            return s,pr,ds,off,k
        def finish(p,h,pr,ds,off,k,i0=i0,rowsl=rowsl):
            base=p*128+h*HDIM
            if not isinstance(p,int): base=pl.multiple_of(base,64)
            dsb=ds.astype(BF); prb=pr.astype(BF)
            dvt[pl.ds(base,HDIM),i0:L]+=dot(gt[pl.ds(base,HDIM),rowsl],prb)
            dkt[pl.ds(base,HDIM),i0:L]+=dot(qt[pl.ds(base,HDIM),rowsl],dsb)
            return dot(dsb,k)
        dsum[:,i0:L]=jnp.zeros((BLOCK,n),F32)
        def pair(p,carry_):
            dq=[]
            for h in range(2):
                s,pr,ds,off,k=head(p,h)
                dsum[:,i0:L]+=ds
                dq.append(finish(p,h,pr,ds,off,k))
            out_ref[rowsl,pl.ds(off,128)]=(jnp.where(lane_low(dq[0].shape),dq[0],dq[1])*scale).astype(BF)
            return carry_
        lax.fori_loop(1,pairs,pair,0)
        s,pr,ds,off,k=head(0,1)
        dsum[:,i0:L]+=ds
        dq1=finish(0,1,pr,ds,off,k)
        s,pr,ds,off,k=head(0,0)
        total=dsum[:,i0:L]+ds
        rows=i0+lax.broadcasted_iota(jnp.int32,(BLOCK,n),0)
        cols=i0+lax.broadcasted_iota(jnp.int32,(BLOCK,n),1)
        picked=(pen_ref[rowsl,i0:L]<1e29)&(cols>rows)&(startr_ref[0:1,i0:L]==0)&(s>0)
        gsel=(split_sum(lower,total)+carry)*(-8.0/L)
        carry=carry+jnp.sum(total,axis=0,keepdims=True)
        ds=ds+jnp.where(picked,gsel,0.0)
        dq0=finish(0,0,pr,ds,off,k)
        out_ref[rowsl,0:128]=(jnp.where(lane_low(dq0.shape),dq0,dq1)*scale).astype(BF)
    for p in range(pairs):
        sl=slice(p*128,(p+1)*128)
        out_ref[:,D+p*128:D+(p+1)*128]=(dkt[sl,:]*scale).T.astype(BF)
        out_ref[:,2*D+p*128:2*D+(p+1)*128]=dvt[sl,:].T.astype(BF)

def attn_bwd(q,k,v,g,o,lse,pen,seg):
    L,D=q.shape
    start=jnp.concatenate([(seg[:-1]!=seg[1:]).astype(jnp.int32),jnp.ones((1,),jnp.int32)])
    vm=pl.BlockSpec(memory_space=pltpu.VMEM)
    return pl.pallas_call(attn_bwd_kernel,
        out_shape=jax.ShapeDtypeStruct((L,3*D),BF),
        in_specs=[vm]*8,out_specs=vm,
        scratch_shapes=[pltpu.VMEM((D,L),BF),pltpu.VMEM((D,L),BF),pltpu.VMEM((D,L),F32),pltpu.VMEM((D,L),F32),pltpu.VMEM((BLOCK,L),F32)],
        compiler_params=pltpu.CompilerParams(vmem_limit_bytes=60*2**20),name="attn_bwd")(q,k,v,g,o,lse,pen,start[None,:])


def layer(tokens, segs, cotangent, weights, fused):
    (w_qkv, q_bias, v_bias, w_out, out_bias, attn_gain, attn_shift, mlp_gain, mlp_shift,
     w_up, up_bias, w_down, down_bias) = weights
    width = tokens.shape[1]
    inputs = tokens.astype(F32)
    normal_one, scale_one = norm_parts(inputs)
    normed = (normal_one * attn_gain + attn_shift).astype(BF)
    projected = dot(normed, w_qkv)
    queries = (projected[:, :width] + q_bias).astype(BF)
    keys = projected[:, width : 2 * width].astype(BF)
    values = (projected[:, 2 * width :] + v_bias).astype(BF)
    attended, stats, penalty = attn_fwd(queries, keys, values, segs)
    residual = inputs + dot(attended, w_out) + out_bias
    normal_two, scale_two = norm_parts(residual)
    normed_two = (normal_two * mlp_gain + mlp_shift).astype(BF)
    upper = dot(normed_two, w_up) + up_bias
    act, gelu_back = jax.vjp(gelu_tanh, upper)
    act = act.astype(BF)
    output = (residual + dot(act, w_down) + down_bias).astype(BF)
    grad_top = cotangent.astype(F32)
    g_down_bias = jnp.sum(grad_top, axis=0)
    g_w_down = dot(act, cotangent, ((0,), (0,)))
    grad_upper = gelu_back(dot(cotangent, w_down, ((1,), (1,))))[0].astype(BF)
    g_up_bias = jnp.sum(grad_upper.astype(F32), axis=0)
    g_w_up = dot(normed_two, grad_upper, ((0,), (0,)))
    grad_two = dot(grad_upper, w_up, ((1,), (1,)))
    g_mlp_gain = jnp.sum(grad_two * normal_two, axis=0)
    g_mlp_shift = jnp.sum(grad_two, axis=0)
    grad_residual = grad_top + norm_back(grad_two, normal_two, scale_two, mlp_gain)
    grad_branch = grad_residual.astype(BF)
    g_out_bias = jnp.sum(grad_branch.astype(F32), axis=0)
    g_w_out = dot(attended, grad_branch, ((0,), (0,)))
    grad_attended = dot(grad_branch, w_out, ((1,), (1,))).astype(BF)
    if fused:
        grad_attended = lax.optimization_barrier(grad_attended)
        start_sums = jnp.sum((grad_attended.astype(F32) * attended.astype(F32)).reshape(-1, HEADS, HDIM), axis=2)
        delta = jnp.pad(start_sums, ((0, 0), (0, 128 - HEADS)))
        zero = jnp.zeros((width,), F32)
        small = jnp.concatenate([zero, zero, g_out_bias, zero, zero, g_mlp_gain, g_mlp_shift, g_down_bias, g_up_bias])
        small = jnp.pad(small.reshape(-1, width), ((0, 4), (0, 0)))
        return attn_back_and_sums(
            queries, keys, values, grad_attended, delta, stats, segs, tokens, attn_gain, attn_shift, w_qkv, small,
            penalty, grad_residual, g_w_out.astype(BF), g_w_down.astype(BF), g_w_up.astype(BF), output)
    grad_proj = attn_bwd(queries, keys, values, grad_attended, attended, stats, penalty, segs)
    bias_sums = jnp.sum(grad_proj.astype(F32), axis=0)
    g_q_bias = bias_sums[:width]
    g_v_bias = bias_sums[2 * width :]
    g_w_qkv = dot(normed, grad_proj, ((0,), (0,)))
    grad_one = dot(grad_proj, w_qkv, ((1,), (1,)))
    g_attn_gain = jnp.sum(grad_one * normal_one, axis=0)
    g_attn_shift = jnp.sum(grad_one, axis=0)
    grad_tokens = grad_residual + norm_back(grad_one, normal_one, scale_one, attn_gain)
    return output, grad_tokens, (
        g_w_qkv, g_q_bias, g_v_bias, g_w_out, g_out_bias, g_attn_gain, g_attn_shift,
        g_mlp_gain, g_mlp_shift, g_w_up, g_up_bias, g_w_down, g_down_bias)


def view(ref, tall, panel, row, rows, col, cols):
    if tall:
        return ref.at[pl.ds(pl.multiple_of(panel * PANEL + row, 16), rows), pl.ds(col, cols)]
    return ref.at[pl.ds(pl.multiple_of(row, 16), rows), pl.ds(pl.multiple_of(panel * PANEL + col, 128), cols)]


def add_into(dst, row, rows, parts):
    def turn(i, carry):
        at = pl.multiple_of(i * STEP, 16)
        here = pl.ds(pl.multiple_of(row + at, 16), STEP)
        total = dst[here, :].astype(F32)
        for part in parts:
            total = total + part[pl.ds(at, STEP), :].astype(F32)
        dst[here, :] = total.astype(BF)
        return carry

    lax.fori_loop(0, rows // STEP, turn, 0)


def rows_at(ref, row, rows):
    return ref.at[pl.ds(pl.multiple_of(row, 16), rows), :]


def remote(src, dst, sent, landed, device):
    return pltpu.make_async_remote_copy(
        src_ref=src, dst_ref=dst, send_sem=sent, recv_sem=landed, device_id=device, device_id_type=MESH
    )


class Place:
    def __init__(self):
        self.z, self.col = lax.axis_index("rows"), lax.axis_index("cols")
        z, col = self.z, self.col
        self.y, self.x, self.c = col // 4, (col // 2) % 2, col % 2
        y, x, c = self.y, self.x, self.c
        self.core = (z, y * 4 + x * 2 + (1 - c))
        self.across_x = (z, y * 4 + (1 - x) * 2 + c)
        self.across_y = (z, (1 - y) * 4 + x * 2 + c)
        self.along_z = [(lax.rem(z + d, 4), col) for d in range(1, 4)]
        self.along_cols = [(z, lax.rem(col + d, 8)) for d in range(1, 8)]

    def greet(self, devices):
        barrier = pltpu.get_barrier_semaphore()
        for device in devices:
            pl.semaphore_signal(barrier, inc=1, device_id=device, device_id_type=MESH)
        pl.semaphore_wait(barrier, len(devices))


class Chunk:
    def __init__(self, place, n, source, result, tall, first, buffers, sems):
        own, from_core, from_one, from_two, from_z = [b.at[n] for b in buffers]
        sent, landed, local = sems
        width = own.shape[-1]
        x, y, z, c = place.x, place.y, place.z, place.c
        S = lambda k: sent.at[n, k]
        R = lambda k: landed.at[n, k]
        src = lambda panel, row, rows: view(source, tall, panel, row, rows, first, width)
        out = lambda panel, row, rows: view(result, tall, panel, row, rows, first, width)
        near, far = [x, y], [y, x]
        to_near = [place.across_x, place.across_y]
        to_far = [place.across_y, place.across_x]
        half, quarter, piece = PANEL // 2, PANEL // 4, PANEL // 16
        both = range(2)
        self.own, self.from_core, self.from_one = own, from_core, from_one
        self.from_two, self.from_z = from_two, from_z
        self.half, self.quarter, self.piece = half, quarter, piece
        self.keep1 = [near[u] * half for u in both]
        self.send1 = [(1 - near[u]) * half for u in both]
        self.keep2 = [self.keep1[u] + far[u] * quarter for u in both]
        self.send2 = [self.keep1[u] + (1 - far[u]) * quarter for u in both]
        self.last = [self.keep2[u] + z * piece for u in both]
        final = lambda u: rows_at(own.at[u], self.last[u], piece)
        self.load = [pltpu.make_async_copy(src(2 * c + u, 0, PANEL), own.at[u], local.at[n, u]) for u in both]
        self.core = [remote(src(2 * (1 - c) + u, 0, PANEL), from_core.at[u], S(u), R(u), place.core) for u in both]
        self.one = [remote(rows_at(own.at[u], self.send1[u], half), from_one.at[u], S(2 + u), R(2 + u), to_near[u]) for u in both]
        self.two = [remote(rows_at(own.at[u], self.send2[u], quarter), from_two.at[u], S(4 + u), R(4 + u), to_far[u]) for u in both]
        self.deep = [[remote(rows_at(own.at[u], self.keep2[u] + dev[0] * piece, piece), from_z.at[u, d],
                             S(6 + 3 * u + d), R(6 + 3 * u + d), dev)
                      for d, dev in enumerate(place.along_z)] for u in both]
        self.store = [pltpu.make_async_copy(final(u), out(2 * c + u, self.last[u], piece), local.at[n, 2 + u]) for u in both]
        self.deep_back = [[remote(final(u), out(2 * c + u, self.last[u], piece), S(12 + 3 * u + d), R(12 + 3 * u + d), dev)
                           for d, dev in enumerate(place.along_z)] for u in both]
        same = lambda panel, row, rows, k, dev: remote(out(panel, row, rows), out(panel, row, rows), S(k), R(k), dev)
        self.two_back = [same(2 * c + u, self.keep2[u], quarter, 18 + u, to_far[u]) for u in both]
        self.one_back = [same(2 * c + u, self.keep1[u], half, 20 + u, to_near[u]) for u in both]
        self.core_back = [same(2 * c + u, 0, PANEL, 22 + u, place.core) for u in both]

    def begin(self):
        for copy in self.core + self.load:
            copy.start()

    def step(self, k):
        both = range(2)
        own = [self.own.at[u] for u in both]
        if k == 0:
            for u in both:
                self.load[u].wait()
                self.core[u].wait_recv()
                add_into(own[u], self.send1[u], self.half, [rows_at(self.from_core.at[u], self.send1[u], self.half)])
                self.one[u].start()
            for u in both:
                add_into(own[u], self.keep1[u], self.half, [rows_at(self.from_core.at[u], self.keep1[u], self.half)])
        elif k == 1:
            for u in both:
                self.one[u].wait_recv()
                add_into(own[u], self.send2[u], self.quarter, [rows_at(self.from_one.at[u], self.send2[u] - self.keep1[u], self.quarter)])
                self.two[u].start()
                add_into(own[u], self.keep2[u], self.quarter, [rows_at(self.from_one.at[u], self.keep2[u] - self.keep1[u], self.quarter)])
        elif k == 2:
            for u in both:
                self.two[u].wait_recv()
                add_into(own[u], self.keep2[u], self.quarter, [self.from_two.at[u]])
                for copy in self.deep[u]:
                    copy.start()
        elif k == 3:
            for u in both:
                for copy in self.deep[u]:
                    copy.wait_recv()
                add_into(own[u], self.last[u], self.piece, [self.from_z.at[u, d] for d in range(3)])
                for copy in self.deep_back[u]:
                    copy.start()
                self.store[u].start()
        elif k == 4:
            for u in both:
                for copy in self.deep_back[u]:
                    copy.wait_recv()
                self.store[u].wait()
                self.two_back[u].start()
        elif k == 5:
            for u in both:
                self.two_back[u].wait_recv()
                self.one_back[u].start()
        elif k == 6:
            for u in both:
                self.one_back[u].wait_recv()
                self.core_back[u].start()
        else:
            for u in both:
                self.core_back[u].wait_recv()
            for copy in (self.core + self.one + self.two + self.deep[0] + self.deep[1] + self.deep_back[0]
                         + self.deep_back[1] + self.two_back + self.one_back + self.core_back):
                copy.wait_send()


class Timeline:
    LINK = ["core", "plane", "plane", "deep", "deep", "plane", "plane", "core"]
    TAKES = [2.5, 6.0, 3.0, 6.0, 6.0, 3.0, 6.0, 2.5]
    WORK = [2.0, 1.0, 0.5, 0.5, 0.1, 0.1, 0.1, 0.1]

    def __init__(self):
        self.now = 0.0
        self.free = {"core": 0.0, "plane": 0.0, "deep": 0.0}
        self.moving = {}
        self.after_first = {}

    def occupy(self, link, takes):
        self.free[link] = max(self.free[link], self.now) + takes
        return self.free[link] + 1.5

    def begin(self, chunk, then=None):
        chunk.begin()
        self.moving[chunk] = (self.occupy(self.LINK[0], self.TAKES[0]), 0)
        self.after_first[chunk] = then

    def turn(self, chunk):
        done, k = self.moving.pop(chunk)
        self.now = max(self.now, done)
        chunk.step(k)
        self.now += self.WORK[k]
        if k < 7:
            self.moving[chunk] = (self.occupy(self.LINK[k + 1], self.TAKES[k + 1]), k + 1)
        if k == 0 and self.after_first[chunk]:
            self.after_first[chunk]()

    def ready(self):
        while self.moving:
            chunk = min(self.moving, key=lambda c: self.moving[c][0])
            if self.moving[chunk][0] > self.now:
                return
            self.turn(chunk)

    def worked(self, takes):
        self.now += takes
        self.ready()

    def finish(self):
        while self.moving:
            self.turn(min(self.moving, key=lambda c: self.moving[c][0]))


class Homeward:
    def __init__(self, place, source, result, sent, landed, local):
        part = source.shape[0] // 8
        self.copies = [remote(rows_at(source, dev[1] * part, part), result.at[place.col], sent.at[i], landed.at[i], dev)
                       for i, dev in enumerate(place.along_cols)]
        self.own = pltpu.make_async_copy(rows_at(source, place.col * part, part), result.at[place.col], local)

    def start(self):
        for copy in self.copies:
            copy.start()
        self.own.start()

    def wait(self):
        for copy in self.copies:
            copy.wait()
        self.own.wait()


def back_kernel(q_ref, k_ref, v_ref, g_ref, delta_ref, lse_ref, startr_ref, tokens_ref, gain_ref, shift_ref,
                w_ref, small_ref, pen_ref, residual_ref, g_out_ref, down_ref, up_ref, output_ref,
                down_out, up_out, side_out, tokens_out, output_out, small_out,
                qt, gt, dkt, dvt, dsum, pen, dqkv, side, gtok, gres, own, from_core, from_one, from_two, from_z,
                sm_acc, sm_rec, sent, landed, local, home_s, home_r, home_l, sm_s, sm_r, pen_s, res_s, out_s):
    L, D = q_ref.shape
    nb = L // BLOCK
    scale = HDIM**-0.5
    c = scale * LOG2E
    pairs = HEADS // 2
    width = PANEL // SPLIT
    place = Place()
    place.greet(place.along_cols + place.along_z)
    buffers, sems = (own, from_core, from_one, from_two, from_z), (sent, landed, local)
    chunks = []
    for source, result, tall in ((down_ref, down_out, True), (up_ref, up_out, False), (side, side_out, False)):
        for j in range(SPLIT):
            chunks.append(Chunk(place, len(chunks), source, result, tall, j * width, buffers, sems))
    early = 2 * SPLIT
    line = Timeline()

    def chain(n):
        if n < early:
            line.begin(chunks[n], lambda: chain(n + 1))

    chain(0)
    pen_copies = [pltpu.make_async_copy(pen_ref.at[b * BLOCK : (b + 1) * BLOCK, :], pen.at[b % 2], pen_s.at[b % 2]) for b in range(nb)]
    res_copies = [pltpu.make_async_copy(residual_ref.at[b * BLOCK : (b + 1) * BLOCK, :], gres.at[b % 2], res_s.at[b % 2]) for b in range(nb)]
    pen_copies[0].start()
    output_home = Homeward(place, output_ref, output_out, home_s.at[0], home_r.at[0], home_l.at[0])
    output_home.start()
    line.occupy("plane", 16.0)
    out_copy = pltpu.make_async_copy(g_out_ref, side.at[:, 3 * D : 4 * D], out_s)
    out_copy.start()
    for p in range(pairs):
        qt[p * 128 : (p + 1) * 128, :] = q_ref[:, p * 128 : (p + 1) * 128].T
        gt[p * 128 : (p + 1) * 128, :] = g_ref[:, p * 128 : (p + 1) * 128].T
    dkt[...] = jnp.zeros_like(dkt)
    dvt[...] = jnp.zeros_like(dvt)
    line.worked(2.0)
    lower = tri(BLOCK, False)
    carry = jnp.zeros((1, L), F32)
    for b in range(nb):
        i0 = b * BLOCK
        n = L - i0
        rowsl = slice(i0, i0 + BLOCK)
        carry = carry[:, -n:]
        pen_copies[b].wait()
        if b + 1 < nb:
            pen_copies[b + 1].start()
        pen_b = pen.at[b % 2, :, i0:L]

        def head(p, h):
            off = p * 128 if isinstance(p, int) else pl.multiple_of(p * 128, 128)
            q = q_ref[rowsl, pl.ds(off, 128)]
            g = g_ref[rowsl, pl.ds(off, 128)]
            k = k_ref[i0:L, pl.ds(off, 128)]
            v = v_ref[i0:L, pl.ds(off, 128)]
            low = lane_low(q.shape)
            mine = low if h == 0 else jnp.logical_not(low)
            lane = lax.broadcasted_iota(jnp.int32, (BLOCK, 128), 1)
            lse = jnp.sum(jnp.where(lane == 2 * p + h, lse_ref[rowsl, :], 0.0), axis=1, keepdims=True)
            delta = jnp.sum(jnp.where(lane == 2 * p + h, delta_ref[rowsl, :], 0.0), axis=1, keepdims=True)
            s = dot(jnp.where(mine, q, jnp.zeros_like(q)), k, NT)
            pr = jnp.exp2(s * c - pen_b[...] - lse)
            dp = dot(jnp.where(mine, g, jnp.zeros_like(g)), v, NT)
            return s, pr, pr * (dp - delta), off, k

        def finish(p, h, pr, ds, k):
            base = p * 128 + h * HDIM
            if not isinstance(p, int):
                base = pl.multiple_of(base, 64)
            dsb = ds.astype(BF)
            dvt[pl.ds(base, HDIM), i0:L] += dot(gt[pl.ds(base, HDIM), rowsl], pr.astype(BF))
            dkt[pl.ds(base, HDIM), i0:L] += dot(qt[pl.ds(base, HDIM), rowsl], dsb)
            return dot(dsb, k)

        def pair(p, carry_):
            dq = []
            for h in range(2):
                s, pr, ds, off, k = head(p, h)
                dsum[:, i0:L] += ds
                dq.append(finish(p, h, pr, ds, k))
            dqkv[rowsl, pl.ds(off, 128)] = (jnp.where(lane_low(dq[0].shape), dq[0], dq[1]) * scale).astype(BF)
            return carry_

        dsum[:, i0:L] = jnp.zeros((BLOCK, n), F32)
        each = 0.62 * (nb - b)
        for begin, end in ((1, 3), (3, pairs)) if b < 2 else ((1, pairs),):
            lax.fori_loop(begin, end, pair, 0)
            line.worked(each * (end - begin))
        s, pr, ds, off, k = head(0, 1)
        dsum[:, i0:L] += ds
        dq1 = finish(0, 1, pr, ds, k)
        s, pr, ds, off, k = head(0, 0)
        total = dsum[:, i0:L] + ds
        rows = i0 + lax.broadcasted_iota(jnp.int32, (BLOCK, n), 0)
        cols = i0 + lax.broadcasted_iota(jnp.int32, (BLOCK, n), 1)
        picked = (pen_b[...] < 1e29) & (cols > rows) & (startr_ref[0:1, i0:L] == 0) & (s > 0)
        gsel = (split_sum(lower, total) + carry) * (-8.0 / L)
        carry = carry + jnp.sum(total, axis=0, keepdims=True)
        ds = ds + jnp.where(picked, gsel, 0.0)
        dq0 = finish(0, 0, pr, ds, k)
        dqkv[rowsl, 0:128] = (jnp.where(lane_low(dq0.shape), dq0, dq1) * scale).astype(BF)
        line.worked(each * 1.2)
    for p in range(pairs):
        sl = slice(p * 128, (p + 1) * 128)
        dqkv[:, D + p * 128 : D + (p + 1) * 128] = (dkt[sl, :] * scale).T.astype(BF)
        dqkv[:, 2 * D + p * 128 : 2 * D + (p + 1) * 128] = dvt[sl, :].T.astype(BF)

    def normal_of(b):
        values = tokens_ref[b * BLOCK : (b + 1) * BLOCK, :].astype(F32)
        return norm_parts(values)

    for b in range(nb):
        normal, _ = normal_of(b)
        normed = (normal * gain_ref[...] + shift_ref[...]).astype(BF)
        for p in range(pairs):
            qt[p * 128 : (p + 1) * 128, b * BLOCK : (b + 1) * BLOCK] = normed[:, p * 128 : (p + 1) * 128].T
    line.worked(3.0)
    out_copy.wait()
    for j in range(SPLIT):
        for panel in range(3):
            at = slice(panel * D + j * width, panel * D + (j + 1) * width)
            side[:, at] = dot(qt[...], dqkv[:, at]).astype(BF)
        line.now += 2.5
        line.begin(chunks[early + j])
        line.ready()
    sm_acc[0] = small_ref[...]
    sm_acc[0, 0:1, :] = jnp.sum(dqkv[:, 0:D].astype(F32), axis=0, keepdims=True)
    sm_acc[0, 1:2, :] = jnp.sum(dqkv[:, 2 * D : 3 * D].astype(F32), axis=0, keepdims=True)
    res_copies[0].start()
    g_gain = jnp.zeros((1, D), F32)
    g_shift = jnp.zeros((1, D), F32)
    for b in range(nb):
        rowsl = slice(b * BLOCK, (b + 1) * BLOCK)
        if b + 1 < nb:
            res_copies[b + 1].start()
        normal, spread = normal_of(b)
        grad = dot(dqkv[rowsl, :], w_ref[...], NT)
        g_gain = g_gain + jnp.sum(grad * normal, axis=0, keepdims=True)
        g_shift = g_shift + jnp.sum(grad, axis=0, keepdims=True)
        back = norm_back(grad, normal, spread, gain_ref[...])
        res_copies[b].wait()
        gtok[rowsl, :] = (gres[b % 2] + back).astype(BF)
        line.worked(3.0)
    tokens_home = Homeward(place, gtok, tokens_out, home_s.at[1], home_r.at[1], home_l.at[1])
    tokens_home.start()
    line.occupy("plane", 16.0)
    sm_acc[0, 3:4, :] = g_gain
    sm_acc[0, 4:5, :] = g_shift
    z, col = place.z, place.col
    friends = [place.core, place.across_x, place.across_y, (z + 1 - 2 * (z % 2), col), (lax.rem(z + 2, 4), col)]
    smalls = [remote(sm_acc.at[i], sm_rec.at[i], sm_s.at[i], sm_r.at[i], friends[i]) for i in range(5)]
    smalls[0].start()
    for i in range(5):
        line.worked(4.0)
        smalls[i].wait_recv()
        following = sm_acc[i] + sm_rec[i]
        if i < 4:
            sm_acc[i + 1] = following
            smalls[i + 1].start()
        else:
            small_out[...] = following
    line.finish()
    for copy in smalls:
        copy.wait_send()
    output_home.wait()
    tokens_home.wait()


def attn_back_and_sums(q, k, v, g, delta, lse, seg, tokens, gain, shift, w_qkv, small, pen, residual, g_out, down, up, output):
    L, D = q.shape
    start = jnp.concatenate([(seg[:-1] != seg[1:]).astype(jnp.int32), jnp.ones((1,), jnp.int32)])
    N, W = 3 * SPLIT, PANEL // SPLIT
    hbm = pl.BlockSpec(memory_space=pl.ANY)
    vm = pl.BlockSpec(memory_space=pltpu.VMEM)
    dma = pltpu.SemaphoreType.DMA
    shape = jax.ShapeDtypeStruct
    return pl.pallas_call(
        back_kernel,
        out_shape=(shape(down.shape, BF), shape(up.shape, BF), shape((D, 4 * D), BF),
                   shape((8, L // 8, D), BF), shape((8, L // 8, D), BF), shape(small.shape, F32)),
        in_specs=[vm] * 12 + [hbm] * 6,
        out_specs=(hbm,) * 5 + (vm,),
        scratch_shapes=[
            pltpu.VMEM((D, L), BF), pltpu.VMEM((D, L), BF), pltpu.VMEM((D, L), F32), pltpu.VMEM((D, L), F32),
            pltpu.VMEM((BLOCK, L), F32), pltpu.VMEM((2, BLOCK, L), F32), pltpu.VMEM((L, 3 * D), BF),
            pltpu.VMEM((D, 4 * D), BF), pltpu.VMEM((L, D), BF), pltpu.VMEM((2, BLOCK, D), F32),
            pltpu.VMEM((N, 2, PANEL, W), BF), pltpu.VMEM((N, 2, PANEL, W), BF), pltpu.VMEM((N, 2, PANEL // 2, W), BF),
            pltpu.VMEM((N, 2, PANEL // 4, W), BF), pltpu.VMEM((N, 2, 3, PANEL // 16, W), BF),
            pltpu.VMEM((5,) + small.shape, F32), pltpu.VMEM((5,) + small.shape, F32),
            dma((N, 24)), dma((N, 24)), dma((N, 4)), dma((2, 7)), dma((2, 7)), dma((2,)), dma((5,)), dma((5,)),
            dma((2,)), dma((2,)), dma,
        ],
        compiler_params=pltpu.CompilerParams(vmem_limit_bytes=VMEM_LIMIT, collective_id=1, has_side_effects=True),
        name="attn_back_and_sums",
    )(q, k, v, g, delta, lse, start[None, :], tokens, gain[None, :], shift[None, :], w_qkv, small, pen, residual, g_out, down, up, output)


def summed_grads(grads, copies):
    grads = [g / copies for g in grads]
    matrices = [i for i, g in enumerate(grads) if g.ndim == 2]
    vectors = [i for i, g in enumerate(grads) if g.ndim == 1]
    big = lax.psum([grads[i].astype(BF) for i in matrices], ("rows", "cols"))
    small = lax.psum(jnp.concatenate([grads[i] for i in vectors]), ("rows", "cols"))
    out = [None] * len(grads)
    for i, g in zip(matrices, big):
        out[i] = g.astype(F32)
    at = 0
    for i in vectors:
        out[i] = small[at : at + grads[i].shape[0]]
        at += grads[i].shape[0]
    return out


def whole_by_permutes(value):
    parts, cols = value.shape[0], lax.axis_size("cols")
    me = lax.axis_index("cols")
    whole = jnp.zeros_like(value)
    own = lax.dynamic_slice_in_dim(value, me, 1, 0)
    whole = lax.dynamic_update_slice_in_dim(whole, own, me, 0)
    for step in range(1, cols):
        block = lax.dynamic_slice_in_dim(value, lax.rem(me + step, cols), 1, 0)
        block = lax.ppermute(block, "cols", [(i, (i + step) % cols) for i in range(cols)])
        whole = lax.dynamic_update_slice_in_dim(whole, block, lax.rem(me - step + cols, cols), 0)
    return whole


def per_device(tokens, segment_ids, cotangent, *weights):
    seqs, part, width = tokens.shape
    cols = lax.axis_size("cols")
    fitting = (lax.axis_size("rows"), cols, seqs) == (4, 8, 8)
    copies = max(1, cols // seqs)
    held = max(1, seqs // cols)
    first = (lax.axis_index("cols") // copies) * held
    segs = lax.dynamic_slice_in_dim(segment_ids, first, held, 0)
    tokens_whole = to_whole(tokens, copies)
    if fitting:
        cotangent_whole = whole_by_permutes(cotangent).reshape(1, -1, width)
    else:
        cotangent_whole = to_whole(cotangent, copies)
    if fitting:
        down, up, side, grad_tokens, output, small = layer(tokens_whole[0], segs[0], cotangent_whole[0], weights, True)
        return (
            output, grad_tokens.astype(F32), side[:, : 3 * width].astype(F32), small[0], small[1],
            side[:, 3 * width :].astype(F32), small[2], small[3], small[4], small[5], small[6],
            up.astype(F32), small[8:12].reshape(-1), down.astype(F32), small[7])
    results = [
        layer(tokens_whole[s], segs[s], cotangent_whole[s], weights, False) for s in range(held)
    ]
    output = jnp.stack([r[0] for r in results])
    grad_tokens = jnp.stack([r[1] for r in results])
    grads = [sum(parts[1:], parts[0]) for parts in zip(*[r[2] for r in results])]
    return (
        to_parts(output, copies),
        to_parts(grad_tokens.astype(BF), copies).astype(F32),
        *summed_grads(grads, copies),
    )


def solution(mesh):
    placed = (P("rows", "cols", None), P("rows", None), P("rows", "cols", None)) + (P(),) * 13
    return jax.shard_map(
        per_device,
        mesh=mesh,
        in_specs=placed,
        out_specs=(P("rows", "cols", None), P("rows", "cols", None)) + (P(),) * 13,
        check_vma=False,
    )
```

```python
import functools

import jax
import jax.numpy as jnp
from jax import lax
from jax.experimental import pallas as pl
from jax.experimental.pallas import tpu as pltpu
from jax.sharding import PartitionSpec as P

HEADS = 12
HDIM = 64
BF = jnp.bfloat16
F32 = jnp.float32
LOG2E = 1.4426950408889634
BIG = 1e30
BLOCK = 256
MESH = pl.DeviceIdType.MESH
PANEL = 768
SPLIT = 2
STEP = 48
ROWS = 256
VMEM_LIMIT = 62 * 2**20


def to_whole(value, copies):
    if copies > 1:
        value = jnp.repeat(value, copies, axis=0)
    return lax.all_to_all(value, "cols", 0, 1, tiled=True)


def to_parts(value, copies):
    parts = lax.all_to_all(value, "cols", 1, 0, tiled=True)
    return parts[::copies] if copies > 1 else parts


def dot(a, b, dims=((1,), (0,))):
    return lax.dot_general(a, b, (dims, ((), ())), preferred_element_type=F32)


def norm_parts(values):
    average = jnp.mean(values, axis=-1, keepdims=True)
    centered = values - average
    scale = lax.rsqrt(jnp.mean(centered * centered, axis=-1, keepdims=True) + 1e-05)
    return centered * scale, scale


def norm_back(grad, normal, scale, gain):
    weighted = grad * gain
    inner = jnp.mean(weighted * normal, axis=-1, keepdims=True)
    return scale * (weighted - jnp.mean(weighted, axis=-1, keepdims=True) - normal * inner)


def gelu_tanh(values):
    return jax.nn.gelu(values, approximate=True)


NT=((1,),(1,))

def tri(size, upper):
    r=lax.broadcasted_iota(jnp.int32,(size,size),0); c=lax.broadcasted_iota(jnp.int32,(size,size),1)
    return jnp.where(c>r if upper else c<r, 1.0, 0.0).astype(BF)

def split_sum(mask, x):
    hi=x.astype(BF)
    lo=(x-hi.astype(F32)).astype(BF)
    return dot(mask,hi)+dot(mask,lo)

def lane_low(shape):
    return lax.broadcasted_iota(jnp.int32,shape,1) < HDIM

def seg_column(segr_ref, i0):
    shape = (BLOCK, BLOCK)
    same = lax.broadcasted_iota(jnp.int32, shape, 0) == lax.broadcasted_iota(jnp.int32, shape, 1)
    ids = segr_ref[0:1, i0 : i0 + BLOCK].astype(F32)
    return jnp.sum(jnp.where(same, ids, 0.0), axis=1, keepdims=True).astype(jnp.int32)


def attend(q_ref, k_ref, v_ref, seg_ref, o_ref, lse_ref, pen_ref):
    segr_ref, startr_ref = seg_ref.at[0:1], seg_ref.at[1:2]
    L = q_ref.shape[0]
    nb = L // BLOCK
    scale = HDIM**-0.5
    upper = tri(BLOCK, True)
    carry = jnp.zeros((1, L), F32)
    for b in range(nb - 1, -1, -1):
        i0 = b * BLOCK
        n = L - i0
        q0 = q_ref[i0 : i0 + BLOCK, 0:128]
        q0 = jnp.where(lane_low(q0.shape), q0, jnp.zeros_like(q0))
        s = dot(q0, k_ref[i0:L, 0:128], NT) * scale
        rows = i0 + lax.broadcasted_iota(jnp.int32, (BLOCK, n), 0)
        cols = i0 + lax.broadcasted_iota(jnp.int32, (BLOCK, n), 1)
        same = seg_column(segr_ref, i0) == segr_ref[0:1, i0:L]
        picked = same & (cols > rows) & (startr_ref[0:1, i0:L] == 0)
        sel = jnp.where(picked, jnp.maximum(s, 0.0), 0.0)
        if b == nb - 1:
            below = jnp.zeros((1, n), F32)
        else:
            below = jnp.concatenate([jnp.zeros((1, BLOCK), F32), carry], axis=1)
        carried = split_sum(upper, sel) + below
        pen_ref[i0 : i0 + BLOCK, i0:L] = jnp.where(same & (cols >= rows), carried * (8.0 / L * LOG2E), BIG)
        carry = below + jnp.sum(sel, axis=0, keepdims=True)
    c = scale * LOG2E
    for b in range(nb):
        i0 = b * BLOCK
        n = L - i0

        def pair(p, stats, i0=i0, n=n):
            off = pl.multiple_of(p * 128, 128)
            q = q_ref[i0 : i0 + BLOCK, pl.ds(off, 128)]
            k = k_ref[i0:L, pl.ds(off, 128)]
            v = v_ref[i0:L, pl.ds(off, 128)]
            low = lane_low(q.shape)
            lowv = lane_low(v.shape)
            lane = lax.broadcasted_iota(jnp.int32, (BLOCK, 128), 1)
            outs = []
            for h in range(2):
                mine = low if h == 0 else jnp.logical_not(low)
                s = dot(jnp.where(mine, q, jnp.zeros_like(q)), k, NT) * c - pen_ref[i0 : i0 + BLOCK, i0:L]
                m = jnp.max(s, axis=1, keepdims=True)
                e = jnp.exp2(s - m).astype(BF)
                ones = jnp.where(lowv if h == 0 else jnp.logical_not(lowv), v, jnp.ones_like(v))
                o = dot(e, ones)
                total = pltpu.roll(o, HDIM, 1)
                outs.append(o / total)
                stats = jnp.where(lane == 2 * p + h, m + jnp.log2(jnp.where(mine, total, o)), stats)
            o_ref[i0 : i0 + BLOCK, pl.ds(off, 128)] = jnp.where(low, outs[0], outs[1]).astype(BF)
            return stats

        lse_ref[i0 : i0 + BLOCK, :] = lax.fori_loop(0, HEADS // 2, pair, jnp.zeros((BLOCK, 128), F32))


def seg_rows(seg):
    starts = jnp.concatenate([(seg[:-1] != seg[1:]).astype(jnp.int32), jnp.ones((1,), jnp.int32)])
    return jnp.stack([seg, starts])


def attn_fwd(q, k, v, seg):
    L, D = q.shape
    vm = pl.BlockSpec(memory_space=pltpu.VMEM)
    return pl.pallas_call(
        attend,
        out_shape=(
            jax.ShapeDtypeStruct((L, D), BF), jax.ShapeDtypeStruct((L, 128), F32), jax.ShapeDtypeStruct((L, L), F32)),
        in_specs=[vm] * 4,
        out_specs=(vm,) * 3,
        compiler_params=pltpu.CompilerParams(vmem_limit_bytes=VMEM_LIMIT),
        name="attn_fwd",
    )(q, k, v, seg_rows(seg))


def attn_bwd_kernel(q_ref,k_ref,v_ref,g_ref,o_ref,lse_ref,pen_ref,startr_ref,out_ref,qt,gt,dkt,dvt,dsum):
    L,D=q_ref.shape; nb=L//BLOCK
    scale=HDIM**-0.5; c=scale*LOG2E
    pairs=HEADS//2
    lower=tri(BLOCK,False)
    for p in range(pairs):
        qt[p*128:(p+1)*128,:]=q_ref[:,p*128:(p+1)*128].T
        gt[p*128:(p+1)*128,:]=g_ref[:,p*128:(p+1)*128].T
    dkt[...]=jnp.zeros_like(dkt); dvt[...]=jnp.zeros_like(dvt)
    carry=jnp.zeros((1,L),F32)
    for b in range(nb):
        i0=b*BLOCK; n=L-i0
        rowsl=slice(i0,i0+BLOCK)
        carry=carry[:,-n:]
        def head(p,h,i0=i0,n=n,rowsl=rowsl):
            static=isinstance(p,int)
            off=p*128 if static else pl.multiple_of(p*128,128)
            q=q_ref[rowsl,pl.ds(off,128)]; g=g_ref[rowsl,pl.ds(off,128)]; o=o_ref[rowsl,pl.ds(off,128)]
            k=k_ref[i0:L,pl.ds(off,128)]; v=v_ref[i0:L,pl.ds(off,128)]
            low=lane_low(q.shape); mine=low if h==0 else jnp.logical_not(low)
            qm=jnp.where(mine,q,jnp.zeros_like(q)); gm=jnp.where(mine,g,jnp.zeros_like(g))
            lane=lax.broadcasted_iota(jnp.int32,(BLOCK,128),1)
            lse=jnp.sum(jnp.where(lane==2*p+h,lse_ref[rowsl,:],0.0),axis=1,keepdims=True)
            delta=jnp.sum(gm.astype(F32)*o.astype(F32),axis=1,keepdims=True)
            s=dot(qm,k,NT)
            pr=jnp.exp2(s*c-pen_ref[rowsl,i0:L]-lse)
            dp=dot(gm,v,NT)
            ds=pr*(dp-delta)
            return s,pr,ds,off,k
        def finish(p,h,pr,ds,off,k,i0=i0,rowsl=rowsl):
            base=p*128+h*HDIM
            if not isinstance(p,int): base=pl.multiple_of(base,64)
            dsb=ds.astype(BF); prb=pr.astype(BF)
            dvt[pl.ds(base,HDIM),i0:L]+=dot(gt[pl.ds(base,HDIM),rowsl],prb)
            dkt[pl.ds(base,HDIM),i0:L]+=dot(qt[pl.ds(base,HDIM),rowsl],dsb)
            return dot(dsb,k)
        dsum[:,i0:L]=jnp.zeros((BLOCK,n),F32)
        def pair(p,carry_):
            dq=[]
            for h in range(2):
                s,pr,ds,off,k=head(p,h)
                dsum[:,i0:L]+=ds
                dq.append(finish(p,h,pr,ds,off,k))
            out_ref[rowsl,pl.ds(off,128)]=(jnp.where(lane_low(dq[0].shape),dq[0],dq[1])*scale).astype(BF)
            return carry_
        lax.fori_loop(1,pairs,pair,0)
        s,pr,ds,off,k=head(0,1)
        dsum[:,i0:L]+=ds
        dq1=finish(0,1,pr,ds,off,k)
        s,pr,ds,off,k=head(0,0)
        total=dsum[:,i0:L]+ds
        rows=i0+lax.broadcasted_iota(jnp.int32,(BLOCK,n),0)
        cols=i0+lax.broadcasted_iota(jnp.int32,(BLOCK,n),1)
        picked=(pen_ref[rowsl,i0:L]<1e29)&(cols>rows)&(startr_ref[0:1,i0:L]==0)&(s>0)
        gsel=(split_sum(lower,total)+carry)*(-8.0/L)
        carry=carry+jnp.sum(total,axis=0,keepdims=True)
        ds=ds+jnp.where(picked,gsel,0.0)
        dq0=finish(0,0,pr,ds,off,k)
        out_ref[rowsl,0:128]=(jnp.where(lane_low(dq0.shape),dq0,dq1)*scale).astype(BF)
    for p in range(pairs):
        sl=slice(p*128,(p+1)*128)
        out_ref[:,D+p*128:D+(p+1)*128]=(dkt[sl,:]*scale).T.astype(BF)
        out_ref[:,2*D+p*128:2*D+(p+1)*128]=dvt[sl,:].T.astype(BF)

def attn_bwd(q,k,v,g,o,lse,pen,seg):
    L,D=q.shape
    start=jnp.concatenate([(seg[:-1]!=seg[1:]).astype(jnp.int32),jnp.ones((1,),jnp.int32)])
    vm=pl.BlockSpec(memory_space=pltpu.VMEM)
    return pl.pallas_call(attn_bwd_kernel,
        out_shape=jax.ShapeDtypeStruct((L,3*D),BF),
        in_specs=[vm]*8,out_specs=vm,
        scratch_shapes=[pltpu.VMEM((D,L),BF),pltpu.VMEM((D,L),BF),pltpu.VMEM((D,L),F32),pltpu.VMEM((D,L),F32),pltpu.VMEM((BLOCK,L),F32)],
        compiler_params=pltpu.CompilerParams(vmem_limit_bytes=60*2**20),name="attn_bwd")(q,k,v,g,o,lse,pen,start[None,:])


def layer(tokens, segs, cotangent, weights, fused):
    (w_qkv, q_bias, v_bias, w_out, out_bias, attn_gain, attn_shift, mlp_gain, mlp_shift,
     w_up, up_bias, w_down, down_bias) = weights
    width = tokens.shape[-1]
    if fused:
        vectors = jnp.concatenate([q_bias, v_bias, out_bias, attn_gain, attn_shift, mlp_gain, mlp_shift, down_bias, up_bias])
        vectors = vectors.reshape(-1, width)
        rows = seg_rows(segs)
        tokens, cotangent, queries, keys, values, attended, stats, penalty = front(tokens, cotangent, w_qkv, vectors, rows)
        output, grad_attended, grad_residual, delta, g_w_out, g_w_up, g_w_down, small = middle(
            attended, tokens, cotangent, vectors, w_out, w_up, w_down)
        return (output, *attn_back_and_sums(
            queries, keys, values, grad_attended, delta, stats, rows, tokens, vectors, w_qkv, small,
            penalty, grad_residual, g_w_out, g_w_down, g_w_up))
    inputs = tokens.astype(F32)
    normal_one, scale_one = norm_parts(inputs)
    normed = (normal_one * attn_gain + attn_shift).astype(BF)
    projected = dot(normed, w_qkv)
    queries = (projected[:, :width] + q_bias).astype(BF)
    keys = projected[:, width : 2 * width].astype(BF)
    values = (projected[:, 2 * width :] + v_bias).astype(BF)
    attended, stats, penalty = attn_fwd(queries, keys, values, segs)
    residual = inputs + dot(attended, w_out) + out_bias
    normal_two, scale_two = norm_parts(residual)
    normed_two = (normal_two * mlp_gain + mlp_shift).astype(BF)
    upper = dot(normed_two, w_up) + up_bias
    act, gelu_back = jax.vjp(gelu_tanh, upper)
    act = act.astype(BF)
    output = (residual + dot(act, w_down) + down_bias).astype(BF)
    grad_top = cotangent.astype(F32)
    g_down_bias = jnp.sum(grad_top, axis=0)
    g_w_down = dot(act, cotangent, ((0,), (0,)))
    grad_upper = gelu_back(dot(cotangent, w_down, ((1,), (1,))))[0].astype(BF)
    g_up_bias = jnp.sum(grad_upper.astype(F32), axis=0)
    g_w_up = dot(normed_two, grad_upper, ((0,), (0,)))
    grad_two = dot(grad_upper, w_up, ((1,), (1,)))
    g_mlp_gain = jnp.sum(grad_two * normal_two, axis=0)
    g_mlp_shift = jnp.sum(grad_two, axis=0)
    grad_residual = grad_top + norm_back(grad_two, normal_two, scale_two, mlp_gain)
    grad_branch = grad_residual.astype(BF)
    g_out_bias = jnp.sum(grad_branch.astype(F32), axis=0)
    g_w_out = dot(attended, grad_branch, ((0,), (0,)))
    grad_attended = dot(grad_branch, w_out, ((1,), (1,))).astype(BF)
    grad_proj = attn_bwd(queries, keys, values, grad_attended, attended, stats, penalty, segs)
    bias_sums = jnp.sum(grad_proj.astype(F32), axis=0)
    g_q_bias = bias_sums[:width]
    g_v_bias = bias_sums[2 * width :]
    g_w_qkv = dot(normed, grad_proj, ((0,), (0,)))
    grad_one = dot(grad_proj, w_qkv, ((1,), (1,)))
    g_attn_gain = jnp.sum(grad_one * normal_one, axis=0)
    g_attn_shift = jnp.sum(grad_one, axis=0)
    grad_tokens = grad_residual + norm_back(grad_one, normal_one, scale_one, attn_gain)
    return output, grad_tokens, (
        g_w_qkv, g_q_bias, g_v_bias, g_w_out, g_out_bias, g_attn_gain, g_attn_shift,
        g_mlp_gain, g_mlp_shift, g_w_up, g_up_bias, g_w_down, g_down_bias)


def view(ref, tall, panel, row, rows, col, cols):
    if tall:
        return ref.at[pl.ds(pl.multiple_of(panel * PANEL + row, 16), rows), pl.ds(col, cols)]
    return ref.at[pl.ds(pl.multiple_of(row, 16), rows), pl.ds(pl.multiple_of(panel * PANEL + col, 128), cols)]


def add_into(dst, row, rows, parts):
    def turn(i, carry):
        at = pl.multiple_of(i * STEP, 16)
        here = pl.ds(pl.multiple_of(row + at, 16), STEP)
        total = dst[here, :].astype(F32)
        for part in parts:
            total = total + part[pl.ds(at, STEP), :].astype(F32)
        dst[here, :] = total.astype(BF)
        return carry

    lax.fori_loop(0, rows // STEP, turn, 0)


def rows_at(ref, row, rows):
    return ref.at[pl.ds(pl.multiple_of(row, 16), rows), :]


def remote(src, dst, sent, landed, device):
    return pltpu.make_async_remote_copy(
        src_ref=src, dst_ref=dst, send_sem=sent, recv_sem=landed, device_id=device, device_id_type=MESH
    )


class Place:
    def __init__(self):
        self.z, self.col = lax.axis_index("rows"), lax.axis_index("cols")
        z, col = self.z, self.col
        self.y, self.x, self.c = col // 4, (col // 2) % 2, col % 2
        y, x, c = self.y, self.x, self.c
        self.core = (z, y * 4 + x * 2 + (1 - c))
        self.across_x = (z, y * 4 + (1 - x) * 2 + c)
        self.across_y = (z, (1 - y) * 4 + x * 2 + c)
        self.along_z = [(lax.rem(z + d, 4), col) for d in range(1, 4)]
        self.along_cols = [(z, lax.rem(col + d, 8)) for d in range(1, 8)]

    def greet(self, devices):
        barrier = pltpu.get_barrier_semaphore()
        for device in devices:
            pl.semaphore_signal(barrier, inc=1, device_id=device, device_id_type=MESH)
        pl.semaphore_wait(barrier, len(devices))


class Chunk:
    def __init__(self, place, n, source, result, tall, first, buffers, sems):
        own, from_core, from_one, from_two, from_z = [b.at[n] for b in buffers]
        sent, landed, local = sems
        width = own.shape[-1]
        x, y, z, c = place.x, place.y, place.z, place.c
        S = lambda k: sent.at[n, k]
        R = lambda k: landed.at[n, k]
        src = lambda panel, row, rows: view(source, tall, panel, row, rows, first, width)
        out = lambda panel, row, rows: view(result, tall, panel, row, rows, first, width)
        near, far = [x, y], [y, x]
        to_near = [place.across_x, place.across_y]
        to_far = [place.across_y, place.across_x]
        half, quarter, piece = PANEL // 2, PANEL // 4, PANEL // 16
        both = range(2)
        self.own, self.from_core, self.from_one = own, from_core, from_one
        self.from_two, self.from_z = from_two, from_z
        self.half, self.quarter, self.piece = half, quarter, piece
        self.keep1 = [near[u] * half for u in both]
        self.send1 = [(1 - near[u]) * half for u in both]
        self.keep2 = [self.keep1[u] + far[u] * quarter for u in both]
        self.send2 = [self.keep1[u] + (1 - far[u]) * quarter for u in both]
        self.last = [self.keep2[u] + z * piece for u in both]
        final = lambda u: rows_at(own.at[u], self.last[u], piece)
        self.load = [pltpu.make_async_copy(src(2 * c + u, 0, PANEL), own.at[u], local.at[n, u]) for u in both]
        self.core = [remote(src(2 * (1 - c) + u, 0, PANEL), from_core.at[u], S(u), R(u), place.core) for u in both]
        self.one = [remote(rows_at(own.at[u], self.send1[u], half), from_one.at[u], S(2 + u), R(2 + u), to_near[u]) for u in both]
        self.two = [remote(rows_at(own.at[u], self.send2[u], quarter), from_two.at[u], S(4 + u), R(4 + u), to_far[u]) for u in both]
        self.deep = [[remote(rows_at(own.at[u], self.keep2[u] + dev[0] * piece, piece), from_z.at[u, d],
                             S(6 + 3 * u + d), R(6 + 3 * u + d), dev)
                      for d, dev in enumerate(place.along_z)] for u in both]
        self.store = [pltpu.make_async_copy(final(u), out(2 * c + u, self.last[u], piece), local.at[n, 2 + u]) for u in both]
        self.deep_back = [[remote(final(u), out(2 * c + u, self.last[u], piece), S(12 + 3 * u + d), R(12 + 3 * u + d), dev)
                           for d, dev in enumerate(place.along_z)] for u in both]
        same = lambda panel, row, rows, k, dev: remote(out(panel, row, rows), out(panel, row, rows), S(k), R(k), dev)
        self.two_back = [same(2 * c + u, self.keep2[u], quarter, 18 + u, to_far[u]) for u in both]
        self.one_back = [same(2 * c + u, self.keep1[u], half, 20 + u, to_near[u]) for u in both]
        self.core_back = [same(2 * c + u, 0, PANEL, 22 + u, place.core) for u in both]

    def begin(self):
        for copy in self.core + self.load:
            copy.start()

    def step(self, k):
        both = range(2)
        own = [self.own.at[u] for u in both]
        if k == 0:
            for u in both:
                self.load[u].wait()
                self.core[u].wait_recv()
                add_into(own[u], self.send1[u], self.half, [rows_at(self.from_core.at[u], self.send1[u], self.half)])
                self.one[u].start()
            for u in both:
                add_into(own[u], self.keep1[u], self.half, [rows_at(self.from_core.at[u], self.keep1[u], self.half)])
        elif k == 1:
            for u in both:
                self.one[u].wait_recv()
                add_into(own[u], self.send2[u], self.quarter, [rows_at(self.from_one.at[u], self.send2[u] - self.keep1[u], self.quarter)])
                self.two[u].start()
                add_into(own[u], self.keep2[u], self.quarter, [rows_at(self.from_one.at[u], self.keep2[u] - self.keep1[u], self.quarter)])
        elif k == 2:
            for u in both:
                self.two[u].wait_recv()
                add_into(own[u], self.keep2[u], self.quarter, [self.from_two.at[u]])
                for copy in self.deep[u]:
                    copy.start()
        elif k == 3:
            for u in both:
                for copy in self.deep[u]:
                    copy.wait_recv()
                add_into(own[u], self.last[u], self.piece, [self.from_z.at[u, d] for d in range(3)])
                for copy in self.deep_back[u]:
                    copy.start()
                self.store[u].start()
        elif k == 4:
            for u in both:
                for copy in self.deep_back[u]:
                    copy.wait_recv()
                self.store[u].wait()
                self.two_back[u].start()
        elif k == 5:
            for u in both:
                self.two_back[u].wait_recv()
                self.one_back[u].start()
        elif k == 6:
            for u in both:
                self.one_back[u].wait_recv()
                self.core_back[u].start()
        else:
            for u in both:
                self.core_back[u].wait_recv()
            for copy in (self.core + self.one + self.two + self.deep[0] + self.deep[1] + self.deep_back[0]
                         + self.deep_back[1] + self.two_back + self.one_back + self.core_back):
                copy.wait_send()


class Timeline:
    LINK = ["core", "plane", "plane", "deep", "deep", "plane", "plane", "core"]
    TAKES = [2.5, 6.0, 3.0, 6.0, 6.0, 3.0, 6.0, 2.5]
    WORK = [2.0, 1.0, 0.5, 0.5, 0.1, 0.1, 0.1, 0.1]

    def __init__(self):
        self.now = 0.0
        self.free = {"core": 0.0, "plane": 0.0, "deep": 0.0}
        self.moving = {}
        self.after_first = {}

    def occupy(self, link, takes):
        self.free[link] = max(self.free[link], self.now) + takes
        return self.free[link] + 1.5

    def begin(self, chunk, then=None):
        chunk.begin()
        self.moving[chunk] = (self.occupy(self.LINK[0], self.TAKES[0]), 0)
        self.after_first[chunk] = then

    def turn(self, chunk):
        done, k = self.moving.pop(chunk)
        self.now = max(self.now, done)
        chunk.step(k)
        self.now += self.WORK[k]
        if k < 7:
            self.moving[chunk] = (self.occupy(self.LINK[k + 1], self.TAKES[k + 1]), k + 1)
        if k == 0 and self.after_first[chunk]:
            self.after_first[chunk]()

    def ready(self):
        while self.moving:
            chunk = min(self.moving, key=lambda c: self.moving[c][0])
            if self.moving[chunk][0] > self.now:
                return
            self.turn(chunk)

    def worked(self, takes):
        self.now += takes
        self.ready()

    def finish(self):
        while self.moving:
            self.turn(min(self.moving, key=lambda c: self.moving[c][0]))


class Homeward:
    def __init__(self, place, source, result, sent, landed, local):
        part = source.shape[0] // 8
        self.copies = [remote(rows_at(source, dev[1] * part, part), result.at[place.col], sent.at[i], landed.at[i], dev)
                       for i, dev in enumerate(place.along_cols)]
        self.own = pltpu.make_async_copy(rows_at(source, place.col * part, part), result.at[place.col], local)

    def start(self):
        for copy in self.copies:
            copy.start()
        self.own.start()

    def wait(self):
        for copy in self.copies:
            copy.wait()
        self.own.wait()


def back_kernel(q_ref, k_ref, v_ref, g_ref, delta_ref, lse_ref, seg_ref, tokens_ref, vec_ref,
                w_ref, small_ref, pen_ref, residual_ref, g_out_ref, down_ref, up_ref,
                down_out, up_out, side_out, tokens_out, small_out,
                qt, gt, dkt, dvt, dsum, pen, dqkv, side, gtok, gres, own, from_core, from_one, from_two, from_z,
                sm_acc, sm_rec, sent, landed, local, home_s, home_r, home_l, sm_s, sm_r, pen_s, res_s, out_s):
    L, D = q_ref.shape
    nb = L // BLOCK
    scale = HDIM**-0.5
    c = scale * LOG2E
    pairs = HEADS // 2
    width = PANEL // SPLIT
    place = Place()
    vec = lambda row: vec_ref[row : row + 1, :]
    startr_ref = seg_ref.at[1:2]
    place.greet(place.along_cols + place.along_z)
    buffers, sems = (own, from_core, from_one, from_two, from_z), (sent, landed, local)
    chunks = []
    for source, result, tall in ((down_ref, down_out, True), (up_ref, up_out, False), (side, side_out, False)):
        for j in range(SPLIT):
            chunks.append(Chunk(place, len(chunks), source, result, tall, j * width, buffers, sems))
    early = 2 * SPLIT
    line = Timeline()

    def chain(n):
        if n < early:
            line.begin(chunks[n], lambda: chain(n + 1))

    chain(0)
    pen_copies = [pltpu.make_async_copy(pen_ref.at[b * BLOCK : (b + 1) * BLOCK, :], pen.at[b % 2], pen_s.at[b % 2]) for b in range(nb)]
    res_copies = [pltpu.make_async_copy(residual_ref.at[b * BLOCK : (b + 1) * BLOCK, :], gres.at[b % 2], res_s.at[b % 2]) for b in range(nb)]
    pen_copies[0].start()
    out_copy = pltpu.make_async_copy(g_out_ref, side.at[:, 3 * D : 4 * D], out_s)
    out_copy.start()
    for p in range(pairs):
        qt[p * 128 : (p + 1) * 128, :] = q_ref[:, p * 128 : (p + 1) * 128].T
        gt[p * 128 : (p + 1) * 128, :] = g_ref[:, p * 128 : (p + 1) * 128].T
    dkt[...] = jnp.zeros_like(dkt)
    dvt[...] = jnp.zeros_like(dvt)
    line.worked(2.0)
    lower = tri(BLOCK, False)
    carry = jnp.zeros((1, L), F32)
    for b in range(nb):
        i0 = b * BLOCK
        n = L - i0
        rowsl = slice(i0, i0 + BLOCK)
        carry = carry[:, -n:]
        pen_copies[b].wait()
        if b + 1 < nb:
            pen_copies[b + 1].start()
        pen_b = pen.at[b % 2, :, i0:L]

        def head(p, h):
            off = p * 128 if isinstance(p, int) else pl.multiple_of(p * 128, 128)
            q = q_ref[rowsl, pl.ds(off, 128)]
            g = g_ref[rowsl, pl.ds(off, 128)]
            k = k_ref[i0:L, pl.ds(off, 128)]
            v = v_ref[i0:L, pl.ds(off, 128)]
            low = lane_low(q.shape)
            mine = low if h == 0 else jnp.logical_not(low)
            lane = lax.broadcasted_iota(jnp.int32, (BLOCK, 128), 1)
            lse = jnp.sum(jnp.where(lane == 2 * p + h, lse_ref[rowsl, :], 0.0), axis=1, keepdims=True)
            delta = jnp.sum(jnp.where(lane == 2 * p + h, delta_ref[rowsl, :], 0.0), axis=1, keepdims=True)
            s = dot(jnp.where(mine, q, jnp.zeros_like(q)), k, NT)
            pr = jnp.exp2(s * c - pen_b[...] - lse)
            dp = dot(jnp.where(mine, g, jnp.zeros_like(g)), v, NT)
            return s, pr, pr * (dp - delta), off, k

        def finish(p, h, pr, ds, k):
            base = p * 128 + h * HDIM
            if not isinstance(p, int):
                base = pl.multiple_of(base, 64)
            dsb = ds.astype(BF)
            dvt[pl.ds(base, HDIM), i0:L] += dot(gt[pl.ds(base, HDIM), rowsl], pr.astype(BF))
            dkt[pl.ds(base, HDIM), i0:L] += dot(qt[pl.ds(base, HDIM), rowsl], dsb)
            return dot(dsb, k)

        def pair(p, carry_):
            dq = []
            for h in range(2):
                s, pr, ds, off, k = head(p, h)
                dsum[:, i0:L] += ds
                dq.append(finish(p, h, pr, ds, k))
            dqkv[rowsl, pl.ds(off, 128)] = (jnp.where(lane_low(dq[0].shape), dq[0], dq[1]) * scale).astype(BF)
            return carry_

        dsum[:, i0:L] = jnp.zeros((BLOCK, n), F32)
        each = 0.62 * (nb - b)
        for begin, end in ((1, 3), (3, pairs)) if b < 2 else ((1, pairs),):
            lax.fori_loop(begin, end, pair, 0)
            line.worked(each * (end - begin))
        s, pr, ds, off, k = head(0, 1)
        dsum[:, i0:L] += ds
        dq1 = finish(0, 1, pr, ds, k)
        s, pr, ds, off, k = head(0, 0)
        total = dsum[:, i0:L] + ds
        rows = i0 + lax.broadcasted_iota(jnp.int32, (BLOCK, n), 0)
        cols = i0 + lax.broadcasted_iota(jnp.int32, (BLOCK, n), 1)
        picked = (pen_b[...] < 1e29) & (cols > rows) & (startr_ref[0:1, i0:L] == 0) & (s > 0)
        gsel = (split_sum(lower, total) + carry) * (-8.0 / L)
        carry = carry + jnp.sum(total, axis=0, keepdims=True)
        ds = ds + jnp.where(picked, gsel, 0.0)
        dq0 = finish(0, 0, pr, ds, k)
        dqkv[rowsl, 0:128] = (jnp.where(lane_low(dq0.shape), dq0, dq1) * scale).astype(BF)
        line.worked(each * 1.2)
    for p in range(pairs):
        sl = slice(p * 128, (p + 1) * 128)
        dqkv[:, D + p * 128 : D + (p + 1) * 128] = (dkt[sl, :] * scale).T.astype(BF)
        dqkv[:, 2 * D + p * 128 : 2 * D + (p + 1) * 128] = dvt[sl, :].T.astype(BF)

    def normal_of(b):
        values = tokens_ref[b * BLOCK : (b + 1) * BLOCK, :].astype(F32)
        return norm_parts(values)

    for b in range(nb):
        normal, _ = normal_of(b)
        normed = (normal * vec(ROW_GAIN1) + vec(ROW_SHIFT1)).astype(BF)
        for p in range(pairs):
            qt[p * 128 : (p + 1) * 128, b * BLOCK : (b + 1) * BLOCK] = normed[:, p * 128 : (p + 1) * 128].T
    line.worked(3.0)
    out_copy.wait()
    for j in range(SPLIT):
        for panel in range(3):
            at = slice(panel * D + j * width, panel * D + (j + 1) * width)
            side[:, at] = dot(qt[...], dqkv[:, at]).astype(BF)
        line.now += 2.5
        line.begin(chunks[early + j])
        line.ready()
    sm_acc[0] = small_ref[...]
    sm_acc[0, 0:1, :] = jnp.sum(dqkv[:, 0:D].astype(F32), axis=0, keepdims=True)
    sm_acc[0, 1:2, :] = jnp.sum(dqkv[:, 2 * D : 3 * D].astype(F32), axis=0, keepdims=True)
    res_copies[0].start()
    g_gain = jnp.zeros((1, D), F32)
    g_shift = jnp.zeros((1, D), F32)
    for b in range(nb):
        rowsl = slice(b * BLOCK, (b + 1) * BLOCK)
        if b + 1 < nb:
            res_copies[b + 1].start()
        normal, spread = normal_of(b)
        grad = dot(dqkv[rowsl, :], w_ref[...], NT)
        g_gain = g_gain + jnp.sum(grad * normal, axis=0, keepdims=True)
        g_shift = g_shift + jnp.sum(grad, axis=0, keepdims=True)
        back = norm_back(grad, normal, spread, vec(ROW_GAIN1))
        res_copies[b].wait()
        gtok[rowsl, :] = (gres[b % 2] + back).astype(BF)
        line.worked(3.0)
    tokens_home = Homeward(place, gtok, tokens_out, home_s, home_r, home_l)
    tokens_home.start()
    line.occupy("plane", 16.0)
    sm_acc[0, 3:4, :] = g_gain
    sm_acc[0, 4:5, :] = g_shift
    z, col = place.z, place.col
    friends = [place.core, place.across_x, place.across_y, (z + 1 - 2 * (z % 2), col), (lax.rem(z + 2, 4), col)]
    smalls = [remote(sm_acc.at[i], sm_rec.at[i], sm_s.at[i], sm_r.at[i], friends[i]) for i in range(5)]
    smalls[0].start()
    for i in range(5):
        line.worked(4.0)
        smalls[i].wait_recv()
        following = sm_acc[i] + sm_rec[i]
        if i < 4:
            sm_acc[i + 1] = following
            smalls[i + 1].start()
        else:
            small_out[...] = following
    line.finish()
    for copy in smalls:
        copy.wait_send()
    tokens_home.wait()


def attn_back_and_sums(q, k, v, g, delta, lse, segs, tokens, vectors, w_qkv, small, pen, residual, g_out, down, up):
    L, D = q.shape
    N, W = 3 * SPLIT, PANEL // SPLIT
    hbm = pl.BlockSpec(memory_space=pl.ANY)
    vm = pl.BlockSpec(memory_space=pltpu.VMEM)
    dma = pltpu.SemaphoreType.DMA
    shape = jax.ShapeDtypeStruct
    return pl.pallas_call(
        back_kernel,
        out_shape=(shape(down.shape, BF), shape(up.shape, BF), shape((D, 4 * D), BF),
                   shape((8, L // 8, D), BF), shape(small.shape, F32)),
        in_specs=[vm] * 11 + [hbm] * 5,
        out_specs=(hbm,) * 4 + (vm,),
        scratch_shapes=[
            pltpu.VMEM((D, L), BF), pltpu.VMEM((D, L), BF), pltpu.VMEM((D, L), F32), pltpu.VMEM((D, L), F32),
            pltpu.VMEM((BLOCK, L), F32), pltpu.VMEM((2, BLOCK, L), F32), pltpu.VMEM((L, 3 * D), BF),
            pltpu.VMEM((D, 4 * D), BF), pltpu.VMEM((L, D), BF), pltpu.VMEM((2, BLOCK, D), F32),
            pltpu.VMEM((N, 2, PANEL, W), BF), pltpu.VMEM((N, 2, PANEL, W), BF), pltpu.VMEM((N, 2, PANEL // 2, W), BF),
            pltpu.VMEM((N, 2, PANEL // 4, W), BF), pltpu.VMEM((N, 2, 3, PANEL // 16, W), BF),
            pltpu.VMEM((5,) + small.shape, F32), pltpu.VMEM((5,) + small.shape, F32),
            dma((N, 24)), dma((N, 24)), dma((N, 4)), dma((7,)), dma((7,)), dma, dma((5,)), dma((5,)),
            dma((2,)), dma((2,)), dma,
        ],
        compiler_params=pltpu.CompilerParams(vmem_limit_bytes=VMEM_LIMIT, collective_id=1, has_side_effects=True),
        name="attn_back_and_sums",
    )(q, k, v, g, delta, lse, segs, tokens, vectors, w_qkv, small, pen, residual, g_out, down, up)


def front_kernel(tokens_ref, cot_ref, w_ref, vec_ref, seg_ref,
                 tokens_out, cot_out, q_ref, k_ref, v_ref, o_ref, lse_ref, pen_ref,
                 whole, w, sent, landed, local):
    L, D = q_ref.shape
    part = L // 8
    place = Place()
    z, y, x, c, col = place.z, place.y, place.x, place.c, place.col

    def other(k):
        flip = lambda bit, coord: 1 - coord if bit else coord
        return (z, flip(k & 4, y) * 4 + flip(k & 2, x) * 2 + flip(k & 1, c))

    place.greet([other(k) for k in range(1, 8)])
    mine = pl.multiple_of(col * part, 16)
    out = [remote(tokens_ref.at[other(k)[1]], rows_at(whole, mine, part), sent.at[0, k], landed.at[0, k], other(k))
           for k in range(1, 8)]
    own = pltpu.make_async_copy(tokens_ref.at[col], rows_at(whole, mine, part), local.at[0])
    load = pltpu.make_async_copy(w_ref, w, local.at[1])
    cots = [remote(cot_ref.at[other(k)[1]], rows_at(cot_out, mine, part), sent.at[1, k], landed.at[1, k], other(k))
            for k in range(1, 8)]
    cot_own = pltpu.make_async_copy(cot_ref.at[col], rows_at(cot_out, mine, part), local.at[2])
    keep = pltpu.make_async_copy(whole, tokens_out, local.at[3])
    own.start()
    for copy in out:
        copy.start()
    load.start()
    cot_own.start()
    own.wait()
    load.wait()
    vec = lambda row: vec_ref[row : row + 1, :]
    for chip in range(4):
        for k in (2 * chip, 2 * chip + 1):
            if k:
                out[k - 1].wait_recv()
        if chip == 3:
            for copy in cots:
                copy.start()
        first = other(2 * chip)[1] - c
        here = pl.ds(pl.multiple_of(first * part, 16), 2 * part)
        normal, _ = norm_parts(whole[here, :].astype(F32))
        normed = (normal * vec(ROW_GAIN1) + vec(ROW_SHIFT1)).astype(BF)
        q_ref[here, :] = (dot(normed, w[:, 0:D]) + vec(ROW_Q)).astype(BF)
        k_ref[here, :] = dot(normed, w[:, D : 2 * D]).astype(BF)
        v_ref[here, :] = (dot(normed, w[:, 2 * D : 3 * D]) + vec(ROW_V)).astype(BF)
    keep.start()
    attend(q_ref, k_ref, v_ref, seg_ref, o_ref, lse_ref, pen_ref)
    keep.wait()
    cot_own.wait()
    for copy in out:
        copy.wait_send()
    for copy in cots:
        copy.wait()


def front(tokens, cotangent, w_qkv, vectors, segs):
    cols, part, D = tokens.shape
    L = cols * part
    hbm = pl.BlockSpec(memory_space=pl.ANY)
    vm = pl.BlockSpec(memory_space=pltpu.VMEM)
    dma = pltpu.SemaphoreType.DMA
    rows = jax.ShapeDtypeStruct((L, D), BF)
    return pl.pallas_call(
        front_kernel,
        out_shape=(rows,) * 6 + (jax.ShapeDtypeStruct((L, 128), F32), jax.ShapeDtypeStruct((L, L), F32)),
        in_specs=[hbm] * 3 + [vm] * 2,
        out_specs=(hbm,) * 2 + (vm,) * 6,
        scratch_shapes=[pltpu.VMEM((L, D), BF), pltpu.VMEM((D, 3 * D), BF), dma((2, 8)), dma((2, 8)), dma((4,))],
        compiler_params=pltpu.CompilerParams(vmem_limit_bytes=VMEM_LIMIT, collective_id=2, has_side_effects=True),
        name="front",
    )(tokens, cotangent, w_qkv, vectors, segs)


ROW_Q, ROW_V, ROW_OUT, ROW_GAIN1, ROW_SHIFT1, ROW_GAIN2, ROW_SHIFT2, ROW_DOWN, ROW_UP = range(9)


def gelu_pair(u):
    slope = 0.7978845608028654
    square = u * u
    t = jnp.tanh(slope * u * (1.0 + 0.044715 * square))
    half = 0.5 * (1.0 + t)
    return u * half, half + (0.5 * slope) * u * (1.0 - t * t) * (1.0 + 3 * 0.044715 * square)


def middle_kernel(att_ref, tok_ref, cot_ref, vec_ref, w_out_ref, w_up_ref, w_down_ref,
                  output_out, g_ref, res_ref, delta_ref, g_out_ref, g_up_ref, g_down_ref, small_ref,
                  w_out, w_up, w_down, act, gu, n2t, dyt, gb, out, load, sent, landed, local):
    L, D = att_ref.shape
    ff = w_up.shape[1]
    place = Place()
    place.greet(place.along_cols)
    loads = [pltpu.make_async_copy(a, b, load.at[i])
             for i, (a, b) in enumerate(((w_out_ref, w_out), (w_up_ref, w_up), (w_down_ref, w_down)))]
    for copy in loads:
        copy.start()
    small_ref[...] = jnp.zeros_like(small_ref)
    features = lax.broadcasted_iota(jnp.int32, (D, 128), 0) // HDIM
    member = jnp.where(features == lax.broadcasted_iota(jnp.int32, (D, 128), 1), 1.0, 0.0).astype(BF)
    vec = lambda row: vec_ref[row : row + 1, :]

    def add_row(row, values):
        small_ref[row : row + 1, :] += jnp.sum(values, axis=0, keepdims=True)

    for copy in loads:
        copy.wait()

    def block(b, carry):
        here = pl.ds(pl.multiple_of(b * ROWS, ROWS), ROWS)
        att = att_ref[here, :]
        dy = cot_ref[here, :]
        residual = tok_ref[here, :].astype(F32) + dot(att, w_out[...]) + vec(ROW_OUT)
        normal, spread = norm_parts(residual)
        n2 = (normal * vec(ROW_GAIN2) + vec(ROW_SHIFT2)).astype(BF)
        n2t[:, here] = n2.T
        dyt[:, here] = dy.T
        top = dy.astype(F32)
        add_row(ROW_DOWN, top)
        total = residual + vec(ROW_DOWN)
        grad_two = jnp.zeros((ROWS, D), F32)
        for j in range(ff // D):
            part = slice(j * D, (j + 1) * D)
            value, slope = gelu_pair(dot(n2, w_up[:, part]) + vec(ROW_UP + j))
            low = value.astype(BF)
            act[here, part] = low
            total = total + dot(low, w_down[part, :])
            grad = (dot(dy, w_down[part, :], NT) * slope).astype(BF)
            gu[here, part] = grad
            add_row(ROW_UP + j, grad.astype(F32))
            grad_two = grad_two + dot(grad, w_up[:, part], NT)
        out[here, :] = total.astype(BF)
        add_row(ROW_GAIN2, grad_two * normal)
        add_row(ROW_SHIFT2, grad_two)
        grad_residual = top + norm_back(grad_two, normal, spread, vec(ROW_GAIN2))
        res_ref[here, :] = grad_residual
        branch = grad_residual.astype(BF)
        gb[here, :] = branch
        add_row(ROW_OUT, branch.astype(F32))
        grad_att = dot(branch, w_out[...], NT).astype(BF)
        g_ref[here, :] = grad_att
        product = grad_att.astype(F32) * att.astype(F32)
        high = product.astype(BF)
        delta_ref[here, :] = dot(high, member) + dot((product - high.astype(F32)).astype(BF), member)
        return carry

    lax.fori_loop(0, L // ROWS, block, 0)
    home = Homeward(place, out, output_out, sent, landed, local)
    home.start()

    def down(i, carry):
        part = pl.ds(pl.multiple_of(i * 256, 256), 256)
        g_down_ref[part, :] = dot(dyt[...], act[:, part]).astype(BF).T
        return carry

    def up(i, carry):
        part = pl.ds(pl.multiple_of(i * 256, 256), 256)
        g_up_ref[:, part] = dot(n2t[...], gu[:, part]).astype(BF)
        return carry

    lax.fori_loop(0, ff // 256, down, 0)
    lax.fori_loop(0, ff // 256, up, 0)
    g_out_ref[...] = dot(att_ref[...], gb[...], ((0,), (0,))).astype(BF)
    home.wait()


def middle(attended, tokens, cotangent, vectors, w_out, w_up, w_down):
    L, D = attended.shape
    ff = w_up.shape[1]
    hbm = pl.BlockSpec(memory_space=pl.ANY)
    vm = pl.BlockSpec(memory_space=pltpu.VMEM)
    dma = pltpu.SemaphoreType.DMA
    shape = jax.ShapeDtypeStruct
    return pl.pallas_call(
        middle_kernel,
        out_shape=(shape((8, L // 8, D), BF), shape((L, D), BF), shape((L, D), F32), shape((L, 128), F32),
                   shape((D, D), BF), shape((D, ff), BF), shape((ff, D), BF), shape((16, D), F32)),
        in_specs=[vm] * 4 + [hbm] * 3,
        out_specs=(hbm,) + (vm,) * 7,
        scratch_shapes=[
            pltpu.VMEM((D, D), BF), pltpu.VMEM((D, ff), BF), pltpu.VMEM((ff, D), BF), pltpu.VMEM((L, ff), BF),
            pltpu.VMEM((L, ff), BF), pltpu.VMEM((D, L), BF), pltpu.VMEM((D, L), BF), pltpu.VMEM((L, D), BF),
            pltpu.VMEM((L, D), BF), dma((3,)), dma((7,)), dma((7,)), dma,
        ],
        compiler_params=pltpu.CompilerParams(vmem_limit_bytes=VMEM_LIMIT, collective_id=3, has_side_effects=True),
        name="middle",
    )(attended, tokens, cotangent, vectors, w_out, w_up, w_down)


def summed_grads(grads, copies):
    grads = [g / copies for g in grads]
    matrices = [i for i, g in enumerate(grads) if g.ndim == 2]
    vectors = [i for i, g in enumerate(grads) if g.ndim == 1]
    big = lax.psum([grads[i].astype(BF) for i in matrices], ("rows", "cols"))
    small = lax.psum(jnp.concatenate([grads[i] for i in vectors]), ("rows", "cols"))
    out = [None] * len(grads)
    for i, g in zip(matrices, big):
        out[i] = g.astype(F32)
    at = 0
    for i in vectors:
        out[i] = small[at : at + grads[i].shape[0]]
        at += grads[i].shape[0]
    return out


def per_device(tokens, segment_ids, cotangent, *weights):
    seqs, part, width = tokens.shape
    cols = lax.axis_size("cols")
    fitting = (lax.axis_size("rows"), cols, seqs) == (4, 8, 8)
    copies = max(1, cols // seqs)
    held = max(1, seqs // cols)
    first = (lax.axis_index("cols") // copies) * held
    segs = lax.dynamic_slice_in_dim(segment_ids, first, held, 0)
    if fitting:
        output, down, up, side, grad_tokens, small = layer(tokens, segs[0], cotangent, weights, True)
        return (
            output, grad_tokens.astype(F32), side[:, : 3 * width].astype(F32), small[ROW_Q], small[ROW_V],
            side[:, 3 * width :].astype(F32), small[ROW_OUT], small[ROW_GAIN1], small[ROW_SHIFT1], small[ROW_GAIN2],
            small[ROW_SHIFT2], up.astype(F32), small[ROW_UP:12].reshape(-1), down.astype(F32), small[ROW_DOWN])
    tokens_whole = to_whole(tokens, copies)
    cotangent_whole = to_whole(cotangent, copies)
    results = [
        layer(tokens_whole[s], segs[s], cotangent_whole[s], weights, False) for s in range(held)
    ]
    output = jnp.stack([r[0] for r in results])
    grad_tokens = jnp.stack([r[1] for r in results])
    grads = [sum(parts[1:], parts[0]) for parts in zip(*[r[2] for r in results])]
    return (
        to_parts(output, copies),
        to_parts(grad_tokens.astype(BF), copies).astype(F32),
        *summed_grads(grads, copies),
    )


def solution(mesh):
    placed = (P("rows", "cols", None), P("rows", None), P("rows", "cols", None)) + (P(),) * 13
    return jax.shard_map(
        per_device,
        mesh=mesh,
        in_specs=placed,
        out_specs=(P("rows", "cols", None), P("rows", "cols", None)) + (P(),) * 13,
        check_vma=False,
    )
```

```python
import functools

import jax
import jax.numpy as jnp
from jax import lax
from jax.experimental import pallas as pl
from jax.experimental.pallas import tpu as pltpu
from jax.sharding import PartitionSpec as P

HEADS = 12
HDIM = 64
BF = jnp.bfloat16
F32 = jnp.float32
LOG2E = 1.4426950408889634
BIG = 1e30
BLOCK = 256
MESH = pl.DeviceIdType.MESH
PANEL = 768
SPLIT = 3
SLOTS = 2 * SPLIT
LAG = 1.0
STEP = 48
ROWS = 256
VMEM_LIMIT = 62 * 2**20


def to_whole(value, copies):
    if copies > 1:
        value = jnp.repeat(value, copies, axis=0)
    return lax.all_to_all(value, "cols", 0, 1, tiled=True)


def to_parts(value, copies):
    parts = lax.all_to_all(value, "cols", 1, 0, tiled=True)
    return parts[::copies] if copies > 1 else parts


def dot(a, b, dims=((1,), (0,))):
    return lax.dot_general(a, b, (dims, ((), ())), preferred_element_type=F32)


def norm_parts(values):
    average = jnp.mean(values, axis=-1, keepdims=True)
    centered = values - average
    scale = lax.rsqrt(jnp.mean(centered * centered, axis=-1, keepdims=True) + 1e-05)
    return centered * scale, scale


def norm_back(grad, normal, scale, gain):
    weighted = grad * gain
    inner = jnp.mean(weighted * normal, axis=-1, keepdims=True)
    return scale * (weighted - jnp.mean(weighted, axis=-1, keepdims=True) - normal * inner)


def gelu_tanh(values):
    return jax.nn.gelu(values, approximate=True)


NT=((1,),(1,))

def tri(size, upper):
    r=lax.broadcasted_iota(jnp.int32,(size,size),0); c=lax.broadcasted_iota(jnp.int32,(size,size),1)
    return jnp.where(c>r if upper else c<r, 1.0, 0.0).astype(BF)

def split_sum(mask, x):
    hi=x.astype(BF)
    lo=(x-hi.astype(F32)).astype(BF)
    return dot(mask,hi)+dot(mask,lo)

def lane_low(shape):
    return lax.broadcasted_iota(jnp.int32,shape,1) < HDIM

def seg_column(segr_ref, i0):
    shape = (BLOCK, BLOCK)
    same = lax.broadcasted_iota(jnp.int32, shape, 0) == lax.broadcasted_iota(jnp.int32, shape, 1)
    ids = segr_ref[0:1, i0 : i0 + BLOCK].astype(F32)
    return jnp.sum(jnp.where(same, ids, 0.0), axis=1, keepdims=True).astype(jnp.int32)


def attend(q_ref, k_ref, v_ref, seg_ref, o_ref, lse_ref, pen_ref):
    segr_ref, startr_ref = seg_ref.at[0:1], seg_ref.at[1:2]
    L = q_ref.shape[0]
    nb = L // BLOCK
    scale = HDIM**-0.5
    upper = tri(BLOCK, True)
    carry = jnp.zeros((1, L), F32)
    for b in range(nb - 1, -1, -1):
        i0 = b * BLOCK
        n = L - i0
        q0 = q_ref[i0 : i0 + BLOCK, 0:128]
        q0 = jnp.where(lane_low(q0.shape), q0, jnp.zeros_like(q0))
        s = dot(q0, k_ref[i0:L, 0:128], NT) * scale
        rows = i0 + lax.broadcasted_iota(jnp.int32, (BLOCK, n), 0)
        cols = i0 + lax.broadcasted_iota(jnp.int32, (BLOCK, n), 1)
        same = seg_column(segr_ref, i0) == segr_ref[0:1, i0:L]
        picked = same & (cols > rows) & (startr_ref[0:1, i0:L] == 0)
        sel = jnp.where(picked, jnp.maximum(s, 0.0), 0.0)
        if b == nb - 1:
            below = jnp.zeros((1, n), F32)
        else:
            below = jnp.concatenate([jnp.zeros((1, BLOCK), F32), carry], axis=1)
        carried = split_sum(upper, sel) + below
        pen_ref[i0 : i0 + BLOCK, i0:L] = jnp.where(same & (cols >= rows), carried * (8.0 / L * LOG2E), BIG)
        carry = below + jnp.sum(sel, axis=0, keepdims=True)
    c = scale * LOG2E
    for b in range(nb):
        i0 = b * BLOCK
        n = L - i0

        def pair(p, stats, i0=i0, n=n):
            off = pl.multiple_of(p * 128, 128)
            q = q_ref[i0 : i0 + BLOCK, pl.ds(off, 128)]
            k = k_ref[i0:L, pl.ds(off, 128)]
            v = v_ref[i0:L, pl.ds(off, 128)]
            low = lane_low(q.shape)
            lowv = lane_low(v.shape)
            lane = lax.broadcasted_iota(jnp.int32, (BLOCK, 128), 1)
            outs = []
            for h in range(2):
                mine = low if h == 0 else jnp.logical_not(low)
                s = dot(jnp.where(mine, q, jnp.zeros_like(q)), k, NT) * c - pen_ref[i0 : i0 + BLOCK, i0:L]
                m = jnp.max(s, axis=1, keepdims=True)
                e = jnp.exp2(s - m).astype(BF)
                ones = jnp.where(lowv if h == 0 else jnp.logical_not(lowv), v, jnp.ones_like(v))
                o = dot(e, ones)
                total = pltpu.roll(o, HDIM, 1)
                outs.append(o / total)
                stats = jnp.where(lane == 2 * p + h, m + jnp.log2(jnp.where(mine, total, o)), stats)
            o_ref[i0 : i0 + BLOCK, pl.ds(off, 128)] = jnp.where(low, outs[0], outs[1]).astype(BF)
            return stats

        lse_ref[i0 : i0 + BLOCK, :] = lax.fori_loop(0, HEADS // 2, pair, jnp.zeros((BLOCK, 128), F32))


def seg_rows(seg):
    starts = jnp.concatenate([(seg[:-1] != seg[1:]).astype(jnp.int32), jnp.ones((1,), jnp.int32)])
    return jnp.stack([seg, starts])


def attn_fwd(q, k, v, seg):
    L, D = q.shape
    vm = pl.BlockSpec(memory_space=pltpu.VMEM)
    return pl.pallas_call(
        attend,
        out_shape=(
            jax.ShapeDtypeStruct((L, D), BF), jax.ShapeDtypeStruct((L, 128), F32), jax.ShapeDtypeStruct((L, L), F32)),
        in_specs=[vm] * 4,
        out_specs=(vm,) * 3,
        compiler_params=pltpu.CompilerParams(vmem_limit_bytes=VMEM_LIMIT),
        name="attn_fwd",
    )(q, k, v, seg_rows(seg))


def attn_bwd_kernel(q_ref,k_ref,v_ref,g_ref,o_ref,lse_ref,pen_ref,startr_ref,out_ref,qt,gt,dkt,dvt,dsum):
    L,D=q_ref.shape; nb=L//BLOCK
    scale=HDIM**-0.5; c=scale*LOG2E
    pairs=HEADS//2
    lower=tri(BLOCK,False)
    for p in range(pairs):
        qt[p*128:(p+1)*128,:]=q_ref[:,p*128:(p+1)*128].T
        gt[p*128:(p+1)*128,:]=g_ref[:,p*128:(p+1)*128].T
    dkt[...]=jnp.zeros_like(dkt); dvt[...]=jnp.zeros_like(dvt)
    carry=jnp.zeros((1,L),F32)
    for b in range(nb):
        i0=b*BLOCK; n=L-i0
        rowsl=slice(i0,i0+BLOCK)
        carry=carry[:,-n:]
        def head(p,h,i0=i0,n=n,rowsl=rowsl):
            static=isinstance(p,int)
            off=p*128 if static else pl.multiple_of(p*128,128)
            q=q_ref[rowsl,pl.ds(off,128)]; g=g_ref[rowsl,pl.ds(off,128)]; o=o_ref[rowsl,pl.ds(off,128)]
            k=k_ref[i0:L,pl.ds(off,128)]; v=v_ref[i0:L,pl.ds(off,128)]
            low=lane_low(q.shape); mine=low if h==0 else jnp.logical_not(low)
            qm=jnp.where(mine,q,jnp.zeros_like(q)); gm=jnp.where(mine,g,jnp.zeros_like(g))
            lane=lax.broadcasted_iota(jnp.int32,(BLOCK,128),1)
            lse=jnp.sum(jnp.where(lane==2*p+h,lse_ref[rowsl,:],0.0),axis=1,keepdims=True)
            delta=jnp.sum(gm.astype(F32)*o.astype(F32),axis=1,keepdims=True)
            s=dot(qm,k,NT)
            pr=jnp.exp2(s*c-pen_ref[rowsl,i0:L]-lse)
            dp=dot(gm,v,NT)
            ds=pr*(dp-delta)
            return s,pr,ds,off,k
        def finish(p,h,pr,ds,off,k,i0=i0,rowsl=rowsl):
            base=p*128+h*HDIM
            if not isinstance(p,int): base=pl.multiple_of(base,64)
            dsb=ds.astype(BF); prb=pr.astype(BF)
            dvt[pl.ds(base,HDIM),i0:L]+=dot(gt[pl.ds(base,HDIM),rowsl],prb)
            dkt[pl.ds(base,HDIM),i0:L]+=dot(qt[pl.ds(base,HDIM),rowsl],dsb)
            return dot(dsb,k)
        dsum[:,i0:L]=jnp.zeros((BLOCK,n),F32)
        def pair(p,carry_):
            dq=[]
            for h in range(2):
                s,pr,ds,off,k=head(p,h)
                dsum[:,i0:L]+=ds
                dq.append(finish(p,h,pr,ds,off,k))
            out_ref[rowsl,pl.ds(off,128)]=(jnp.where(lane_low(dq[0].shape),dq[0],dq[1])*scale).astype(BF)
            return carry_
        lax.fori_loop(1,pairs,pair,0)
        s,pr,ds,off,k=head(0,1)
        dsum[:,i0:L]+=ds
        dq1=finish(0,1,pr,ds,off,k)
        s,pr,ds,off,k=head(0,0)
        total=dsum[:,i0:L]+ds
        rows=i0+lax.broadcasted_iota(jnp.int32,(BLOCK,n),0)
        cols=i0+lax.broadcasted_iota(jnp.int32,(BLOCK,n),1)
        picked=(pen_ref[rowsl,i0:L]<1e29)&(cols>rows)&(startr_ref[0:1,i0:L]==0)&(s>0)
        gsel=(split_sum(lower,total)+carry)*(-8.0/L)
        carry=carry+jnp.sum(total,axis=0,keepdims=True)
        ds=ds+jnp.where(picked,gsel,0.0)
        dq0=finish(0,0,pr,ds,off,k)
        out_ref[rowsl,0:128]=(jnp.where(lane_low(dq0.shape),dq0,dq1)*scale).astype(BF)
    for p in range(pairs):
        sl=slice(p*128,(p+1)*128)
        out_ref[:,D+p*128:D+(p+1)*128]=(dkt[sl,:]*scale).T.astype(BF)
        out_ref[:,2*D+p*128:2*D+(p+1)*128]=dvt[sl,:].T.astype(BF)

def attn_bwd(q,k,v,g,o,lse,pen,seg):
    L,D=q.shape
    start=jnp.concatenate([(seg[:-1]!=seg[1:]).astype(jnp.int32),jnp.ones((1,),jnp.int32)])
    vm=pl.BlockSpec(memory_space=pltpu.VMEM)
    return pl.pallas_call(attn_bwd_kernel,
        out_shape=jax.ShapeDtypeStruct((L,3*D),BF),
        in_specs=[vm]*8,out_specs=vm,
        scratch_shapes=[pltpu.VMEM((D,L),BF),pltpu.VMEM((D,L),BF),pltpu.VMEM((D,L),F32),pltpu.VMEM((D,L),F32),pltpu.VMEM((BLOCK,L),F32)],
        compiler_params=pltpu.CompilerParams(vmem_limit_bytes=60*2**20),name="attn_bwd")(q,k,v,g,o,lse,pen,start[None,:])


def layer(tokens, segs, cotangent, weights, fused):
    (w_qkv, q_bias, v_bias, w_out, out_bias, attn_gain, attn_shift, mlp_gain, mlp_shift,
     w_up, up_bias, w_down, down_bias) = weights
    width = tokens.shape[-1]
    if fused:
        vectors = jnp.concatenate([q_bias, v_bias, out_bias, attn_gain, attn_shift, mlp_gain, mlp_shift, down_bias, up_bias])
        vectors = vectors.reshape(-1, width)
        rows = seg_rows(segs)
        tokens, cotangent, queries, keys, values, attended, stats, penalty = front(tokens, cotangent, w_qkv, vectors, rows)
        output, grad_tokens, down, up, side, small = rest(
            attended, tokens, cotangent, queries, keys, values, stats, penalty, vectors, rows, w_qkv, w_out, w_up, w_down)[:6]
        return output, down, up, side, grad_tokens, small
    inputs = tokens.astype(F32)
    normal_one, scale_one = norm_parts(inputs)
    normed = (normal_one * attn_gain + attn_shift).astype(BF)
    projected = dot(normed, w_qkv)
    queries = (projected[:, :width] + q_bias).astype(BF)
    keys = projected[:, width : 2 * width].astype(BF)
    values = (projected[:, 2 * width :] + v_bias).astype(BF)
    attended, stats, penalty = attn_fwd(queries, keys, values, segs)
    residual = inputs + dot(attended, w_out) + out_bias
    normal_two, scale_two = norm_parts(residual)
    normed_two = (normal_two * mlp_gain + mlp_shift).astype(BF)
    upper = dot(normed_two, w_up) + up_bias
    act, gelu_back = jax.vjp(gelu_tanh, upper)
    act = act.astype(BF)
    output = (residual + dot(act, w_down) + down_bias).astype(BF)
    grad_top = cotangent.astype(F32)
    g_down_bias = jnp.sum(grad_top, axis=0)
    g_w_down = dot(act, cotangent, ((0,), (0,)))
    grad_upper = gelu_back(dot(cotangent, w_down, ((1,), (1,))))[0].astype(BF)
    g_up_bias = jnp.sum(grad_upper.astype(F32), axis=0)
    g_w_up = dot(normed_two, grad_upper, ((0,), (0,)))
    grad_two = dot(grad_upper, w_up, ((1,), (1,)))
    g_mlp_gain = jnp.sum(grad_two * normal_two, axis=0)
    g_mlp_shift = jnp.sum(grad_two, axis=0)
    grad_residual = grad_top + norm_back(grad_two, normal_two, scale_two, mlp_gain)
    grad_branch = grad_residual.astype(BF)
    g_out_bias = jnp.sum(grad_branch.astype(F32), axis=0)
    g_w_out = dot(attended, grad_branch, ((0,), (0,)))
    grad_attended = dot(grad_branch, w_out, ((1,), (1,))).astype(BF)
    grad_proj = attn_bwd(queries, keys, values, grad_attended, attended, stats, penalty, segs)
    bias_sums = jnp.sum(grad_proj.astype(F32), axis=0)
    g_q_bias = bias_sums[:width]
    g_v_bias = bias_sums[2 * width :]
    g_w_qkv = dot(normed, grad_proj, ((0,), (0,)))
    grad_one = dot(grad_proj, w_qkv, ((1,), (1,)))
    g_attn_gain = jnp.sum(grad_one * normal_one, axis=0)
    g_attn_shift = jnp.sum(grad_one, axis=0)
    grad_tokens = grad_residual + norm_back(grad_one, normal_one, scale_one, attn_gain)
    return output, grad_tokens, (
        g_w_qkv, g_q_bias, g_v_bias, g_w_out, g_out_bias, g_attn_gain, g_attn_shift,
        g_mlp_gain, g_mlp_shift, g_w_up, g_up_bias, g_w_down, g_down_bias)


def view(ref, tall, panel, row, rows, col, cols):
    if tall:
        return ref.at[pl.ds(pl.multiple_of(panel * PANEL + row, 16), rows), pl.ds(col, cols)]
    return ref.at[pl.ds(pl.multiple_of(row, 16), rows), pl.ds(pl.multiple_of(panel * PANEL + col, 128), cols)]


def add_into(dst, row, rows, parts):
    def turn(i, carry):
        at = pl.multiple_of(i * STEP, 16)
        here = pl.ds(pl.multiple_of(row + at, 16), STEP)
        total = dst[here, :].astype(F32)
        for part in parts:
            total = total + part[pl.ds(at, STEP), :].astype(F32)
        dst[here, :] = total.astype(BF)
        return carry

    lax.fori_loop(0, rows // STEP, turn, 0)


def rows_at(ref, row, rows):
    return ref.at[pl.ds(pl.multiple_of(row, 16), rows), :]


def remote(src, dst, sent, landed, device):
    return pltpu.make_async_remote_copy(
        src_ref=src, dst_ref=dst, send_sem=sent, recv_sem=landed, device_id=device, device_id_type=MESH
    )


class Place:
    def __init__(self):
        self.z, self.col = lax.axis_index("rows"), lax.axis_index("cols")
        z, col = self.z, self.col
        self.y, self.x, self.c = col // 4, (col // 2) % 2, col % 2
        y, x, c = self.y, self.x, self.c
        self.core = (z, y * 4 + x * 2 + (1 - c))
        self.across_x = (z, y * 4 + (1 - x) * 2 + c)
        self.across_y = (z, (1 - y) * 4 + x * 2 + c)
        self.along_z = [(lax.rem(z + d, 4), col) for d in range(1, 4)]
        self.along_cols = [(z, lax.rem(col + d, 8)) for d in range(1, 8)]

    def greet(self, devices):
        barrier = pltpu.get_barrier_semaphore()
        for device in devices:
            pl.semaphore_signal(barrier, inc=1, device_id=device, device_id_type=MESH)
        pl.semaphore_wait(barrier, len(devices))


class Chunk:
    def __init__(self, place, n, source, result, tall, first, buffers, sems):
        own, from_core, from_one, from_two, from_z = [b.at[n % SLOTS] for b in buffers]
        sent, landed, local = sems
        width = own.shape[-1]
        x, y, z, c = place.x, place.y, place.z, place.c
        S = lambda k: sent.at[n, k]
        R = lambda k: landed.at[n, k]
        src = lambda panel, row, rows: view(source, tall, panel, row, rows, first, width)
        out = lambda panel, row, rows: view(result, tall, panel, row, rows, first, width)
        near, far = [x, y], [y, x]
        to_near = [place.across_x, place.across_y]
        to_far = [place.across_y, place.across_x]
        half, quarter, piece = PANEL // 2, PANEL // 4, PANEL // 16
        both = range(2)
        self.own, self.from_core, self.from_one = own, from_core, from_one
        self.from_two, self.from_z = from_two, from_z
        self.half, self.quarter, self.piece = half, quarter, piece
        self.keep1 = [near[u] * half for u in both]
        self.send1 = [(1 - near[u]) * half for u in both]
        self.keep2 = [self.keep1[u] + far[u] * quarter for u in both]
        self.send2 = [self.keep1[u] + (1 - far[u]) * quarter for u in both]
        self.last = [self.keep2[u] + z * piece for u in both]
        final = lambda u: rows_at(own.at[u], self.last[u], piece)
        self.load = [pltpu.make_async_copy(src(2 * c + u, 0, PANEL), own.at[u], local.at[n, u]) for u in both]
        self.core = [remote(src(2 * (1 - c) + u, 0, PANEL), from_core.at[u], S(u), R(u), place.core) for u in both]
        self.one = [remote(rows_at(own.at[u], self.send1[u], half), from_one.at[u], S(2 + u), R(2 + u), to_near[u]) for u in both]
        self.two = [remote(rows_at(own.at[u], self.send2[u], quarter), from_two.at[u], S(4 + u), R(4 + u), to_far[u]) for u in both]
        self.deep = [[remote(rows_at(own.at[u], self.keep2[u] + dev[0] * piece, piece), from_z.at[u, d],
                             S(6 + 3 * u + d), R(6 + 3 * u + d), dev)
                      for d, dev in enumerate(place.along_z)] for u in both]
        self.store = [pltpu.make_async_copy(final(u), out(2 * c + u, self.last[u], piece), local.at[n, 2 + u]) for u in both]
        self.deep_back = [[remote(final(u), out(2 * c + u, self.last[u], piece), S(12 + 3 * u + d), R(12 + 3 * u + d), dev)
                           for d, dev in enumerate(place.along_z)] for u in both]
        same = lambda panel, row, rows, k, dev: remote(out(panel, row, rows), out(panel, row, rows), S(k), R(k), dev)
        self.two_back = [same(2 * c + u, self.keep2[u], quarter, 18 + u, to_far[u]) for u in both]
        self.one_back = [same(2 * c + u, self.keep1[u], half, 20 + u, to_near[u]) for u in both]
        self.core_back = [same(2 * c + u, 0, PANEL, 22 + u, place.core) for u in both]

    def begin(self):
        for copy in self.core + self.load:
            copy.start()

    def step(self, k):
        both = range(2)
        own = [self.own.at[u] for u in both]
        if k == 0:
            for u in both:
                self.load[u].wait()
                self.core[u].wait_recv()
                add_into(own[u], self.send1[u], self.half, [rows_at(self.from_core.at[u], self.send1[u], self.half)])
                self.one[u].start()
            for u in both:
                add_into(own[u], self.keep1[u], self.half, [rows_at(self.from_core.at[u], self.keep1[u], self.half)])
        elif k == 1:
            for u in both:
                self.one[u].wait_recv()
                add_into(own[u], self.send2[u], self.quarter, [rows_at(self.from_one.at[u], self.send2[u] - self.keep1[u], self.quarter)])
                self.two[u].start()
                add_into(own[u], self.keep2[u], self.quarter, [rows_at(self.from_one.at[u], self.keep2[u] - self.keep1[u], self.quarter)])
        elif k == 2:
            for u in both:
                self.two[u].wait_recv()
                add_into(own[u], self.keep2[u], self.quarter, [self.from_two.at[u]])
                for copy in self.deep[u]:
                    copy.start()
        elif k == 3:
            for u in both:
                for copy in self.deep[u]:
                    copy.wait_recv()
                add_into(own[u], self.last[u], self.piece, [self.from_z.at[u, d] for d in range(3)])
                for copy in self.deep_back[u]:
                    copy.start()
                self.store[u].start()
        elif k == 4:
            for u in both:
                for copy in self.deep_back[u]:
                    copy.wait_recv()
                self.store[u].wait()
                self.two_back[u].start()
        elif k == 5:
            for u in both:
                self.two_back[u].wait_recv()
                self.one_back[u].start()
        elif k == 6:
            for u in both:
                self.one_back[u].wait_recv()
                self.core_back[u].start()
        else:
            for u in both:
                self.core_back[u].wait_recv()
            for copy in (self.core + self.one + self.two + self.deep[0] + self.deep[1] + self.deep_back[0]
                         + self.deep_back[1] + self.two_back + self.one_back + self.core_back):
                copy.wait_send()


class Timeline:
    LINK = ["core", "plane", "plane", "deep", "deep", "plane", "plane", "core"]
    TAKES = [t * LAG * 2 / SPLIT for t in (2.5, 6.3, 3.2, 5.8, 5.8, 3.2, 6.3, 2.5)]
    WORK = [t * 2 / SPLIT for t in (2.0, 1.0, 0.5, 0.5, 0.1, 0.1, 0.1, 0.1)]

    def __init__(self):
        self.now = 0.0
        self.free = {"core": 0.0, "plane": 0.0, "deep": 0.0}
        self.moving = {}
        self.after_first = {}

    def occupy(self, link, takes):
        self.free[link] = max(self.free[link], self.now) + takes
        return self.free[link] + 2.0

    def begin(self, chunk, then=None):
        chunk.begin()
        self.moving[chunk] = (self.occupy(self.LINK[0], self.TAKES[0]), 0)
        self.after_first[chunk] = then

    def begin_all(self, chunks):
        self.begin(chunks[0], (lambda: self.begin_all(chunks[1:])) if chunks[1:] else None)

    def turn(self, chunk):
        done, k = self.moving.pop(chunk)
        self.now = max(self.now, done)
        chunk.step(k)
        self.now += self.WORK[k]
        if k < 7:
            self.moving[chunk] = (self.occupy(self.LINK[k + 1], self.TAKES[k + 1]), k + 1)
        if k == 0 and self.after_first[chunk]:
            self.after_first[chunk]()

    def ready(self):
        while self.moving:
            chunk = min(self.moving, key=lambda c: self.moving[c][0])
            if self.moving[chunk][0] > self.now:
                return
            self.turn(chunk)

    def worked(self, takes):
        self.now += takes
        self.ready()

    def complete(self, chunk):
        while chunk in self.moving:
            self.turn(min(self.moving, key=lambda c: self.moving[c][0]))

    def finish(self):
        while self.moving:
            self.turn(min(self.moving, key=lambda c: self.moving[c][0]))


class Homeward:
    def __init__(self, place, source, result, sent, landed, local):
        part = source.shape[0] // 8
        self.copies = [remote(rows_at(source, dev[1] * part, part), result.at[place.col], sent.at[i], landed.at[i], dev)
                       for i, dev in enumerate(place.along_cols)]
        self.own = pltpu.make_async_copy(rows_at(source, place.col * part, part), result.at[place.col], local)

    def start(self):
        for copy in self.copies:
            copy.start()
        self.own.start()

    def wait(self):
        for copy in self.copies:
            copy.wait()
        self.own.wait()


def front_kernel(tokens_ref, cot_ref, w_ref, vec_ref, seg_ref,
                 tokens_out, cot_out, q_ref, k_ref, v_ref, o_ref, lse_ref, pen_ref,
                 whole, w, sent, landed, local):
    L, D = q_ref.shape
    part = L // 8
    place = Place()
    z, y, x, c, col = place.z, place.y, place.x, place.c, place.col

    def other(k):
        flip = lambda bit, coord: 1 - coord if bit else coord
        return (z, flip(k & 4, y) * 4 + flip(k & 2, x) * 2 + flip(k & 1, c))

    place.greet([other(k) for k in range(1, 8)])
    mine = pl.multiple_of(col * part, 16)
    out = [remote(tokens_ref.at[other(k)[1]], rows_at(whole, mine, part), sent.at[0, k], landed.at[0, k], other(k))
           for k in range(1, 8)]
    own = pltpu.make_async_copy(tokens_ref.at[col], rows_at(whole, mine, part), local.at[0])
    load = pltpu.make_async_copy(w_ref, w, local.at[1])
    cots = [remote(cot_ref.at[other(k)[1]], rows_at(cot_out, mine, part), sent.at[1, k], landed.at[1, k], other(k))
            for k in range(1, 8)]
    cot_own = pltpu.make_async_copy(cot_ref.at[col], rows_at(cot_out, mine, part), local.at[2])
    keep = pltpu.make_async_copy(whole, tokens_out, local.at[3])
    own.start()
    for copy in out:
        copy.start()
    load.start()
    cot_own.start()
    own.wait()
    load.wait()
    vec = lambda row: vec_ref[row : row + 1, :]
    for chip in range(4):
        for k in (2 * chip, 2 * chip + 1):
            if k:
                out[k - 1].wait_recv()
        if chip == 3:
            for copy in cots:
                copy.start()
        first = other(2 * chip)[1] - c
        here = pl.ds(pl.multiple_of(first * part, 16), 2 * part)
        normal, _ = norm_parts(whole[here, :].astype(F32))
        normed = (normal * vec(ROW_GAIN1) + vec(ROW_SHIFT1)).astype(BF)
        q_ref[here, :] = (dot(normed, w[:, 0:D]) + vec(ROW_Q)).astype(BF)
        k_ref[here, :] = dot(normed, w[:, D : 2 * D]).astype(BF)
        v_ref[here, :] = (dot(normed, w[:, 2 * D : 3 * D]) + vec(ROW_V)).astype(BF)
    keep.start()
    attend(q_ref, k_ref, v_ref, seg_ref, o_ref, lse_ref, pen_ref)
    keep.wait()
    cot_own.wait()
    for copy in out:
        copy.wait_send()
    for copy in cots:
        copy.wait()


def front(tokens, cotangent, w_qkv, vectors, segs):
    cols, part, D = tokens.shape
    L = cols * part
    hbm = pl.BlockSpec(memory_space=pl.ANY)
    vm = pl.BlockSpec(memory_space=pltpu.VMEM)
    dma = pltpu.SemaphoreType.DMA
    rows = jax.ShapeDtypeStruct((L, D), BF)
    return pl.pallas_call(
        front_kernel,
        out_shape=(rows,) * 6 + (jax.ShapeDtypeStruct((L, 128), F32), jax.ShapeDtypeStruct((L, L), F32)),
        in_specs=[hbm] * 3 + [vm] * 2,
        out_specs=(hbm,) * 2 + (vm,) * 6,
        scratch_shapes=[pltpu.VMEM((L, D), BF), pltpu.VMEM((D, 3 * D), BF), dma((2, 8)), dma((2, 8)), dma((4,))],
        compiler_params=pltpu.CompilerParams(vmem_limit_bytes=VMEM_LIMIT, collective_id=2, has_side_effects=True),
        name="front",
    )(tokens, cotangent, w_qkv, vectors, segs)


ROW_Q, ROW_V, ROW_OUT, ROW_GAIN1, ROW_SHIFT1, ROW_GAIN2, ROW_SHIFT2, ROW_DOWN, ROW_UP = range(9)


def gelu_pair(u):
    slope = 0.7978845608028654
    square = u * u
    t = jnp.tanh(slope * u * (1.0 + 0.044715 * square))
    half = 0.5 * (1.0 + t)
    return u * half, half + (0.5 * slope) * u * (1.0 - t * t) * (1.0 + 3 * 0.044715 * square)


def rest_kernel(att_hbm, tok_hbm, cot_hbm, q_hbm, k_hbm, v_hbm, lse_hbm, pen_hbm, vec_ref, seg_ref,
                w_qkv_hbm, w_out_hbm, w_up_hbm, w_down_hbm,
                output_out, tokens_out, down_out, up_out, side_out, small_out, down_part, up_part, out_part, res_part,
                tok, g, delta, sm_acc, sm_rec, own, from_core, from_one, from_two, from_z,
                sent, landed, local, home_s, home_r, home_l, sm_s, sm_r, in_s, stage_s, res_s, pen_s):
    L, D = tok.shape
    ff = w_up_hbm.shape[1]
    nb = L // BLOCK
    width = PANEL // SPLIT
    pairs = HEADS // 2
    place = Place()
    place.greet(place.along_cols + place.along_z)
    buffers, sems = (own, from_core, from_one, from_two, from_z), (sent, landed, local)
    chunks = []
    for source, result, tall in ((down_part, down_out, True), (up_part, up_out, False)):
        for j in range(SPLIT):
            chunks.append(Chunk(place, len(chunks), source, result, tall, j * width, buffers, sems))
    line = Timeline()
    vec = lambda row: vec_ref[row : row + 1, :]
    sm_acc[0] = jnp.zeros_like(sm_acc[0])

    def add_row(row, values):
        sm_acc[0, row : row + 1, :] += jnp.sum(values, axis=0, keepdims=True)

    def feed_forward(w_out, w_up, w_down, act, gu, n2t, gb, out, att, cot, res, stage):
        loads = [pltpu.make_async_copy(a, b, in_s.at[i]) for i, (a, b) in enumerate((
            (att_hbm, att), (tok_hbm, tok), (w_out_hbm, w_out), (cot_hbm, cot), (w_up_hbm, w_up), (w_down_hbm, w_down)))]
        for copy in loads:
            copy.start()
        features = lax.broadcasted_iota(jnp.int32, (D, 128), 0) // HDIM
        member = jnp.where(features == lax.broadcasted_iota(jnp.int32, (D, 128), 1), 1.0, 0.0).astype(BF)
        for copy in loads:
            copy.wait()

        def forward(b, carry):
            here = pl.ds(pl.multiple_of(b * ROWS, ROWS), ROWS)
            dy = cot[here, :]
            residual = tok[here, :].astype(F32) + dot(att[here, :], w_out[...]) + vec(ROW_OUT)
            res[here, :] = residual
            normal, _ = norm_parts(residual)
            n2 = (normal * vec(ROW_GAIN2) + vec(ROW_SHIFT2)).astype(BF)
            n2t[:, here] = n2.T
            add_row(ROW_DOWN, dy.astype(F32))
            total = residual + vec(ROW_DOWN)
            for j in range(ff // D):
                part = slice(j * D, (j + 1) * D)
                value, slope = gelu_pair(dot(n2, w_up[:, part]) + vec(ROW_UP + j))
                low = value.astype(BF)
                act[here, part] = low
                gu[here, part] = slope.astype(BF)
                total = total + dot(low, w_down[part, :])
            out[here, :] = total.astype(BF)
            return carry

        def backward(b):
            here = slice(b * ROWS, (b + 1) * ROWS)
            dy = cot[here, :]
            normal, spread = norm_parts(res[here, :])
            grad_two = jnp.zeros((ROWS, D), F32)
            for j in range(ff // D):
                part = slice(j * D, (j + 1) * D)
                grad = (dot(dy, w_down[part, :], NT) * gu[here, part].astype(F32)).astype(BF)
                gu[here, part] = grad
                add_row(ROW_UP + j, grad.astype(F32))
                grad_two = grad_two + dot(grad, w_up[:, part], NT)
            add_row(ROW_GAIN2, grad_two * normal)
            add_row(ROW_SHIFT2, grad_two)
            grad_residual = dy.astype(F32) + norm_back(grad_two, normal, spread, vec(ROW_GAIN2))
            res[here, :] = grad_residual
            branch = grad_residual.astype(BF)
            gb[here, :] = branch
            add_row(ROW_OUT, branch.astype(F32))
            grad_att = dot(branch, w_out[...], NT).astype(BF)
            g[here, :] = grad_att
            product = grad_att.astype(F32) * att[here, :].astype(F32)
            high = product.astype(BF)
            delta[here, :] = dot(high, member) + dot((product - high.astype(F32)).astype(BF), member)

        lax.fori_loop(0, L // ROWS, forward, 0)
        home = Homeward(place, out, output_out, home_s.at[0], home_r.at[0], home_l.at[0])
        home.start()
        line.occupy("plane", 16.0)
        tiles = ff // 256
        stored = [pltpu.make_async_copy(stage.at[i % 2], down_part.at[i * 256 : (i + 1) * 256, :], stage_s.at[i % 2])
                  for i in range(tiles)]
        for i in range(tiles):
            if i > 1:
                stored[i - 2].wait()
            stage[i % 2] = dot(act[:, i * 256 : (i + 1) * 256], cot[...], ((0,), (0,))).astype(BF)
            stored[i].start()
        stored[tiles - 2].wait()
        stored[tiles - 1].wait()
        line.worked(6.0)
        line.begin_all(chunks[:SPLIT])
        for b in range(L // ROWS):
            backward(b)
            line.worked(4.3)
        tiles = ff // D
        spread = [pltpu.make_async_copy(w_down.at[i * D : (i + 1) * D, :], up_part.at[:, i * D : (i + 1) * D], stage_s.at[2 + i])
                  for i in range(tiles)]
        for i in range(tiles):
            for j in range(D // 256):
                w_down[i * D : (i + 1) * D, j * 256 : (j + 1) * 256] = dot(n2t[...], gu[:, i * D + j * 256 : i * D + (j + 1) * 256]).astype(BF)
            spread[i].start()
            line.worked(1.6)
        w_out[...] = dot(att[...], gb[...], ((0,), (0,))).astype(BF)
        keep = [pltpu.make_async_copy(w_out, out_part, res_s.at[0]), pltpu.make_async_copy(res, res_part, res_s.at[1])]
        for copy in keep:
            copy.start()
        for copy in spread:
            copy.wait()
        line.worked(1.5)
        line.begin_all(chunks[SPLIT:])
        for copy in keep:
            copy.wait()
        home.wait()

    dma = pltpu.SemaphoreType.DMA
    pl.run_scoped(
        feed_forward, pltpu.VMEM((D, D), BF), pltpu.VMEM((D, ff), BF), pltpu.VMEM((ff, D), BF), pltpu.VMEM((L, ff), BF),
        pltpu.VMEM((L, ff), BF), pltpu.VMEM((D, L), BF), pltpu.VMEM((L, D), BF),
        pltpu.VMEM((L, D), BF), pltpu.VMEM((L, D), BF), pltpu.VMEM((L, D), BF), pltpu.VMEM((L, D), F32),
        pltpu.VMEM((2, 256, D), BF))

    def attention(q_ref, k_ref, v_ref, lse_ref, w_ref, qt, gt, dkt, dvt, dsum, pen, dqkv, side, gtok, gres):
        scale = HDIM**-0.5
        c = scale * LOG2E
        startr_ref = seg_ref.at[1:2]
        loads = [pltpu.make_async_copy(a, b, in_s.at[i]) for i, (a, b) in enumerate((
            (q_hbm, q_ref), (k_hbm, k_ref), (v_hbm, v_ref), (lse_hbm, lse_ref), (w_qkv_hbm, w_ref)))]
        pen_copies = [pltpu.make_async_copy(pen_hbm.at[b * BLOCK : (b + 1) * BLOCK, :], pen.at[b % 2], pen_s.at[b % 2])
                      for b in range(nb)]
        res_copies = [pltpu.make_async_copy(res_part.at[b * BLOCK : (b + 1) * BLOCK, :], gres.at[b % 2], res_s.at[b % 2])
                      for b in range(nb)]
        for copy in loads[:4]:
            copy.start()
        pen_copies[0].start()
        loads[4].start()
        out_copy = pltpu.make_async_copy(out_part, side.at[:, 3 * D : 4 * D], in_s.at[5])
        out_copy.start()
        dkt[...] = jnp.zeros_like(dkt)
        dvt[...] = jnp.zeros_like(dvt)
        for p in range(pairs):
            gt[p * 128 : (p + 1) * 128, :] = g[:, p * 128 : (p + 1) * 128].T
        for copy in loads[:4]:
            copy.wait()
        for p in range(pairs):
            qt[p * 128 : (p + 1) * 128, :] = q_ref[:, p * 128 : (p + 1) * 128].T
        line.worked(3.0)
        lower = tri(BLOCK, False)
        carry = jnp.zeros((1, L), F32)
        for b in range(nb):
            i0 = b * BLOCK
            n = L - i0
            rowsl = slice(i0, i0 + BLOCK)
            carry = carry[:, -n:]
            pen_copies[b].wait()
            if b + 1 < nb:
                pen_copies[b + 1].start()
            pen_b = pen.at[b % 2, :, i0:L]

            def head(p, h):
                off = p * 128 if isinstance(p, int) else pl.multiple_of(p * 128, 128)
                q = q_ref[rowsl, pl.ds(off, 128)]
                gh = g[rowsl, pl.ds(off, 128)]
                k = k_ref[i0:L, pl.ds(off, 128)]
                v = v_ref[i0:L, pl.ds(off, 128)]
                low = lane_low(q.shape)
                mine = low if h == 0 else jnp.logical_not(low)
                lane = lax.broadcasted_iota(jnp.int32, (BLOCK, 128), 1)
                lse = jnp.sum(jnp.where(lane == 2 * p + h, lse_ref[rowsl, :], 0.0), axis=1, keepdims=True)
                shift = jnp.sum(jnp.where(lane == 2 * p + h, delta[rowsl, :], 0.0), axis=1, keepdims=True)
                s = dot(jnp.where(mine, q, jnp.zeros_like(q)), k, NT)
                pr = jnp.exp2(s * c - pen_b[...] - lse)
                dp = dot(jnp.where(mine, gh, jnp.zeros_like(gh)), v, NT)
                return s, pr, pr * (dp - shift), off, k

            def finish(p, h, pr, ds, k):
                base = p * 128 + h * HDIM
                if not isinstance(p, int):
                    base = pl.multiple_of(base, 64)
                dsb = ds.astype(BF)
                dvt[pl.ds(base, HDIM), i0:L] += dot(gt[pl.ds(base, HDIM), rowsl], pr.astype(BF))
                dkt[pl.ds(base, HDIM), i0:L] += dot(qt[pl.ds(base, HDIM), rowsl], dsb)
                return dot(dsb, k)

            def pair(p, carry_):
                dq = []
                for h in range(2):
                    s, pr, ds, off, k = head(p, h)
                    dsum[:, i0:L] += ds
                    dq.append(finish(p, h, pr, ds, k))
                dqkv[rowsl, pl.ds(off, 128)] = (jnp.where(lane_low(dq[0].shape), dq[0], dq[1]) * scale).astype(BF)
                return carry_

            dsum[:, i0:L] = jnp.zeros((BLOCK, n), F32)
            each = 0.42 * (nb - b)
            for begin, end in ((1, 3), (3, pairs)) if b < 2 else ((1, pairs),):
                lax.fori_loop(begin, end, pair, 0)
                line.worked(each * (end - begin))
            s, pr, ds, off, k = head(0, 1)
            dsum[:, i0:L] += ds
            dq1 = finish(0, 1, pr, ds, k)
            s, pr, ds, off, k = head(0, 0)
            total = dsum[:, i0:L] + ds
            rows = i0 + lax.broadcasted_iota(jnp.int32, (BLOCK, n), 0)
            cols = i0 + lax.broadcasted_iota(jnp.int32, (BLOCK, n), 1)
            picked = (pen_b[...] < 1e29) & (cols > rows) & (startr_ref[0:1, i0:L] == 0) & (s > 0)
            gsel = (split_sum(lower, total) + carry) * (-8.0 / L)
            carry = carry + jnp.sum(total, axis=0, keepdims=True)
            ds = ds + jnp.where(picked, gsel, 0.0)
            dq0 = finish(0, 0, pr, ds, k)
            dqkv[rowsl, 0:128] = (jnp.where(lane_low(dq0.shape), dq0, dq1) * scale).astype(BF)
            line.worked(each * 1.2)
        for p in range(pairs):
            sl = slice(p * 128, (p + 1) * 128)
            dqkv[:, D + p * 128 : D + (p + 1) * 128] = (dkt[sl, :] * scale).T.astype(BF)
            dqkv[:, 2 * D + p * 128 : 2 * D + (p + 1) * 128] = dvt[sl, :].T.astype(BF)

        def normal_of(b):
            return norm_parts(tok[b * BLOCK : (b + 1) * BLOCK, :].astype(F32))

        for b in range(nb):
            normal, _ = normal_of(b)
            normed = (normal * vec(ROW_GAIN1) + vec(ROW_SHIFT1)).astype(BF)
            for p in range(pairs):
                qt[p * 128 : (p + 1) * 128, b * BLOCK : (b + 1) * BLOCK] = normed[:, p * 128 : (p + 1) * 128].T
        line.worked(3.0)
        out_copy.wait()
        for j in range(SPLIT):
            for panel in range(3):
                at = slice(panel * D + j * width, panel * D + (j + 1) * width)
                side[:, at] = dot(qt[...], dqkv[:, at]).astype(BF)
            line.now += 5.0 / SPLIT
            line.complete(chunks[j])
            line.begin(Chunk(place, 2 * SPLIT + j, side, side_out, False, j * width, buffers, sems))
            line.ready()
        sm_acc[0, 0:1, :] = jnp.sum(dqkv[:, 0:D].astype(F32), axis=0, keepdims=True)
        sm_acc[0, 1:2, :] = jnp.sum(dqkv[:, 2 * D : 3 * D].astype(F32), axis=0, keepdims=True)
        res_copies[0].start()
        loads[4].wait()
        g_gain = jnp.zeros((1, D), F32)
        g_shift = jnp.zeros((1, D), F32)
        for b in range(nb):
            rowsl = slice(b * BLOCK, (b + 1) * BLOCK)
            if b + 1 < nb:
                res_copies[b + 1].start()
            normal, spread = normal_of(b)
            grad = dot(dqkv[rowsl, :], w_ref[...], NT)
            g_gain = g_gain + jnp.sum(grad * normal, axis=0, keepdims=True)
            g_shift = g_shift + jnp.sum(grad, axis=0, keepdims=True)
            back = norm_back(grad, normal, spread, vec(ROW_GAIN1))
            res_copies[b].wait()
            gtok[rowsl, :] = (gres[b % 2] + back).astype(BF)
            line.worked(2.0)
        tokens_home = Homeward(place, gtok, tokens_out, home_s.at[1], home_r.at[1], home_l.at[1])
        tokens_home.start()
        line.occupy("plane", 16.0)
        sm_acc[0, 3:4, :] = g_gain
        sm_acc[0, 4:5, :] = g_shift
        z, col = place.z, place.col
        friends = [place.core, place.across_x, place.across_y, (z + 1 - 2 * (z % 2), col), (lax.rem(z + 2, 4), col)]
        smalls = [remote(sm_acc.at[i], sm_rec.at[i], sm_s.at[i], sm_r.at[i], friends[i]) for i in range(5)]
        smalls[0].start()
        for i in range(5):
            line.worked(4.0)
            smalls[i].wait_recv()
            following = sm_acc[i] + sm_rec[i]
            if i < 4:
                sm_acc[i + 1] = following
                smalls[i + 1].start()
            else:
                small_out[...] = following
        line.finish()
        for copy in smalls:
            copy.wait_send()
        tokens_home.wait()

    pl.run_scoped(
        attention, pltpu.VMEM((L, D), BF), pltpu.VMEM((L, D), BF), pltpu.VMEM((L, D), BF), pltpu.VMEM((L, 128), F32),
        pltpu.VMEM((D, 3 * D), BF), pltpu.VMEM((D, L), BF), pltpu.VMEM((D, L), BF), pltpu.VMEM((D, L), F32),
        pltpu.VMEM((D, L), F32), pltpu.VMEM((BLOCK, L), F32), pltpu.VMEM((2, BLOCK, L), F32), pltpu.VMEM((L, 3 * D), BF),
        pltpu.VMEM((D, 4 * D), BF), pltpu.VMEM((L, D), BF), pltpu.VMEM((2, BLOCK, D), F32))


def rest(attended, tokens, cotangent, q, k, v, lse, pen, vectors, segs, w_qkv, w_out, w_up, w_down):
    L, D = attended.shape
    ff = w_up.shape[1]
    N, W = 3 * SPLIT, PANEL // SPLIT
    hbm = pl.BlockSpec(memory_space=pl.ANY)
    vm = pl.BlockSpec(memory_space=pltpu.VMEM)
    dma = pltpu.SemaphoreType.DMA
    shape = jax.ShapeDtypeStruct
    rows = shape((8, L // 8, D), BF)
    wide, tall = shape((D, ff), BF), shape((ff, D), BF)
    return pl.pallas_call(
        rest_kernel,
        out_shape=(rows, rows, tall, wide, wide, shape((16, D), F32), tall, wide, shape((D, D), BF), shape((L, D), F32)),
        in_specs=[hbm] * 8 + [vm] * 2 + [hbm] * 4,
        out_specs=(hbm,) * 5 + (vm,) + (hbm,) * 4,
        scratch_shapes=[
            pltpu.VMEM((L, D), BF), pltpu.VMEM((L, D), BF), pltpu.VMEM((L, 128), F32), pltpu.VMEM((5, 16, D), F32),
            pltpu.VMEM((5, 16, D), F32), pltpu.VMEM((SLOTS, 2, PANEL, W), BF), pltpu.VMEM((SLOTS, 2, PANEL, W), BF),
            pltpu.VMEM((SLOTS, 2, PANEL // 2, W), BF), pltpu.VMEM((SLOTS, 2, PANEL // 4, W), BF),
            pltpu.VMEM((SLOTS, 2, 3, PANEL // 16, W), BF),
            dma((N, 24)), dma((N, 24)), dma((N, 4)), dma((2, 7)), dma((2, 7)), dma((2,)), dma((5,)), dma((5,)),
            dma((6,)), dma((6,)), dma((2,)), dma((2,)),
        ],
        compiler_params=pltpu.CompilerParams(vmem_limit_bytes=VMEM_LIMIT, collective_id=1, has_side_effects=True),
        name="rest",
    )(attended, tokens, cotangent, q, k, v, lse, pen, vectors, segs, w_qkv, w_out, w_up, w_down)


def summed_grads(grads, copies):
    grads = [g / copies for g in grads]
    matrices = [i for i, g in enumerate(grads) if g.ndim == 2]
    vectors = [i for i, g in enumerate(grads) if g.ndim == 1]
    big = lax.psum([grads[i].astype(BF) for i in matrices], ("rows", "cols"))
    small = lax.psum(jnp.concatenate([grads[i] for i in vectors]), ("rows", "cols"))
    out = [None] * len(grads)
    for i, g in zip(matrices, big):
        out[i] = g.astype(F32)
    at = 0
    for i in vectors:
        out[i] = small[at : at + grads[i].shape[0]]
        at += grads[i].shape[0]
    return out


def per_device(tokens, segment_ids, cotangent, *weights):
    seqs, part, width = tokens.shape
    cols = lax.axis_size("cols")
    fitting = (lax.axis_size("rows"), cols, seqs) == (4, 8, 8)
    copies = max(1, cols // seqs)
    held = max(1, seqs // cols)
    first = (lax.axis_index("cols") // copies) * held
    segs = lax.dynamic_slice_in_dim(segment_ids, first, held, 0)
    if fitting:
        output, down, up, side, grad_tokens, small = layer(tokens, segs[0], cotangent, weights, True)
        return (
            output, grad_tokens.astype(F32), side[:, : 3 * width].astype(F32), small[ROW_Q], small[ROW_V],
            side[:, 3 * width :].astype(F32), small[ROW_OUT], small[ROW_GAIN1], small[ROW_SHIFT1], small[ROW_GAIN2],
            small[ROW_SHIFT2], up.astype(F32), small[ROW_UP:12].reshape(-1), down.astype(F32), small[ROW_DOWN])
    tokens_whole = to_whole(tokens, copies)
    cotangent_whole = to_whole(cotangent, copies)
    results = [
        layer(tokens_whole[s], segs[s], cotangent_whole[s], weights, False) for s in range(held)
    ]
    output = jnp.stack([r[0] for r in results])
    grad_tokens = jnp.stack([r[1] for r in results])
    grads = [sum(parts[1:], parts[0]) for parts in zip(*[r[2] for r in results])]
    return (
        to_parts(output, copies),
        to_parts(grad_tokens.astype(BF), copies).astype(F32),
        *summed_grads(grads, copies),
    )


def solution(mesh):
    placed = (P("rows", "cols", None), P("rows", None), P("rows", "cols", None)) + (P(),) * 13
    return jax.shard_map(
        per_device,
        mesh=mesh,
        in_specs=placed,
        out_specs=(P("rows", "cols", None), P("rows", "cols", None)) + (P(),) * 13,
        check_vma=False,
    )
```

```python
import functools

import jax
import jax.numpy as jnp
from jax import lax
from jax.experimental import pallas as pl
from jax.experimental.pallas import tpu as pltpu
from jax.sharding import PartitionSpec as P

HEADS = 12
HDIM = 64
BF = jnp.bfloat16
F32 = jnp.float32
LOG2E = 1.4426950408889634
BIG = 1e30
BLOCK = 256
FRONT = 512
MESH = pl.DeviceIdType.MESH
PANEL = 768
SPLIT = 3
SLOTS = 2 * SPLIT
LAG = 1.0
STEP = 48
ROWS = 256
VMEM_LIMIT = 62 * 2**20


def to_whole(value, copies):
    if copies > 1:
        value = jnp.repeat(value, copies, axis=0)
    return lax.all_to_all(value, "cols", 0, 1, tiled=True)


def to_parts(value, copies):
    parts = lax.all_to_all(value, "cols", 1, 0, tiled=True)
    return parts[::copies] if copies > 1 else parts


def dot(a, b, dims=((1,), (0,))):
    return lax.dot_general(a, b, (dims, ((), ())), preferred_element_type=F32)


def norm_parts(values):
    average = jnp.mean(values, axis=-1, keepdims=True)
    centered = values - average
    scale = lax.rsqrt(jnp.mean(centered * centered, axis=-1, keepdims=True) + 1e-05)
    return centered * scale, scale


def norm_back(grad, normal, scale, gain):
    weighted = grad * gain
    inner = jnp.mean(weighted * normal, axis=-1, keepdims=True)
    return scale * (weighted - jnp.mean(weighted, axis=-1, keepdims=True) - normal * inner)


def gelu_tanh(values):
    return jax.nn.gelu(values, approximate=True)


NT=((1,),(1,))

def tri(size, upper):
    r=lax.broadcasted_iota(jnp.int32,(size,size),0); c=lax.broadcasted_iota(jnp.int32,(size,size),1)
    return jnp.where(c>r if upper else c<r, 1.0, 0.0).astype(BF)

def split_sum(mask, x):
    hi=x.astype(BF)
    lo=(x-hi.astype(F32)).astype(BF)
    return dot(mask,hi)+dot(mask,lo)

def lane_low(shape):
    return lax.broadcasted_iota(jnp.int32,shape,1) < HDIM

def seg_column(segr_ref, i0):
    shape = (FRONT, FRONT)
    same = lax.broadcasted_iota(jnp.int32, shape, 0) == lax.broadcasted_iota(jnp.int32, shape, 1)
    ids = segr_ref[0:1, i0 : i0 + FRONT].astype(F32)
    return jnp.sum(jnp.where(same, ids, 0.0), axis=1, keepdims=True).astype(jnp.int32)


def attend(q_ref, k_ref, v_ref, seg_ref, o_ref, lse_ref, pen_ref):
    segr_ref, startr_ref = seg_ref.at[0:1], seg_ref.at[1:2]
    L = q_ref.shape[0]
    nb = L // FRONT
    scale = HDIM**-0.5
    upper = tri(FRONT, True)
    carry = jnp.zeros((1, L), F32)
    for b in range(nb - 1, -1, -1):
        i0 = b * FRONT
        n = L - i0
        q0 = q_ref[i0 : i0 + FRONT, 0:128]
        q0 = jnp.where(lane_low(q0.shape), q0, jnp.zeros_like(q0))
        s = dot(q0, k_ref[i0:L, 0:128], NT) * scale
        rows = i0 + lax.broadcasted_iota(jnp.int32, (FRONT, n), 0)
        cols = i0 + lax.broadcasted_iota(jnp.int32, (FRONT, n), 1)
        same = seg_column(segr_ref, i0) == segr_ref[0:1, i0:L]
        picked = same & (cols > rows) & (startr_ref[0:1, i0:L] == 0)
        sel = jnp.where(picked, jnp.maximum(s, 0.0), 0.0)
        if b == nb - 1:
            below = jnp.zeros((1, n), F32)
        else:
            below = jnp.concatenate([jnp.zeros((1, FRONT), F32), carry], axis=1)
        carried = split_sum(upper, sel) + below
        pen_ref[i0 : i0 + FRONT, i0:L] = jnp.where(same & (cols >= rows), carried * (8.0 / L * LOG2E), BIG)
        carry = below + jnp.sum(sel, axis=0, keepdims=True)
    c = scale * LOG2E
    for b in range(nb):
        i0 = b * FRONT
        n = L - i0

        def pair(p, stats, i0=i0, n=n):
            off = pl.multiple_of(p * 128, 128)
            q = q_ref[i0 : i0 + FRONT, pl.ds(off, 128)]
            k = k_ref[i0:L, pl.ds(off, 128)]
            v = v_ref[i0:L, pl.ds(off, 128)]
            low = lane_low(q.shape)
            lowv = lane_low(v.shape)
            lane = lax.broadcasted_iota(jnp.int32, (FRONT, 128), 1)
            outs = []
            for h in range(2):
                mine = low if h == 0 else jnp.logical_not(low)
                s = dot(jnp.where(mine, q, jnp.zeros_like(q)), k, NT) * c - pen_ref[i0 : i0 + FRONT, i0:L]
                m = jnp.max(s, axis=1, keepdims=True)
                e = jnp.exp2(s - m).astype(BF)
                ones = jnp.where(lowv if h == 0 else jnp.logical_not(lowv), v, jnp.ones_like(v))
                o = dot(e, ones)
                total = pltpu.roll(o, HDIM, 1)
                outs.append(o / total)
                stats = jnp.where(lane == 2 * p + h, m + jnp.log2(jnp.where(mine, total, o)), stats)
            o_ref[i0 : i0 + FRONT, pl.ds(off, 128)] = jnp.where(low, outs[0], outs[1]).astype(BF)
            return stats

        lse_ref[i0 : i0 + FRONT, :] = lax.fori_loop(0, HEADS // 2, pair, jnp.zeros((FRONT, 128), F32))


def seg_rows(seg):
    starts = jnp.concatenate([(seg[:-1] != seg[1:]).astype(jnp.int32), jnp.ones((1,), jnp.int32)])
    return jnp.stack([seg, starts])


def attn_fwd(q, k, v, seg):
    L, D = q.shape
    vm = pl.BlockSpec(memory_space=pltpu.VMEM)
    return pl.pallas_call(
        attend,
        out_shape=(
            jax.ShapeDtypeStruct((L, D), BF), jax.ShapeDtypeStruct((L, 128), F32), jax.ShapeDtypeStruct((L, L), F32)),
        in_specs=[vm] * 4,
        out_specs=(vm,) * 3,
        compiler_params=pltpu.CompilerParams(vmem_limit_bytes=VMEM_LIMIT),
        name="attn_fwd",
    )(q, k, v, seg_rows(seg))


def attn_bwd_kernel(q_ref,k_ref,v_ref,g_ref,o_ref,lse_ref,pen_ref,startr_ref,out_ref,qt,gt,dkt,dvt,dsum):
    L,D=q_ref.shape; nb=L//BLOCK
    scale=HDIM**-0.5; c=scale*LOG2E
    pairs=HEADS//2
    lower=tri(BLOCK,False)
    for p in range(pairs):
        qt[p*128:(p+1)*128,:]=q_ref[:,p*128:(p+1)*128].T
        gt[p*128:(p+1)*128,:]=g_ref[:,p*128:(p+1)*128].T
    dkt[...]=jnp.zeros_like(dkt); dvt[...]=jnp.zeros_like(dvt)
    carry=jnp.zeros((1,L),F32)
    for b in range(nb):
        i0=b*BLOCK; n=L-i0
        rowsl=slice(i0,i0+BLOCK)
        carry=carry[:,-n:]
        def head(p,h,i0=i0,n=n,rowsl=rowsl):
            static=isinstance(p,int)
            off=p*128 if static else pl.multiple_of(p*128,128)
            q=q_ref[rowsl,pl.ds(off,128)]; g=g_ref[rowsl,pl.ds(off,128)]; o=o_ref[rowsl,pl.ds(off,128)]
            k=k_ref[i0:L,pl.ds(off,128)]; v=v_ref[i0:L,pl.ds(off,128)]
            low=lane_low(q.shape); mine=low if h==0 else jnp.logical_not(low)
            qm=jnp.where(mine,q,jnp.zeros_like(q)); gm=jnp.where(mine,g,jnp.zeros_like(g))
            lane=lax.broadcasted_iota(jnp.int32,(BLOCK,128),1)
            lse=jnp.sum(jnp.where(lane==2*p+h,lse_ref[rowsl,:],0.0),axis=1,keepdims=True)
            delta=jnp.sum(gm.astype(F32)*o.astype(F32),axis=1,keepdims=True)
            s=dot(qm,k,NT)
            pr=jnp.exp2(s*c-pen_ref[rowsl,i0:L]-lse)
            dp=dot(gm,v,NT)
            ds=pr*(dp-delta)
            return s,pr,ds,off,k
        def finish(p,h,pr,ds,off,k,i0=i0,rowsl=rowsl):
            base=p*128+h*HDIM
            if not isinstance(p,int): base=pl.multiple_of(base,64)
            dsb=ds.astype(BF); prb=pr.astype(BF)
            dvt[pl.ds(base,HDIM),i0:L]+=dot(gt[pl.ds(base,HDIM),rowsl],prb)
            dkt[pl.ds(base,HDIM),i0:L]+=dot(qt[pl.ds(base,HDIM),rowsl],dsb)
            return dot(dsb,k)
        dsum[:,i0:L]=jnp.zeros((BLOCK,n),F32)
        def pair(p,carry_):
            dq=[]
            for h in range(2):
                s,pr,ds,off,k=head(p,h)
                dsum[:,i0:L]+=ds
                dq.append(finish(p,h,pr,ds,off,k))
            out_ref[rowsl,pl.ds(off,128)]=(jnp.where(lane_low(dq[0].shape),dq[0],dq[1])*scale).astype(BF)
            return carry_
        lax.fori_loop(1,pairs,pair,0)
        s,pr,ds,off,k=head(0,1)
        dsum[:,i0:L]+=ds
        dq1=finish(0,1,pr,ds,off,k)
        s,pr,ds,off,k=head(0,0)
        total=dsum[:,i0:L]+ds
        rows=i0+lax.broadcasted_iota(jnp.int32,(BLOCK,n),0)
        cols=i0+lax.broadcasted_iota(jnp.int32,(BLOCK,n),1)
        picked=(pen_ref[rowsl,i0:L]<1e29)&(cols>rows)&(startr_ref[0:1,i0:L]==0)&(s>0)
        gsel=(split_sum(lower,total)+carry)*(-8.0/L)
        carry=carry+jnp.sum(total,axis=0,keepdims=True)
        ds=ds+jnp.where(picked,gsel,0.0)
        dq0=finish(0,0,pr,ds,off,k)
        out_ref[rowsl,0:128]=(jnp.where(lane_low(dq0.shape),dq0,dq1)*scale).astype(BF)
    for p in range(pairs):
        sl=slice(p*128,(p+1)*128)
        out_ref[:,D+p*128:D+(p+1)*128]=(dkt[sl,:]*scale).T.astype(BF)
        out_ref[:,2*D+p*128:2*D+(p+1)*128]=dvt[sl,:].T.astype(BF)

def attn_bwd(q,k,v,g,o,lse,pen,seg):
    L,D=q.shape
    start=jnp.concatenate([(seg[:-1]!=seg[1:]).astype(jnp.int32),jnp.ones((1,),jnp.int32)])
    vm=pl.BlockSpec(memory_space=pltpu.VMEM)
    return pl.pallas_call(attn_bwd_kernel,
        out_shape=jax.ShapeDtypeStruct((L,3*D),BF),
        in_specs=[vm]*8,out_specs=vm,
        scratch_shapes=[pltpu.VMEM((D,L),BF),pltpu.VMEM((D,L),BF),pltpu.VMEM((D,L),F32),pltpu.VMEM((D,L),F32),pltpu.VMEM((BLOCK,L),F32)],
        compiler_params=pltpu.CompilerParams(vmem_limit_bytes=60*2**20),name="attn_bwd")(q,k,v,g,o,lse,pen,start[None,:])


def layer(tokens, segs, cotangent, weights, fused):
    (w_qkv, q_bias, v_bias, w_out, out_bias, attn_gain, attn_shift, mlp_gain, mlp_shift,
     w_up, up_bias, w_down, down_bias) = weights
    width = tokens.shape[-1]
    if fused:
        vectors = (q_bias, v_bias, out_bias, attn_gain, attn_shift, mlp_gain, mlp_shift, down_bias, up_bias)
        tokens, cotangent, queries, keys, values, attended, stats, penalty = front(tokens, cotangent, w_qkv, vectors, segs)
        output, grad_tokens, down, up, side, small = rest(
            attended, tokens, cotangent, queries, keys, values, stats, penalty, vectors, segs, w_qkv, w_out, w_up, w_down)[:6]
        return output, down, up, side, grad_tokens, small
    inputs = tokens.astype(F32)
    normal_one, scale_one = norm_parts(inputs)
    normed = (normal_one * attn_gain + attn_shift).astype(BF)
    projected = dot(normed, w_qkv)
    queries = (projected[:, :width] + q_bias).astype(BF)
    keys = projected[:, width : 2 * width].astype(BF)
    values = (projected[:, 2 * width :] + v_bias).astype(BF)
    attended, stats, penalty = attn_fwd(queries, keys, values, segs)
    residual = inputs + dot(attended, w_out) + out_bias
    normal_two, scale_two = norm_parts(residual)
    normed_two = (normal_two * mlp_gain + mlp_shift).astype(BF)
    upper = dot(normed_two, w_up) + up_bias
    act, gelu_back = jax.vjp(gelu_tanh, upper)
    act = act.astype(BF)
    output = (residual + dot(act, w_down) + down_bias).astype(BF)
    grad_top = cotangent.astype(F32)
    g_down_bias = jnp.sum(grad_top, axis=0)
    g_w_down = dot(act, cotangent, ((0,), (0,)))
    grad_upper = gelu_back(dot(cotangent, w_down, ((1,), (1,))))[0].astype(BF)
    g_up_bias = jnp.sum(grad_upper.astype(F32), axis=0)
    g_w_up = dot(normed_two, grad_upper, ((0,), (0,)))
    grad_two = dot(grad_upper, w_up, ((1,), (1,)))
    g_mlp_gain = jnp.sum(grad_two * normal_two, axis=0)
    g_mlp_shift = jnp.sum(grad_two, axis=0)
    grad_residual = grad_top + norm_back(grad_two, normal_two, scale_two, mlp_gain)
    grad_branch = grad_residual.astype(BF)
    g_out_bias = jnp.sum(grad_branch.astype(F32), axis=0)
    g_w_out = dot(attended, grad_branch, ((0,), (0,)))
    grad_attended = dot(grad_branch, w_out, ((1,), (1,))).astype(BF)
    grad_proj = attn_bwd(queries, keys, values, grad_attended, attended, stats, penalty, segs)
    bias_sums = jnp.sum(grad_proj.astype(F32), axis=0)
    g_q_bias = bias_sums[:width]
    g_v_bias = bias_sums[2 * width :]
    g_w_qkv = dot(normed, grad_proj, ((0,), (0,)))
    grad_one = dot(grad_proj, w_qkv, ((1,), (1,)))
    g_attn_gain = jnp.sum(grad_one * normal_one, axis=0)
    g_attn_shift = jnp.sum(grad_one, axis=0)
    grad_tokens = grad_residual + norm_back(grad_one, normal_one, scale_one, attn_gain)
    return output, grad_tokens, (
        g_w_qkv, g_q_bias, g_v_bias, g_w_out, g_out_bias, g_attn_gain, g_attn_shift,
        g_mlp_gain, g_mlp_shift, g_w_up, g_up_bias, g_w_down, g_down_bias)


def view(ref, tall, panel, row, rows, col, cols):
    if tall:
        return ref.at[pl.ds(pl.multiple_of(panel * PANEL + row, 16), rows), pl.ds(col, cols)]
    return ref.at[pl.ds(pl.multiple_of(row, 16), rows), pl.ds(pl.multiple_of(panel * PANEL + col, 128), cols)]


def add_into(dst, row, rows, parts):
    def turn(i, carry):
        at = pl.multiple_of(i * STEP, 16)
        here = pl.ds(pl.multiple_of(row + at, 16), STEP)
        total = dst[here, :].astype(F32)
        for part in parts:
            total = total + part[pl.ds(at, STEP), :].astype(F32)
        dst[here, :] = total.astype(BF)
        return carry

    lax.fori_loop(0, rows // STEP, turn, 0)


def rows_at(ref, row, rows):
    return ref.at[pl.ds(pl.multiple_of(row, 16), rows), :]


def remote(src, dst, sent, landed, device):
    return pltpu.make_async_remote_copy(
        src_ref=src, dst_ref=dst, send_sem=sent, recv_sem=landed, device_id=device, device_id_type=MESH
    )


class Place:
    def __init__(self):
        self.z, self.col = lax.axis_index("rows"), lax.axis_index("cols")
        z, col = self.z, self.col
        self.y, self.x, self.c = col // 4, (col // 2) % 2, col % 2
        y, x, c = self.y, self.x, self.c
        self.core = (z, y * 4 + x * 2 + (1 - c))
        self.across_x = (z, y * 4 + (1 - x) * 2 + c)
        self.across_y = (z, (1 - y) * 4 + x * 2 + c)
        self.along_z = [(lax.rem(z + d, 4), col) for d in range(1, 4)]
        self.along_cols = [(z, lax.rem(col + d, 8)) for d in range(1, 8)]

    def greet(self, devices):
        barrier = pltpu.get_barrier_semaphore()
        for device in devices:
            pl.semaphore_signal(barrier, inc=1, device_id=device, device_id_type=MESH)
        pl.semaphore_wait(barrier, len(devices))


class Chunk:
    def __init__(self, place, n, source, result, tall, first, buffers, sems):
        own, from_core, from_one, from_two, from_z = [b.at[n % SLOTS] for b in buffers]
        sent, landed, local = sems
        width = own.shape[-1]
        x, y, z, c = place.x, place.y, place.z, place.c
        S = lambda k: sent.at[n, k]
        R = lambda k: landed.at[n, k]
        src = lambda panel, row, rows: view(source, tall, panel, row, rows, first, width)
        out = lambda panel, row, rows: view(result, tall, panel, row, rows, first, width)
        near, far = [x, y], [y, x]
        to_near = [place.across_x, place.across_y]
        to_far = [place.across_y, place.across_x]
        half, quarter, piece = PANEL // 2, PANEL // 4, PANEL // 16
        both = range(2)
        self.own, self.from_core, self.from_one = own, from_core, from_one
        self.from_two, self.from_z = from_two, from_z
        self.half, self.quarter, self.piece = half, quarter, piece
        self.keep1 = [near[u] * half for u in both]
        self.send1 = [(1 - near[u]) * half for u in both]
        self.keep2 = [self.keep1[u] + far[u] * quarter for u in both]
        self.send2 = [self.keep1[u] + (1 - far[u]) * quarter for u in both]
        self.last = [self.keep2[u] + z * piece for u in both]
        final = lambda u: rows_at(own.at[u], self.last[u], piece)
        self.load = [pltpu.make_async_copy(src(2 * c + u, 0, PANEL), own.at[u], local.at[n, u]) for u in both]
        self.core = [remote(src(2 * (1 - c) + u, 0, PANEL), from_core.at[u], S(u), R(u), place.core) for u in both]
        self.one = [remote(rows_at(own.at[u], self.send1[u], half), from_one.at[u], S(2 + u), R(2 + u), to_near[u]) for u in both]
        self.two = [remote(rows_at(own.at[u], self.send2[u], quarter), from_two.at[u], S(4 + u), R(4 + u), to_far[u]) for u in both]
        self.deep = [[remote(rows_at(own.at[u], self.keep2[u] + dev[0] * piece, piece), from_z.at[u, d],
                             S(6 + 3 * u + d), R(6 + 3 * u + d), dev)
                      for d, dev in enumerate(place.along_z)] for u in both]
        self.store = [pltpu.make_async_copy(final(u), out(2 * c + u, self.last[u], piece), local.at[n, 2 + u]) for u in both]
        self.deep_back = [[remote(final(u), out(2 * c + u, self.last[u], piece), S(12 + 3 * u + d), R(12 + 3 * u + d), dev)
                           for d, dev in enumerate(place.along_z)] for u in both]
        same = lambda panel, row, rows, k, dev: remote(out(panel, row, rows), out(panel, row, rows), S(k), R(k), dev)
        self.two_back = [same(2 * c + u, self.keep2[u], quarter, 18 + u, to_far[u]) for u in both]
        self.one_back = [same(2 * c + u, self.keep1[u], half, 20 + u, to_near[u]) for u in both]
        self.core_back = [same(2 * c + u, 0, PANEL, 22 + u, place.core) for u in both]

    def begin(self):
        for copy in self.core + self.load:
            copy.start()

    def step(self, k):
        both = range(2)
        own = [self.own.at[u] for u in both]
        if k == 0:
            for u in both:
                self.load[u].wait()
                self.core[u].wait_recv()
                add_into(own[u], self.send1[u], self.half, [rows_at(self.from_core.at[u], self.send1[u], self.half)])
                self.one[u].start()
            for u in both:
                add_into(own[u], self.keep1[u], self.half, [rows_at(self.from_core.at[u], self.keep1[u], self.half)])
        elif k == 1:
            for u in both:
                self.one[u].wait_recv()
                add_into(own[u], self.send2[u], self.quarter, [rows_at(self.from_one.at[u], self.send2[u] - self.keep1[u], self.quarter)])
                self.two[u].start()
                add_into(own[u], self.keep2[u], self.quarter, [rows_at(self.from_one.at[u], self.keep2[u] - self.keep1[u], self.quarter)])
        elif k == 2:
            for u in both:
                self.two[u].wait_recv()
                add_into(own[u], self.keep2[u], self.quarter, [self.from_two.at[u]])
                for copy in self.deep[u]:
                    copy.start()
        elif k == 3:
            for u in both:
                for copy in self.deep[u]:
                    copy.wait_recv()
                add_into(own[u], self.last[u], self.piece, [self.from_z.at[u, d] for d in range(3)])
                for copy in self.deep_back[u]:
                    copy.start()
                self.store[u].start()
        elif k == 4:
            for u in both:
                for copy in self.deep_back[u]:
                    copy.wait_recv()
                self.store[u].wait()
                self.two_back[u].start()
        elif k == 5:
            for u in both:
                self.two_back[u].wait_recv()
                self.one_back[u].start()
        elif k == 6:
            for u in both:
                self.one_back[u].wait_recv()
                self.core_back[u].start()
        else:
            for u in both:
                self.core_back[u].wait_recv()
            for copy in (self.core + self.one + self.two + self.deep[0] + self.deep[1] + self.deep_back[0]
                         + self.deep_back[1] + self.two_back + self.one_back + self.core_back):
                copy.wait_send()


class Timeline:
    LINK = ["core", "plane", "plane", "deep", "deep", "plane", "plane", "core"]
    TAKES = [t * LAG * 2 / SPLIT for t in (2.5, 6.3, 3.2, 5.8, 5.8, 3.2, 6.3, 2.5)]
    WORK = [t * 2 / SPLIT for t in (2.0, 1.0, 0.5, 0.5, 0.1, 0.1, 0.1, 0.1)]

    def __init__(self):
        self.now = 0.0
        self.free = {"core": 0.0, "plane": 0.0, "deep": 0.0}
        self.moving = {}
        self.after_first = {}

    def occupy(self, link, takes):
        self.free[link] = max(self.free[link], self.now) + takes
        return self.free[link] + 2.0

    def begin(self, chunk, then=None):
        chunk.begin()
        self.moving[chunk] = (self.occupy(self.LINK[0], self.TAKES[0]), 0)
        self.after_first[chunk] = then

    def begin_all(self, chunks):
        self.begin(chunks[0], (lambda: self.begin_all(chunks[1:])) if chunks[1:] else None)

    def turn(self, chunk):
        done, k = self.moving.pop(chunk)
        self.now = max(self.now, done)
        chunk.step(k)
        self.now += self.WORK[k]
        if k < 7:
            self.moving[chunk] = (self.occupy(self.LINK[k + 1], self.TAKES[k + 1]), k + 1)
        if k == 0 and self.after_first[chunk]:
            self.after_first[chunk]()

    def ready(self):
        while self.moving:
            chunk = min(self.moving, key=lambda c: self.moving[c][0])
            if self.moving[chunk][0] > self.now:
                return
            self.turn(chunk)

    def worked(self, takes):
        self.now += takes
        self.ready()

    def complete(self, chunk):
        while chunk in self.moving:
            self.turn(min(self.moving, key=lambda c: self.moving[c][0]))

    def finish(self):
        while self.moving:
            self.turn(min(self.moving, key=lambda c: self.moving[c][0]))


class Homeward:
    def __init__(self, place, source, result, sent, landed, local):
        part = source.shape[0] // 8
        self.copies = [remote(rows_at(source, dev[1] * part, part), result.at[place.col], sent.at[i], landed.at[i], dev)
                       for i, dev in enumerate(place.along_cols)]
        self.own = pltpu.make_async_copy(rows_at(source, place.col * part, part), result.at[place.col], local)

    def start(self):
        for copy in self.copies:
            copy.start()
        self.own.start()

    def wait(self):
        for copy in self.copies:
            copy.wait()
        self.own.wait()


def fill_segments(seg_ref, all_ref, row):
    L = seg_ref.shape[1]
    ids = all_ref[pl.ds(row, 1), :]
    after = pltpu.roll(ids, L - 1, 1)
    lane = lax.broadcasted_iota(jnp.int32, (1, L), 1)
    seg_ref[0:1, :] = ids
    seg_ref[1:2, :] = jnp.where((ids != after) | (lane == L - 1), 1, 0)


def row_reader(refs):
    places = []
    for ref in refs:
        places += [(ref, i) for i in range(ref.shape[0] // PANEL)]

    def read(row):
        ref, i = places[row]
        return ref[i * PANEL : (i + 1) * PANEL].reshape(1, PANEL)

    return read


def front_kernel(tokens_ref, cot_ref, w_ref, seg_all, *refs):
    vectors, refs = refs[:9], refs[9:]
    front_body(row_reader(vectors), tokens_ref, cot_ref, w_ref, seg_all, *refs)


def front_body(vec, tokens_ref, cot_ref, w_ref, seg_all,
                 tokens_out, cot_out, q_ref, k_ref, v_ref, o_ref, lse_ref, pen_ref,
                 whole, w, seg_ref, sent, landed, local):
    L, D = q_ref.shape
    part = L // 8
    place = Place()
    z, y, x, c, col = place.z, place.y, place.x, place.c, place.col

    def other(k):
        flip = lambda bit, coord: 1 - coord if bit else coord
        return (z, flip(k & 4, y) * 4 + flip(k & 2, x) * 2 + flip(k & 1, c))

    place.greet([other(k) for k in range(1, 8)])
    mine = pl.multiple_of(col * part, 16)
    out = [remote(tokens_ref.at[other(k)[1]], rows_at(whole, mine, part), sent.at[0, k], landed.at[0, k], other(k))
           for k in range(1, 8)]
    own = pltpu.make_async_copy(tokens_ref.at[col], rows_at(whole, mine, part), local.at[0])
    load = pltpu.make_async_copy(w_ref, w, local.at[1])
    cots = [remote(cot_ref.at[other(k)[1]], rows_at(cot_out, mine, part), sent.at[1, k], landed.at[1, k], other(k))
            for k in range(1, 8)]
    cot_own = pltpu.make_async_copy(cot_ref.at[col], rows_at(cot_out, mine, part), local.at[2])
    keep = pltpu.make_async_copy(whole, tokens_out, local.at[3])
    own.start()
    fill_segments(seg_ref, seg_all, col)
    for copy in out:
        copy.start()
    load.start()
    cot_own.start()
    own.wait()
    load.wait()
    for chip in range(4):
        for k in (2 * chip, 2 * chip + 1):
            if k:
                out[k - 1].wait_recv()
        if chip == 3:
            for copy in cots:
                copy.start()
        first = other(2 * chip)[1] - c
        here = pl.ds(pl.multiple_of(first * part, 16), 2 * part)
        normal, _ = norm_parts(whole[here, :].astype(F32))
        normed = (normal * vec(ROW_GAIN1) + vec(ROW_SHIFT1)).astype(BF)
        q_ref[here, :] = (dot(normed, w[:, 0:D]) + vec(ROW_Q)).astype(BF)
        k_ref[here, :] = dot(normed, w[:, D : 2 * D]).astype(BF)
        v_ref[here, :] = (dot(normed, w[:, 2 * D : 3 * D]) + vec(ROW_V)).astype(BF)
    keep.start()
    attend(q_ref, k_ref, v_ref, seg_ref, o_ref, lse_ref, pen_ref)
    keep.wait()
    cot_own.wait()
    for copy in out:
        copy.wait_send()
    for copy in cots:
        copy.wait()


def front(tokens, cotangent, w_qkv, vectors, segs):
    cols, part, D = tokens.shape
    L = cols * part
    hbm = pl.BlockSpec(memory_space=pl.ANY)
    vm = pl.BlockSpec(memory_space=pltpu.VMEM)
    dma = pltpu.SemaphoreType.DMA
    rows = jax.ShapeDtypeStruct((L, D), BF)
    return pl.pallas_call(
        front_kernel,
        out_shape=(rows,) * 6 + (jax.ShapeDtypeStruct((L, 128), F32), jax.ShapeDtypeStruct((L, L), F32)),
        in_specs=[hbm] * 3 + [vm] * 10,
        out_specs=(hbm,) * 2 + (vm,) * 6,
        scratch_shapes=[pltpu.VMEM((L, D), BF), pltpu.VMEM((D, 3 * D), BF), pltpu.VMEM((2, L), jnp.int32), dma((2, 8)), dma((2, 8)), dma((4,))],
        compiler_params=pltpu.CompilerParams(vmem_limit_bytes=VMEM_LIMIT, collective_id=2, has_side_effects=True),
        name="front",
    )(tokens, cotangent, w_qkv, segs, *vectors)


ROW_Q, ROW_V, ROW_OUT, ROW_GAIN1, ROW_SHIFT1, ROW_GAIN2, ROW_SHIFT2, ROW_DOWN, ROW_UP = range(9)


def gelu_pair(u):
    slope = 0.7978845608028654
    square = u * u
    t = jnp.tanh(slope * u * (1.0 + 0.044715 * square))
    half = 0.5 * (1.0 + t)
    return u * half, half + (0.5 * slope) * u * (1.0 - t * t) * (1.0 + 3 * 0.044715 * square)


def rest_kernel(*refs):
    rest_body(row_reader(refs[:9]), *refs[9:])


def rest_body(vec, att_hbm, tok_hbm, cot_hbm, q_hbm, k_hbm, v_hbm, lse_hbm, pen_hbm, seg_all,
                w_qkv_hbm, w_out_hbm, w_up_hbm, w_down_hbm,
                output_out, tokens_out, down_out, up_out, side_out, small_out, down_part, up_part, out_part, res_part,
                seg_ref, tok, g, delta, sm_acc, sm_rec, own, from_core, from_one, from_two, from_z,
                sent, landed, local, home_s, home_r, home_l, sm_s, sm_r, in_s, stage_s, res_s, pen_s):
    L, D = tok.shape
    ff = w_up_hbm.shape[1]
    nb = L // BLOCK
    width = PANEL // SPLIT
    pairs = HEADS // 2
    place = Place()
    place.greet(place.along_cols + place.along_z)
    buffers, sems = (own, from_core, from_one, from_two, from_z), (sent, landed, local)
    chunks = []
    for source, result, tall in ((down_part, down_out, True), (up_part, up_out, False)):
        for j in range(SPLIT):
            chunks.append(Chunk(place, len(chunks), source, result, tall, j * width, buffers, sems))
    line = Timeline()
    fill_segments(seg_ref, seg_all, place.col)
    sm_acc[0] = jnp.zeros_like(sm_acc[0])

    def add_row(row, values):
        sm_acc[0, row : row + 1, :] += jnp.sum(values, axis=0, keepdims=True)

    def feed_forward(w_out, w_up, w_down, act, gu, n2t, gb, out, att, cot, res, stage):
        loads = [pltpu.make_async_copy(a, b, in_s.at[i]) for i, (a, b) in enumerate((
            (att_hbm, att), (tok_hbm, tok), (w_out_hbm, w_out), (cot_hbm, cot), (w_up_hbm, w_up), (w_down_hbm, w_down)))]
        for copy in loads:
            copy.start()
        features = lax.broadcasted_iota(jnp.int32, (D, 128), 0) // HDIM
        member = jnp.where(features == lax.broadcasted_iota(jnp.int32, (D, 128), 1), 1.0, 0.0).astype(BF)
        for copy in loads:
            copy.wait()

        def forward(b, carry):
            here = pl.ds(pl.multiple_of(b * ROWS, ROWS), ROWS)
            dy = cot[here, :]
            residual = tok[here, :].astype(F32) + dot(att[here, :], w_out[...]) + vec(ROW_OUT)
            res[here, :] = residual
            normal, _ = norm_parts(residual)
            n2 = (normal * vec(ROW_GAIN2) + vec(ROW_SHIFT2)).astype(BF)
            n2t[:, here] = n2.T
            add_row(ROW_DOWN, dy.astype(F32))
            total = residual + vec(ROW_DOWN)
            for j in range(ff // D):
                part = slice(j * D, (j + 1) * D)
                value, slope = gelu_pair(dot(n2, w_up[:, part]) + vec(ROW_UP + j))
                low = value.astype(BF)
                act[here, part] = low
                gu[here, part] = slope.astype(BF)
                total = total + dot(low, w_down[part, :])
            out[here, :] = total.astype(BF)
            return carry

        def backward(b):
            here = slice(b * ROWS, (b + 1) * ROWS)
            dy = cot[here, :]
            normal, spread = norm_parts(res[here, :])
            grad_two = jnp.zeros((ROWS, D), F32)
            for j in range(ff // D):
                part = slice(j * D, (j + 1) * D)
                grad = (dot(dy, w_down[part, :], NT) * gu[here, part].astype(F32)).astype(BF)
                gu[here, part] = grad
                add_row(ROW_UP + j, grad.astype(F32))
                grad_two = grad_two + dot(grad, w_up[:, part], NT)
            add_row(ROW_GAIN2, grad_two * normal)
            add_row(ROW_SHIFT2, grad_two)
            grad_residual = dy.astype(F32) + norm_back(grad_two, normal, spread, vec(ROW_GAIN2))
            res[here, :] = grad_residual
            branch = grad_residual.astype(BF)
            gb[here, :] = branch
            add_row(ROW_OUT, branch.astype(F32))
            grad_att = dot(branch, w_out[...], NT).astype(BF)
            g[here, :] = grad_att
            product = grad_att.astype(F32) * att[here, :].astype(F32)
            high = product.astype(BF)
            delta[here, :] = dot(high, member) + dot((product - high.astype(F32)).astype(BF), member)

        lax.fori_loop(0, L // ROWS, forward, 0)
        home = Homeward(place, out, output_out, home_s.at[0], home_r.at[0], home_l.at[0])
        home.start()
        line.occupy("plane", 16.0)
        tiles = ff // 256
        stored = [pltpu.make_async_copy(stage.at[i % 2], down_part.at[i * 256 : (i + 1) * 256, :], stage_s.at[i % 2])
                  for i in range(tiles)]
        for i in range(tiles):
            if i > 1:
                stored[i - 2].wait()
            stage[i % 2] = dot(act[:, i * 256 : (i + 1) * 256], cot[...], ((0,), (0,))).astype(BF)
            stored[i].start()
        stored[tiles - 2].wait()
        stored[tiles - 1].wait()
        line.worked(6.0)
        line.begin_all(chunks[:SPLIT])
        for b in range(L // ROWS):
            backward(b)
            line.worked(4.3)
        tiles = ff // D
        spread = [pltpu.make_async_copy(w_down.at[i * D : (i + 1) * D, :], up_part.at[:, i * D : (i + 1) * D], stage_s.at[2 + i])
                  for i in range(tiles)]
        for i in range(tiles):
            for j in range(D // 256):
                w_down[i * D : (i + 1) * D, j * 256 : (j + 1) * 256] = dot(n2t[...], gu[:, i * D + j * 256 : i * D + (j + 1) * 256]).astype(BF)
            spread[i].start()
            line.worked(1.6)
        w_out[...] = dot(att[...], gb[...], ((0,), (0,))).astype(BF)
        keep = [pltpu.make_async_copy(w_out, out_part, res_s.at[0]), pltpu.make_async_copy(res, res_part, res_s.at[1])]
        for copy in keep:
            copy.start()
        for copy in spread:
            copy.wait()
        line.worked(1.5)
        line.begin_all(chunks[SPLIT:])
        for copy in keep:
            copy.wait()
        home.wait()

    dma = pltpu.SemaphoreType.DMA
    pl.run_scoped(
        feed_forward, pltpu.VMEM((D, D), BF), pltpu.VMEM((D, ff), BF), pltpu.VMEM((ff, D), BF), pltpu.VMEM((L, ff), BF),
        pltpu.VMEM((L, ff), BF), pltpu.VMEM((D, L), BF), pltpu.VMEM((L, D), BF),
        pltpu.VMEM((L, D), BF), pltpu.VMEM((L, D), BF), pltpu.VMEM((L, D), BF), pltpu.VMEM((L, D), F32),
        pltpu.VMEM((2, 256, D), BF))

    def attention(q_ref, k_ref, v_ref, lse_ref, w_ref, qt, gt, dkt, dvt, dsum, pen, dqkv, side, gtok, gres):
        scale = HDIM**-0.5
        c = scale * LOG2E
        startr_ref = seg_ref.at[1:2]
        loads = [pltpu.make_async_copy(a, b, in_s.at[i]) for i, (a, b) in enumerate((
            (q_hbm, q_ref), (k_hbm, k_ref), (v_hbm, v_ref), (lse_hbm, lse_ref), (w_qkv_hbm, w_ref)))]
        pen_copies = [pltpu.make_async_copy(pen_hbm.at[b * BLOCK : (b + 1) * BLOCK, :], pen.at[b % 2], pen_s.at[b % 2])
                      for b in range(nb)]
        res_copies = [pltpu.make_async_copy(res_part.at[b * BLOCK : (b + 1) * BLOCK, :], gres.at[b % 2], res_s.at[b % 2])
                      for b in range(nb)]
        for copy in loads[:4]:
            copy.start()
        pen_copies[0].start()
        loads[4].start()
        out_copy = pltpu.make_async_copy(out_part, side.at[:, 3 * D : 4 * D], in_s.at[5])
        out_copy.start()
        dkt[...] = jnp.zeros_like(dkt)
        dvt[...] = jnp.zeros_like(dvt)
        for p in range(pairs):
            gt[p * 128 : (p + 1) * 128, :] = g[:, p * 128 : (p + 1) * 128].T
        for copy in loads[:4]:
            copy.wait()
        for p in range(pairs):
            qt[p * 128 : (p + 1) * 128, :] = q_ref[:, p * 128 : (p + 1) * 128].T
        line.worked(3.0)
        lower = tri(BLOCK, False)
        carry = jnp.zeros((1, L), F32)
        for b in range(nb):
            i0 = b * BLOCK
            n = L - i0
            rowsl = slice(i0, i0 + BLOCK)
            carry = carry[:, -n:]
            pen_copies[b].wait()
            if b + 1 < nb:
                pen_copies[b + 1].start()
            pen_b = pen.at[b % 2, :, i0:L]

            def head(p, h):
                off = p * 128 if isinstance(p, int) else pl.multiple_of(p * 128, 128)
                q = q_ref[rowsl, pl.ds(off, 128)]
                gh = g[rowsl, pl.ds(off, 128)]
                k = k_ref[i0:L, pl.ds(off, 128)]
                v = v_ref[i0:L, pl.ds(off, 128)]
                low = lane_low(q.shape)
                mine = low if h == 0 else jnp.logical_not(low)
                lane = lax.broadcasted_iota(jnp.int32, (BLOCK, 128), 1)
                lse = jnp.sum(jnp.where(lane == 2 * p + h, lse_ref[rowsl, :], 0.0), axis=1, keepdims=True)
                shift = jnp.sum(jnp.where(lane == 2 * p + h, delta[rowsl, :], 0.0), axis=1, keepdims=True)
                s = dot(jnp.where(mine, q, jnp.zeros_like(q)), k, NT)
                pr = jnp.exp2(s * c - pen_b[...] - lse)
                dp = dot(jnp.where(mine, gh, jnp.zeros_like(gh)), v, NT)
                return s, pr, pr * (dp - shift), off, k

            def finish(p, h, pr, ds, k):
                base = p * 128 + h * HDIM
                if not isinstance(p, int):
                    base = pl.multiple_of(base, 64)
                dsb = ds.astype(BF)
                dvt[pl.ds(base, HDIM), i0:L] += dot(gt[pl.ds(base, HDIM), rowsl], pr.astype(BF))
                dkt[pl.ds(base, HDIM), i0:L] += dot(qt[pl.ds(base, HDIM), rowsl], dsb)
                return dot(dsb, k)

            def pair(p, carry_):
                dq = []
                for h in range(2):
                    s, pr, ds, off, k = head(p, h)
                    dsum[:, i0:L] += ds
                    dq.append(finish(p, h, pr, ds, k))
                dqkv[rowsl, pl.ds(off, 128)] = (jnp.where(lane_low(dq[0].shape), dq[0], dq[1]) * scale).astype(BF)
                return carry_

            dsum[:, i0:L] = jnp.zeros((BLOCK, n), F32)
            each = 0.42 * (BLOCK // 256) * (n // 256)
            for begin, end in ((1, 3), (3, pairs)) if b < 2 else ((1, pairs),):
                lax.fori_loop(begin, end, pair, 0)
                line.worked(each * (end - begin))
            s, pr, ds, off, k = head(0, 1)
            dsum[:, i0:L] += ds
            dq1 = finish(0, 1, pr, ds, k)
            s, pr, ds, off, k = head(0, 0)
            total = dsum[:, i0:L] + ds
            rows = i0 + lax.broadcasted_iota(jnp.int32, (BLOCK, n), 0)
            cols = i0 + lax.broadcasted_iota(jnp.int32, (BLOCK, n), 1)
            picked = (pen_b[...] < 1e29) & (cols > rows) & (startr_ref[0:1, i0:L] == 0) & (s > 0)
            gsel = (split_sum(lower, total) + carry) * (-8.0 / L)
            carry = carry + jnp.sum(total, axis=0, keepdims=True)
            ds = ds + jnp.where(picked, gsel, 0.0)
            dq0 = finish(0, 0, pr, ds, k)
            dqkv[rowsl, 0:128] = (jnp.where(lane_low(dq0.shape), dq0, dq1) * scale).astype(BF)
            line.worked(each * 1.2)
        for p in range(pairs):
            sl = slice(p * 128, (p + 1) * 128)
            dqkv[:, D + p * 128 : D + (p + 1) * 128] = (dkt[sl, :] * scale).T.astype(BF)
            dqkv[:, 2 * D + p * 128 : 2 * D + (p + 1) * 128] = dvt[sl, :].T.astype(BF)

        def normal_of(b):
            return norm_parts(tok[b * BLOCK : (b + 1) * BLOCK, :].astype(F32))

        for b in range(nb):
            normal, _ = normal_of(b)
            normed = (normal * vec(ROW_GAIN1) + vec(ROW_SHIFT1)).astype(BF)
            for p in range(pairs):
                qt[p * 128 : (p + 1) * 128, b * BLOCK : (b + 1) * BLOCK] = normed[:, p * 128 : (p + 1) * 128].T
        line.worked(3.0)
        out_copy.wait()
        for j in range(SPLIT):
            for panel in range(3):
                at = slice(panel * D + j * width, panel * D + (j + 1) * width)
                side[:, at] = dot(qt[...], dqkv[:, at]).astype(BF)
            line.now += 5.0 / SPLIT
            line.complete(chunks[j])
            line.begin(Chunk(place, 2 * SPLIT + j, side, side_out, False, j * width, buffers, sems))
            line.ready()
        sm_acc[0, 0:1, :] = jnp.sum(dqkv[:, 0:D].astype(F32), axis=0, keepdims=True)
        sm_acc[0, 1:2, :] = jnp.sum(dqkv[:, 2 * D : 3 * D].astype(F32), axis=0, keepdims=True)
        res_copies[0].start()
        loads[4].wait()
        g_gain = jnp.zeros((1, D), F32)
        g_shift = jnp.zeros((1, D), F32)
        for b in range(nb):
            rowsl = slice(b * BLOCK, (b + 1) * BLOCK)
            if b + 1 < nb:
                res_copies[b + 1].start()
            normal, spread = normal_of(b)
            grad = dot(dqkv[rowsl, :], w_ref[...], NT)
            g_gain = g_gain + jnp.sum(grad * normal, axis=0, keepdims=True)
            g_shift = g_shift + jnp.sum(grad, axis=0, keepdims=True)
            back = norm_back(grad, normal, spread, vec(ROW_GAIN1))
            res_copies[b].wait()
            gtok[rowsl, :] = (gres[b % 2] + back).astype(BF)
            line.worked(2.0)
        tokens_home = Homeward(place, gtok, tokens_out, home_s.at[1], home_r.at[1], home_l.at[1])
        tokens_home.start()
        line.occupy("plane", 16.0)
        sm_acc[0, 3:4, :] = g_gain
        sm_acc[0, 4:5, :] = g_shift
        z, col = place.z, place.col
        friends = [place.core, place.across_x, place.across_y, (z + 1 - 2 * (z % 2), col), (lax.rem(z + 2, 4), col)]
        smalls = [remote(sm_acc.at[i], sm_rec.at[i], sm_s.at[i], sm_r.at[i], friends[i]) for i in range(5)]
        smalls[0].start()
        for i in range(5):
            line.worked(4.0)
            smalls[i].wait_recv()
            following = sm_acc[i] + sm_rec[i]
            if i < 4:
                sm_acc[i + 1] = following
                smalls[i + 1].start()
            else:
                small_out[...] = following
        line.finish()
        for copy in smalls:
            copy.wait_send()
        tokens_home.wait()

    pl.run_scoped(
        attention, pltpu.VMEM((L, D), BF), pltpu.VMEM((L, D), BF), pltpu.VMEM((L, D), BF), pltpu.VMEM((L, 128), F32),
        pltpu.VMEM((D, 3 * D), BF), pltpu.VMEM((D, L), BF), pltpu.VMEM((D, L), BF), pltpu.VMEM((D, L), F32),
        pltpu.VMEM((D, L), F32), pltpu.VMEM((BLOCK, L), F32), pltpu.VMEM((2, BLOCK, L), F32), pltpu.VMEM((L, 3 * D), BF),
        pltpu.VMEM((D, 4 * D), BF), pltpu.VMEM((L, D), BF), pltpu.VMEM((2, BLOCK, D), F32))


def rest(attended, tokens, cotangent, q, k, v, lse, pen, vectors, segs, w_qkv, w_out, w_up, w_down):
    L, D = attended.shape
    ff = w_up.shape[1]
    N, W = 3 * SPLIT, PANEL // SPLIT
    hbm = pl.BlockSpec(memory_space=pl.ANY)
    vm = pl.BlockSpec(memory_space=pltpu.VMEM)
    dma = pltpu.SemaphoreType.DMA
    shape = jax.ShapeDtypeStruct
    rows = shape((8, L // 8, D), BF)
    wide, tall = shape((D, ff), BF), shape((ff, D), BF)
    return pl.pallas_call(
        rest_kernel,
        out_shape=(rows, rows, tall, wide, wide, shape((16, D), F32), tall, wide, shape((D, D), BF), shape((L, D), F32)),
        in_specs=[vm] * 9 + [hbm] * 8 + [vm] + [hbm] * 4,
        out_specs=(hbm,) * 5 + (vm,) + (hbm,) * 4,
        scratch_shapes=[
            pltpu.VMEM((2, L), jnp.int32), pltpu.VMEM((L, D), BF), pltpu.VMEM((L, D), BF), pltpu.VMEM((L, 128), F32), pltpu.VMEM((5, 16, D), F32),
            pltpu.VMEM((5, 16, D), F32), pltpu.VMEM((SLOTS, 2, PANEL, W), BF), pltpu.VMEM((SLOTS, 2, PANEL, W), BF),
            pltpu.VMEM((SLOTS, 2, PANEL // 2, W), BF), pltpu.VMEM((SLOTS, 2, PANEL // 4, W), BF),
            pltpu.VMEM((SLOTS, 2, 3, PANEL // 16, W), BF),
            dma((N, 24)), dma((N, 24)), dma((N, 4)), dma((2, 7)), dma((2, 7)), dma((2,)), dma((5,)), dma((5,)),
            dma((6,)), dma((6,)), dma((2,)), dma((2,)),
        ],
        compiler_params=pltpu.CompilerParams(vmem_limit_bytes=VMEM_LIMIT, collective_id=1, has_side_effects=True),
        name="rest",
    )(*vectors, attended, tokens, cotangent, q, k, v, lse, pen, segs, w_qkv, w_out, w_up, w_down)


def widen_kernel(tok_in, down_in, up_in, side_in, tok_out, down_out, up_out, qkv_out, out_out):
    tok_out[...] = tok_in[...].astype(F32)
    down_out[...] = down_in[...].astype(F32)
    up_out[...] = up_in[...].astype(F32)
    split = qkv_out.shape[1]
    qkv_out[...] = side_in[:, :split].astype(F32)
    out_out[...] = side_in[:, split:].astype(F32)


def widen(tok, down, up, side):
    parts, part, D = tok.shape
    steps = 2 * parts
    block = lambda a: pl.BlockSpec((a[0] // steps, a[1]), lambda i: (i, 0))
    tok_spec = pl.BlockSpec((1, part // 2, D), lambda i: (i // 2, i % 2, 0))
    shapes = [down.shape, up.shape, (D, 3 * D), (D, D)]
    return pl.pallas_call(
        widen_kernel,
        grid=(steps,),
        out_shape=[jax.ShapeDtypeStruct(a, F32) for a in [tok.shape] + shapes],
        in_specs=[tok_spec, block(down.shape), block(up.shape), block(side.shape)],
        out_specs=[tok_spec] + [block(a) for a in shapes],
        compiler_params=pltpu.CompilerParams(vmem_limit_bytes=VMEM_LIMIT),
        name="widen",
    )(tok, down, up, side)


def summed_grads(grads, copies):
    grads = [g / copies for g in grads]
    matrices = [i for i, g in enumerate(grads) if g.ndim == 2]
    vectors = [i for i, g in enumerate(grads) if g.ndim == 1]
    big = lax.psum([grads[i].astype(BF) for i in matrices], ("rows", "cols"))
    small = lax.psum(jnp.concatenate([grads[i] for i in vectors]), ("rows", "cols"))
    out = [None] * len(grads)
    for i, g in zip(matrices, big):
        out[i] = g.astype(F32)
    at = 0
    for i in vectors:
        out[i] = small[at : at + grads[i].shape[0]]
        at += grads[i].shape[0]
    return out


def per_device(tokens, segment_ids, cotangent, *weights):
    seqs, part, width = tokens.shape
    cols = lax.axis_size("cols")
    fitting = (lax.axis_size("rows"), cols, seqs) == (4, 8, 8)
    copies = max(1, cols // seqs)
    held = max(1, seqs // cols)
    first = (lax.axis_index("cols") // copies) * held
    segs = lax.dynamic_slice_in_dim(segment_ids, first, held, 0)
    if fitting:
        output, down, up, side, grad_tokens, small = layer(tokens, segment_ids, cotangent, weights, True)
        grad_tokens, g_w_down, g_w_up, g_w_qkv, g_w_out = widen(grad_tokens, down, up, side)
        return (
            output, grad_tokens, g_w_qkv, small[ROW_Q], small[ROW_V], g_w_out, small[ROW_OUT], small[ROW_GAIN1],
            small[ROW_SHIFT1], small[ROW_GAIN2], small[ROW_SHIFT2], g_w_up, small[ROW_UP:12].reshape(-1), g_w_down,
            small[ROW_DOWN])
    tokens_whole = to_whole(tokens, copies)
    cotangent_whole = to_whole(cotangent, copies)
    results = [
        layer(tokens_whole[s], segs[s], cotangent_whole[s], weights, False) for s in range(held)
    ]
    output = jnp.stack([r[0] for r in results])
    grad_tokens = jnp.stack([r[1] for r in results])
    grads = [sum(parts[1:], parts[0]) for parts in zip(*[r[2] for r in results])]
    return (
        to_parts(output, copies),
        to_parts(grad_tokens.astype(BF), copies).astype(F32),
        *summed_grads(grads, copies),
    )


def solution(mesh):
    placed = (P("rows", "cols", None), P("rows", None), P("rows", "cols", None)) + (P(),) * 13
    return jax.shard_map(
        per_device,
        mesh=mesh,
        in_specs=placed,
        out_specs=(P("rows", "cols", None), P("rows", "cols", None)) + (P(),) * 13,
        check_vma=False,
    )
```

```python
import functools

import jax
import jax.numpy as jnp
from jax import lax
from jax.experimental import pallas as pl
from jax.experimental.pallas import tpu as pltpu
from jax.sharding import PartitionSpec as P

HEADS = 12
HDIM = 64
BF = jnp.bfloat16
F32 = jnp.float32
LOG2E = 1.4426950408889634
BIG = 1e30
BLOCK = 256
FRONT = 512
MESH = pl.DeviceIdType.MESH
PANEL = 768
SPLIT = 3
SLOTS = 2 * SPLIT
LAG = 1.0
STEP = 48
ROWS = 256
VMEM_LIMIT = 62 * 2**20


def to_whole(value, copies):
    if copies > 1:
        value = jnp.repeat(value, copies, axis=0)
    return lax.all_to_all(value, "cols", 0, 1, tiled=True)


def to_parts(value, copies):
    parts = lax.all_to_all(value, "cols", 1, 0, tiled=True)
    return parts[::copies] if copies > 1 else parts


def dot(a, b, dims=((1,), (0,))):
    return lax.dot_general(a, b, (dims, ((), ())), preferred_element_type=F32)


def norm_parts(values):
    average = jnp.mean(values, axis=-1, keepdims=True)
    centered = values - average
    scale = lax.rsqrt(jnp.mean(centered * centered, axis=-1, keepdims=True) + 1e-05)
    return centered * scale, scale


def norm_back(grad, normal, scale, gain):
    weighted = grad * gain
    inner = jnp.mean(weighted * normal, axis=-1, keepdims=True)
    return scale * (weighted - jnp.mean(weighted, axis=-1, keepdims=True) - normal * inner)


def gelu_tanh(values):
    return jax.nn.gelu(values, approximate=True)


NT=((1,),(1,))

def tri(size, upper):
    r=lax.broadcasted_iota(jnp.int32,(size,size),0); c=lax.broadcasted_iota(jnp.int32,(size,size),1)
    return jnp.where(c>r if upper else c<r, 1.0, 0.0).astype(BF)

def split_sum(mask, x):
    hi=x.astype(BF)
    lo=(x-hi.astype(F32)).astype(BF)
    return dot(mask,hi)+dot(mask,lo)

def lane_low(shape):
    return lax.broadcasted_iota(jnp.int32,shape,1) < HDIM

def seg_column(segr_ref, i0):
    shape = (FRONT, FRONT)
    same = lax.broadcasted_iota(jnp.int32, shape, 0) == lax.broadcasted_iota(jnp.int32, shape, 1)
    ids = segr_ref[0:1, i0 : i0 + FRONT].astype(F32)
    return jnp.sum(jnp.where(same, ids, 0.0), axis=1, keepdims=True).astype(jnp.int32)


def attend(q_ref, k_ref, v_ref, seg_ref, o_ref, lse_ref, pen_ref):
    segr_ref, startr_ref = seg_ref.at[0:1], seg_ref.at[1:2]
    L = q_ref.shape[0]
    nb = L // FRONT
    scale = HDIM**-0.5
    upper = tri(FRONT, True)
    carry = jnp.zeros((1, L), F32)
    for b in range(nb - 1, -1, -1):
        i0 = b * FRONT
        n = L - i0
        q0 = q_ref[i0 : i0 + FRONT, 0:128]
        q0 = jnp.where(lane_low(q0.shape), q0, jnp.zeros_like(q0))
        s = dot(q0, k_ref[i0:L, 0:128], NT) * scale
        rows = i0 + lax.broadcasted_iota(jnp.int32, (FRONT, n), 0)
        cols = i0 + lax.broadcasted_iota(jnp.int32, (FRONT, n), 1)
        same = seg_column(segr_ref, i0) == segr_ref[0:1, i0:L]
        picked = same & (cols > rows) & (startr_ref[0:1, i0:L] == 0)
        sel = jnp.where(picked, jnp.maximum(s, 0.0), 0.0)
        if b == nb - 1:
            below = jnp.zeros((1, n), F32)
        else:
            below = jnp.concatenate([jnp.zeros((1, FRONT), F32), carry], axis=1)
        carried = split_sum(upper, sel) + below
        pen_ref[i0 : i0 + FRONT, i0:L] = jnp.where(same & (cols >= rows), carried * (8.0 / L * LOG2E), BIG)
        carry = below + jnp.sum(sel, axis=0, keepdims=True)
    c = scale * LOG2E
    for b in range(nb):
        i0 = b * FRONT
        n = L - i0

        def pair(p, stats, i0=i0, n=n):
            off = pl.multiple_of(p * 128, 128)
            q = q_ref[i0 : i0 + FRONT, pl.ds(off, 128)]
            k = k_ref[i0:L, pl.ds(off, 128)]
            v = v_ref[i0:L, pl.ds(off, 128)]
            low = lane_low(q.shape)
            lowv = lane_low(v.shape)
            lane = lax.broadcasted_iota(jnp.int32, (FRONT, 128), 1)
            outs = []
            for h in range(2):
                mine = low if h == 0 else jnp.logical_not(low)
                s = dot(jnp.where(mine, q, jnp.zeros_like(q)), k, NT) * c - pen_ref[i0 : i0 + FRONT, i0:L]
                m = jnp.max(s, axis=1, keepdims=True)
                e = jnp.exp2(s - m).astype(BF)
                ones = jnp.where(lowv if h == 0 else jnp.logical_not(lowv), v, jnp.ones_like(v))
                o = dot(e, ones)
                total = pltpu.roll(o, HDIM, 1)
                outs.append(o / total)
                stats = jnp.where(lane == 2 * p + h, m + jnp.log2(jnp.where(mine, total, o)), stats)
            o_ref[i0 : i0 + FRONT, pl.ds(off, 128)] = jnp.where(low, outs[0], outs[1]).astype(BF)
            return stats

        lse_ref[i0 : i0 + FRONT, :] = lax.fori_loop(0, HEADS // 2, pair, jnp.zeros((FRONT, 128), F32))


def seg_rows(seg):
    starts = jnp.concatenate([(seg[:-1] != seg[1:]).astype(jnp.int32), jnp.ones((1,), jnp.int32)])
    return jnp.stack([seg, starts])


def attn_fwd(q, k, v, seg):
    L, D = q.shape
    vm = pl.BlockSpec(memory_space=pltpu.VMEM)
    return pl.pallas_call(
        attend,
        out_shape=(
            jax.ShapeDtypeStruct((L, D), BF), jax.ShapeDtypeStruct((L, 128), F32), jax.ShapeDtypeStruct((L, L), F32)),
        in_specs=[vm] * 4,
        out_specs=(vm,) * 3,
        compiler_params=pltpu.CompilerParams(vmem_limit_bytes=VMEM_LIMIT),
        name="attn_fwd",
    )(q, k, v, seg_rows(seg))


def attn_bwd_kernel(q_ref,k_ref,v_ref,g_ref,o_ref,lse_ref,pen_ref,startr_ref,out_ref,qt,gt,dkt,dvt,dsum):
    L,D=q_ref.shape; nb=L//BLOCK
    scale=HDIM**-0.5; c=scale*LOG2E
    pairs=HEADS//2
    lower=tri(BLOCK,False)
    for p in range(pairs):
        qt[p*128:(p+1)*128,:]=q_ref[:,p*128:(p+1)*128].T
        gt[p*128:(p+1)*128,:]=g_ref[:,p*128:(p+1)*128].T
    dkt[...]=jnp.zeros_like(dkt); dvt[...]=jnp.zeros_like(dvt)
    carry=jnp.zeros((1,L),F32)
    for b in range(nb):
        i0=b*BLOCK; n=L-i0
        rowsl=slice(i0,i0+BLOCK)
        carry=carry[:,-n:]
        def head(p,h,i0=i0,n=n,rowsl=rowsl):
            static=isinstance(p,int)
            off=p*128 if static else pl.multiple_of(p*128,128)
            q=q_ref[rowsl,pl.ds(off,128)]; g=g_ref[rowsl,pl.ds(off,128)]; o=o_ref[rowsl,pl.ds(off,128)]
            k=k_ref[i0:L,pl.ds(off,128)]; v=v_ref[i0:L,pl.ds(off,128)]
            low=lane_low(q.shape); mine=low if h==0 else jnp.logical_not(low)
            qm=jnp.where(mine,q,jnp.zeros_like(q)); gm=jnp.where(mine,g,jnp.zeros_like(g))
            lane=lax.broadcasted_iota(jnp.int32,(BLOCK,128),1)
            lse=jnp.sum(jnp.where(lane==2*p+h,lse_ref[rowsl,:],0.0),axis=1,keepdims=True)
            delta=jnp.sum(gm.astype(F32)*o.astype(F32),axis=1,keepdims=True)
            s=dot(qm,k,NT)
            pr=jnp.exp2(s*c-pen_ref[rowsl,i0:L]-lse)
            dp=dot(gm,v,NT)
            ds=pr*(dp-delta)
            return s,pr,ds,off,k
        def finish(p,h,pr,ds,off,k,i0=i0,rowsl=rowsl):
            base=p*128+h*HDIM
            if not isinstance(p,int): base=pl.multiple_of(base,64)
            dsb=ds.astype(BF); prb=pr.astype(BF)
            dvt[pl.ds(base,HDIM),i0:L]+=dot(gt[pl.ds(base,HDIM),rowsl],prb)
            dkt[pl.ds(base,HDIM),i0:L]+=dot(qt[pl.ds(base,HDIM),rowsl],dsb)
            return dot(dsb,k)
        dsum[:,i0:L]=jnp.zeros((BLOCK,n),F32)
        def pair(p,carry_):
            dq=[]
            for h in range(2):
                s,pr,ds,off,k=head(p,h)
                dsum[:,i0:L]+=ds
                dq.append(finish(p,h,pr,ds,off,k))
            out_ref[rowsl,pl.ds(off,128)]=(jnp.where(lane_low(dq[0].shape),dq[0],dq[1])*scale).astype(BF)
            return carry_
        lax.fori_loop(1,pairs,pair,0)
        s,pr,ds,off,k=head(0,1)
        dsum[:,i0:L]+=ds
        dq1=finish(0,1,pr,ds,off,k)
        s,pr,ds,off,k=head(0,0)
        total=dsum[:,i0:L]+ds
        rows=i0+lax.broadcasted_iota(jnp.int32,(BLOCK,n),0)
        cols=i0+lax.broadcasted_iota(jnp.int32,(BLOCK,n),1)
        picked=(pen_ref[rowsl,i0:L]<1e29)&(cols>rows)&(startr_ref[0:1,i0:L]==0)&(s>0)
        gsel=(split_sum(lower,total)+carry)*(-8.0/L)
        carry=carry+jnp.sum(total,axis=0,keepdims=True)
        ds=ds+jnp.where(picked,gsel,0.0)
        dq0=finish(0,0,pr,ds,off,k)
        out_ref[rowsl,0:128]=(jnp.where(lane_low(dq0.shape),dq0,dq1)*scale).astype(BF)
    for p in range(pairs):
        sl=slice(p*128,(p+1)*128)
        out_ref[:,D+p*128:D+(p+1)*128]=(dkt[sl,:]*scale).T.astype(BF)
        out_ref[:,2*D+p*128:2*D+(p+1)*128]=dvt[sl,:].T.astype(BF)

def attn_bwd(q,k,v,g,o,lse,pen,seg):
    L,D=q.shape
    start=jnp.concatenate([(seg[:-1]!=seg[1:]).astype(jnp.int32),jnp.ones((1,),jnp.int32)])
    vm=pl.BlockSpec(memory_space=pltpu.VMEM)
    return pl.pallas_call(attn_bwd_kernel,
        out_shape=jax.ShapeDtypeStruct((L,3*D),BF),
        in_specs=[vm]*8,out_specs=vm,
        scratch_shapes=[pltpu.VMEM((D,L),BF),pltpu.VMEM((D,L),BF),pltpu.VMEM((D,L),F32),pltpu.VMEM((D,L),F32),pltpu.VMEM((BLOCK,L),F32)],
        compiler_params=pltpu.CompilerParams(vmem_limit_bytes=60*2**20),name="attn_bwd")(q,k,v,g,o,lse,pen,start[None,:])


def layer(tokens, segs, cotangent, weights, fused):
    (w_qkv, q_bias, v_bias, w_out, out_bias, attn_gain, attn_shift, mlp_gain, mlp_shift,
     w_up, up_bias, w_down, down_bias) = weights
    width = tokens.shape[-1]
    if fused:
        vectors = (q_bias, v_bias, out_bias, attn_gain, attn_shift, mlp_gain, mlp_shift, down_bias, up_bias)
        tokens, cotangent, queries, keys, values, attended, stats, penalty = front(tokens, cotangent, w_qkv, vectors, segs)
        output, grad_tokens, down, up, side, small = rest(
            attended, tokens, cotangent, queries, keys, values, stats, penalty, vectors, segs, w_qkv, w_out, w_up, w_down)[:6]
        return output, down, up, side, grad_tokens, small
    inputs = tokens.astype(F32)
    normal_one, scale_one = norm_parts(inputs)
    normed = (normal_one * attn_gain + attn_shift).astype(BF)
    projected = dot(normed, w_qkv)
    queries = (projected[:, :width] + q_bias).astype(BF)
    keys = projected[:, width : 2 * width].astype(BF)
    values = (projected[:, 2 * width :] + v_bias).astype(BF)
    attended, stats, penalty = attn_fwd(queries, keys, values, segs)
    residual = inputs + dot(attended, w_out) + out_bias
    normal_two, scale_two = norm_parts(residual)
    normed_two = (normal_two * mlp_gain + mlp_shift).astype(BF)
    upper = dot(normed_two, w_up) + up_bias
    act, gelu_back = jax.vjp(gelu_tanh, upper)
    act = act.astype(BF)
    output = (residual + dot(act, w_down) + down_bias).astype(BF)
    grad_top = cotangent.astype(F32)
    g_down_bias = jnp.sum(grad_top, axis=0)
    g_w_down = dot(act, cotangent, ((0,), (0,)))
    grad_upper = gelu_back(dot(cotangent, w_down, ((1,), (1,))))[0].astype(BF)
    g_up_bias = jnp.sum(grad_upper.astype(F32), axis=0)
    g_w_up = dot(normed_two, grad_upper, ((0,), (0,)))
    grad_two = dot(grad_upper, w_up, ((1,), (1,)))
    g_mlp_gain = jnp.sum(grad_two * normal_two, axis=0)
    g_mlp_shift = jnp.sum(grad_two, axis=0)
    grad_residual = grad_top + norm_back(grad_two, normal_two, scale_two, mlp_gain)
    grad_branch = grad_residual.astype(BF)
    g_out_bias = jnp.sum(grad_branch.astype(F32), axis=0)
    g_w_out = dot(attended, grad_branch, ((0,), (0,)))
    grad_attended = dot(grad_branch, w_out, ((1,), (1,))).astype(BF)
    grad_proj = attn_bwd(queries, keys, values, grad_attended, attended, stats, penalty, segs)
    bias_sums = jnp.sum(grad_proj.astype(F32), axis=0)
    g_q_bias = bias_sums[:width]
    g_v_bias = bias_sums[2 * width :]
    g_w_qkv = dot(normed, grad_proj, ((0,), (0,)))
    grad_one = dot(grad_proj, w_qkv, ((1,), (1,)))
    g_attn_gain = jnp.sum(grad_one * normal_one, axis=0)
    g_attn_shift = jnp.sum(grad_one, axis=0)
    grad_tokens = grad_residual + norm_back(grad_one, normal_one, scale_one, attn_gain)
    return output, grad_tokens, (
        g_w_qkv, g_q_bias, g_v_bias, g_w_out, g_out_bias, g_attn_gain, g_attn_shift,
        g_mlp_gain, g_mlp_shift, g_w_up, g_up_bias, g_w_down, g_down_bias)


def view(ref, tall, panel, row, rows, col, cols):
    if tall:
        return ref.at[pl.ds(pl.multiple_of(panel * PANEL + row, 16), rows), pl.ds(col, cols)]
    return ref.at[pl.ds(pl.multiple_of(row, 16), rows), pl.ds(pl.multiple_of(panel * PANEL + col, 128), cols)]


def add_into(dst, row, rows, parts):
    def turn(i, carry):
        at = pl.multiple_of(i * STEP, 16)
        here = pl.ds(pl.multiple_of(row + at, 16), STEP)
        total = dst[here, :].astype(F32)
        for part in parts:
            total = total + part[pl.ds(at, STEP), :].astype(F32)
        dst[here, :] = total.astype(BF)
        return carry

    lax.fori_loop(0, rows // STEP, turn, 0)


def rows_at(ref, row, rows):
    return ref.at[pl.ds(pl.multiple_of(row, 16), rows), :]


def remote(src, dst, sent, landed, device):
    return pltpu.make_async_remote_copy(
        src_ref=src, dst_ref=dst, send_sem=sent, recv_sem=landed, device_id=device, device_id_type=MESH
    )


class Place:
    def __init__(self):
        self.z, self.col = lax.axis_index("rows"), lax.axis_index("cols")
        z, col = self.z, self.col
        self.y, self.x, self.c = col // 4, (col // 2) % 2, col % 2
        y, x, c = self.y, self.x, self.c
        self.core = (z, y * 4 + x * 2 + (1 - c))
        self.across_x = (z, y * 4 + (1 - x) * 2 + c)
        self.across_y = (z, (1 - y) * 4 + x * 2 + c)
        self.along_z = [(lax.rem(z + d, 4), col) for d in range(1, 4)]
        self.along_cols = [(z, lax.rem(col + d, 8)) for d in range(1, 8)]

    def greet(self, devices):
        barrier = pltpu.get_barrier_semaphore()
        for device in devices:
            pl.semaphore_signal(barrier, inc=1, device_id=device, device_id_type=MESH)
        pl.semaphore_wait(barrier, len(devices))


class Chunk:
    def __init__(self, place, n, source, result, tall, first, buffers, sems):
        own, from_core, from_one, from_two, from_z = [b.at[n % SLOTS] for b in buffers]
        sent, landed, local = sems
        width = own.shape[-1]
        x, y, z, c = place.x, place.y, place.z, place.c
        S = lambda k: sent.at[n, k]
        R = lambda k: landed.at[n, k]
        src = lambda panel, row, rows: view(source, tall, panel, row, rows, first, width)
        out = lambda panel, row, rows: view(result, tall, panel, row, rows, first, width)
        near, far = [x, y], [y, x]
        to_near = [place.across_x, place.across_y]
        to_far = [place.across_y, place.across_x]
        half, quarter, piece = PANEL // 2, PANEL // 4, PANEL // 16
        both = range(2)
        self.own, self.from_core, self.from_one = own, from_core, from_one
        self.from_two, self.from_z = from_two, from_z
        self.half, self.quarter, self.piece = half, quarter, piece
        self.keep1 = [near[u] * half for u in both]
        self.send1 = [(1 - near[u]) * half for u in both]
        self.keep2 = [self.keep1[u] + far[u] * quarter for u in both]
        self.send2 = [self.keep1[u] + (1 - far[u]) * quarter for u in both]
        self.last = [self.keep2[u] + z * piece for u in both]
        final = lambda u: rows_at(own.at[u], self.last[u], piece)
        self.load = [pltpu.make_async_copy(src(2 * c + u, 0, PANEL), own.at[u], local.at[n, u]) for u in both]
        self.core = [remote(src(2 * (1 - c) + u, 0, PANEL), from_core.at[u], S(u), R(u), place.core) for u in both]
        self.one = [remote(rows_at(own.at[u], self.send1[u], half), from_one.at[u], S(2 + u), R(2 + u), to_near[u]) for u in both]
        self.two = [remote(rows_at(own.at[u], self.send2[u], quarter), from_two.at[u], S(4 + u), R(4 + u), to_far[u]) for u in both]
        self.deep = [[remote(rows_at(own.at[u], self.keep2[u] + dev[0] * piece, piece), from_z.at[u, d],
                             S(6 + 3 * u + d), R(6 + 3 * u + d), dev)
                      for d, dev in enumerate(place.along_z)] for u in both]
        self.store = [pltpu.make_async_copy(final(u), out(2 * c + u, self.last[u], piece), local.at[n, 2 + u]) for u in both]
        self.deep_back = [[remote(final(u), out(2 * c + u, self.last[u], piece), S(12 + 3 * u + d), R(12 + 3 * u + d), dev)
                           for d, dev in enumerate(place.along_z)] for u in both]
        same = lambda panel, row, rows, k, dev: remote(out(panel, row, rows), out(panel, row, rows), S(k), R(k), dev)
        self.two_back = [same(2 * c + u, self.keep2[u], quarter, 18 + u, to_far[u]) for u in both]
        self.one_back = [same(2 * c + u, self.keep1[u], half, 20 + u, to_near[u]) for u in both]
        self.core_back = [same(2 * c + u, 0, PANEL, 22 + u, place.core) for u in both]

    def begin(self):
        for copy in self.core + self.load:
            copy.start()

    def step(self, k):
        both = range(2)
        own = [self.own.at[u] for u in both]
        if k == 0:
            for u in both:
                self.load[u].wait()
                self.core[u].wait_recv()
                add_into(own[u], self.send1[u], self.half, [rows_at(self.from_core.at[u], self.send1[u], self.half)])
                self.one[u].start()
            for u in both:
                add_into(own[u], self.keep1[u], self.half, [rows_at(self.from_core.at[u], self.keep1[u], self.half)])
        elif k == 1:
            for u in both:
                self.one[u].wait_recv()
                add_into(own[u], self.send2[u], self.quarter, [rows_at(self.from_one.at[u], self.send2[u] - self.keep1[u], self.quarter)])
                self.two[u].start()
                add_into(own[u], self.keep2[u], self.quarter, [rows_at(self.from_one.at[u], self.keep2[u] - self.keep1[u], self.quarter)])
        elif k == 2:
            for u in both:
                self.two[u].wait_recv()
                add_into(own[u], self.keep2[u], self.quarter, [self.from_two.at[u]])
                for copy in self.deep[u]:
                    copy.start()
        elif k == 3:
            for u in both:
                for copy in self.deep[u]:
                    copy.wait_recv()
                add_into(own[u], self.last[u], self.piece, [self.from_z.at[u, d] for d in range(3)])
                for copy in self.deep_back[u]:
                    copy.start()
                self.store[u].start()
        elif k == 4:
            for u in both:
                for copy in self.deep_back[u]:
                    copy.wait_recv()
                self.store[u].wait()
                self.two_back[u].start()
        elif k == 5:
            for u in both:
                self.two_back[u].wait_recv()
                self.one_back[u].start()
        elif k == 6:
            for u in both:
                self.one_back[u].wait_recv()
                self.core_back[u].start()
        else:
            for u in both:
                self.core_back[u].wait_recv()
            for copy in (self.core + self.one + self.two + self.deep[0] + self.deep[1] + self.deep_back[0]
                         + self.deep_back[1] + self.two_back + self.one_back + self.core_back):
                copy.wait_send()


class Timeline:
    LINK = ["core", "plane", "plane", "deep", "deep", "plane", "plane", "core"]
    TAKES = [t * LAG * 2 / SPLIT for t in (2.5, 6.3, 3.2, 5.8, 5.8, 3.2, 6.3, 2.5)]
    WORK = [t * 2 / SPLIT for t in (2.0, 1.0, 0.5, 0.5, 0.1, 0.1, 0.1, 0.1)]

    def __init__(self):
        self.now = 0.0
        self.free = {"core": 0.0, "plane": 0.0, "deep": 0.0}
        self.moving = {}
        self.after_first = {}

    def occupy(self, link, takes):
        self.free[link] = max(self.free[link], self.now) + takes
        return self.free[link] + 2.0

    def begin(self, chunk, then=None):
        chunk.begin()
        self.moving[chunk] = (self.occupy(self.LINK[0], self.TAKES[0]), 0)
        self.after_first[chunk] = then

    def begin_all(self, chunks):
        self.begin(chunks[0], (lambda: self.begin_all(chunks[1:])) if chunks[1:] else None)

    def turn(self, chunk):
        done, k = self.moving.pop(chunk)
        self.now = max(self.now, done)
        chunk.step(k)
        self.now += self.WORK[k]
        if k < 7:
            self.moving[chunk] = (self.occupy(self.LINK[k + 1], self.TAKES[k + 1]), k + 1)
        if k == 0 and self.after_first[chunk]:
            self.after_first[chunk]()

    def ready(self):
        while self.moving:
            chunk = min(self.moving, key=lambda c: self.moving[c][0])
            if self.moving[chunk][0] > self.now:
                return
            self.turn(chunk)

    def worked(self, takes):
        self.now += takes
        self.ready()

    def complete(self, chunk):
        while chunk in self.moving:
            self.turn(min(self.moving, key=lambda c: self.moving[c][0]))

    def finish(self):
        while self.moving:
            self.turn(min(self.moving, key=lambda c: self.moving[c][0]))


class Homeward:
    def __init__(self, place, source, result, sent, landed, local):
        part = source.shape[0] // 8
        self.copies = [remote(rows_at(source, dev[1] * part, part), result.at[place.col], sent.at[i], landed.at[i], dev)
                       for i, dev in enumerate(place.along_cols)]
        self.own = pltpu.make_async_copy(rows_at(source, place.col * part, part), result.at[place.col], local)

    def start(self):
        for copy in self.copies:
            copy.start()
        self.own.start()

    def wait(self):
        for copy in self.copies:
            copy.wait()
        self.own.wait()


def fill_segments(seg_ref, all_ref, row):
    L = seg_ref.shape[1]
    ids = all_ref[pl.ds(row, 1), :]
    after = pltpu.roll(ids, L - 1, 1)
    lane = lax.broadcasted_iota(jnp.int32, (1, L), 1)
    seg_ref[0:1, :] = ids
    seg_ref[1:2, :] = jnp.where((ids != after) | (lane == L - 1), 1, 0)


def row_reader(refs):
    places = []
    for ref in refs:
        places += [(ref, i) for i in range(ref.shape[0] // PANEL)]

    def read(row):
        ref, i = places[row]
        return ref[i * PANEL : (i + 1) * PANEL].reshape(1, PANEL)

    return read


def front_kernel(tokens_ref, cot_ref, w_ref, seg_all, *refs):
    vectors, refs = refs[:9], refs[9:]
    front_body(row_reader(vectors), tokens_ref, cot_ref, w_ref, seg_all, *refs)


def front_body(vec, tokens_ref, cot_ref, w_ref, seg_all,
                 tokens_out, cot_out, q_ref, k_ref, v_ref, o_ref, lse_ref, pen_ref,
                 whole, w, seg_ref, sent, landed, local):
    L, D = q_ref.shape
    part = L // 8
    place = Place()
    z, y, x, c, col = place.z, place.y, place.x, place.c, place.col

    def other(k):
        flip = lambda bit, coord: 1 - coord if bit else coord
        return (z, flip(k & 4, y) * 4 + flip(k & 2, x) * 2 + flip(k & 1, c))

    place.greet([other(k) for k in range(1, 8)])
    mine = pl.multiple_of(col * part, 16)
    out = [remote(tokens_ref.at[other(k)[1]], rows_at(whole, mine, part), sent.at[0, k], landed.at[0, k], other(k))
           for k in range(1, 8)]
    own = pltpu.make_async_copy(tokens_ref.at[col], rows_at(whole, mine, part), local.at[0])
    load = pltpu.make_async_copy(w_ref, w, local.at[1])
    cots = [remote(cot_ref.at[other(k)[1]], rows_at(cot_out, mine, part), sent.at[1, k], landed.at[1, k], other(k))
            for k in range(1, 8)]
    cot_own = pltpu.make_async_copy(cot_ref.at[col], rows_at(cot_out, mine, part), local.at[2])
    keep = pltpu.make_async_copy(whole, tokens_out, local.at[3])
    own.start()
    fill_segments(seg_ref, seg_all, col)
    for copy in out:
        copy.start()
    load.start()
    cot_own.start()
    own.wait()
    load.wait()
    for chip in range(4):
        for k in (2 * chip, 2 * chip + 1):
            if k:
                out[k - 1].wait_recv()
        if chip == 3:
            for copy in cots:
                copy.start()
        first = other(2 * chip)[1] - c
        here = pl.ds(pl.multiple_of(first * part, 16), 2 * part)
        normal, _ = norm_parts(whole[here, :].astype(F32))
        normed = (normal * vec(ROW_GAIN1) + vec(ROW_SHIFT1)).astype(BF)
        q_ref[here, :] = (dot(normed, w[:, 0:D]) + vec(ROW_Q)).astype(BF)
        k_ref[here, :] = dot(normed, w[:, D : 2 * D]).astype(BF)
        v_ref[here, :] = (dot(normed, w[:, 2 * D : 3 * D]) + vec(ROW_V)).astype(BF)
    keep.start()
    attend(q_ref, k_ref, v_ref, seg_ref, o_ref, lse_ref, pen_ref)
    keep.wait()
    cot_own.wait()
    for copy in out:
        copy.wait_send()
    for copy in cots:
        copy.wait()


def front(tokens, cotangent, w_qkv, vectors, segs):
    cols, part, D = tokens.shape
    L = cols * part
    hbm = pl.BlockSpec(memory_space=pl.ANY)
    vm = pl.BlockSpec(memory_space=pltpu.VMEM)
    dma = pltpu.SemaphoreType.DMA
    rows = jax.ShapeDtypeStruct((L, D), BF)
    return pl.pallas_call(
        front_kernel,
        out_shape=(rows,) * 6 + (jax.ShapeDtypeStruct((L, 128), F32), jax.ShapeDtypeStruct((L, L), F32)),
        in_specs=[hbm] * 3 + [vm] * 10,
        out_specs=(hbm,) * 2 + (vm,) * 6,
        scratch_shapes=[pltpu.VMEM((L, D), BF), pltpu.VMEM((D, 3 * D), BF), pltpu.VMEM((2, L), jnp.int32), dma((2, 8)), dma((2, 8)), dma((4,))],
        compiler_params=pltpu.CompilerParams(vmem_limit_bytes=VMEM_LIMIT, collective_id=2, has_side_effects=True),
        name="front",
    )(tokens, cotangent, w_qkv, segs, *vectors)


ROW_Q, ROW_V, ROW_OUT, ROW_GAIN1, ROW_SHIFT1, ROW_GAIN2, ROW_SHIFT2, ROW_DOWN, ROW_UP = range(9)


def gelu_pair(u):
    slope = 0.7978845608028654
    square = u * u
    t = jnp.tanh(slope * u * (1.0 + 0.044715 * square))
    half = 0.5 * (1.0 + t)
    return u * half, half + (0.5 * slope) * u * (1.0 - t * t) * (1.0 + 3 * 0.044715 * square)


def rest_kernel(*refs):
    rest_body(row_reader(refs[:9]), *refs[9:])


def rest_body(vec, att_hbm, tok_hbm, cot_hbm, q_hbm, k_hbm, v_hbm, lse_hbm, pen_hbm, seg_all,
                w_qkv_hbm, w_out_hbm, w_up_hbm, w_down_hbm,
                output_out, tokens_out, down_out, up_out, side_out, small_out, down_part, up_part, out_part, res_part,
                seg_ref, tok, g, delta, sm_acc, sm_rec, own, from_core, from_one, from_two, from_z,
                sent, landed, local, home_s, home_r, home_l, sm_s, sm_r, in_s, stage_s, res_s, pen_s):
    L, D = tok.shape
    ff = w_up_hbm.shape[1]
    nb = L // BLOCK
    width = PANEL // SPLIT
    pairs = HEADS // 2
    place = Place()
    place.greet(place.along_cols + place.along_z)
    buffers, sems = (own, from_core, from_one, from_two, from_z), (sent, landed, local)
    chunks = []
    for source, result, tall in ((down_part, down_out, True), (up_part, up_out, False)):
        for j in range(SPLIT):
            chunks.append(Chunk(place, len(chunks), source, result, tall, j * width, buffers, sems))
    line = Timeline()
    fill_segments(seg_ref, seg_all, place.col)
    sm_acc[0] = jnp.zeros_like(sm_acc[0])

    def add_row(row, values):
        sm_acc[0, row : row + 1, :] += jnp.sum(values, axis=0, keepdims=True)

    def feed_forward(w_out, w_up, w_down, act, gu, n2t, gb, out, att, cot, res, stage):
        loads = [pltpu.make_async_copy(a, b, in_s.at[i]) for i, (a, b) in enumerate((
            (att_hbm, att), (tok_hbm, tok), (w_out_hbm, w_out), (cot_hbm, cot), (w_up_hbm, w_up), (w_down_hbm, w_down)))]
        for copy in loads:
            copy.start()
        features = lax.broadcasted_iota(jnp.int32, (D, 128), 0) // HDIM
        member = jnp.where(features == lax.broadcasted_iota(jnp.int32, (D, 128), 1), 1.0, 0.0).astype(BF)
        for copy in loads:
            copy.wait()

        def forward(b, carry):
            here = pl.ds(pl.multiple_of(b * ROWS, ROWS), ROWS)
            dy = cot[here, :]
            residual = tok[here, :].astype(F32) + dot(att[here, :], w_out[...]) + vec(ROW_OUT)
            res[here, :] = residual
            normal, _ = norm_parts(residual)
            n2 = (normal * vec(ROW_GAIN2) + vec(ROW_SHIFT2)).astype(BF)
            n2t[:, here] = n2.T
            add_row(ROW_DOWN, dy.astype(F32))
            total = residual + vec(ROW_DOWN)
            for j in range(ff // D):
                part = slice(j * D, (j + 1) * D)
                value, slope = gelu_pair(dot(n2, w_up[:, part]) + vec(ROW_UP + j))
                low = value.astype(BF)
                act[here, part] = low
                gu[here, part] = slope.astype(BF)
                total = total + dot(low, w_down[part, :])
            out[here, :] = total.astype(BF)
            return carry

        def backward(b):
            here = slice(b * ROWS, (b + 1) * ROWS)
            dy = cot[here, :]
            normal, spread = norm_parts(res[here, :])
            grad_two = jnp.zeros((ROWS, D), F32)
            for j in range(ff // D):
                part = slice(j * D, (j + 1) * D)
                grad = (dot(dy, w_down[part, :], NT) * gu[here, part].astype(F32)).astype(BF)
                gu[here, part] = grad
                add_row(ROW_UP + j, grad.astype(F32))
                grad_two = grad_two + dot(grad, w_up[:, part], NT)
            add_row(ROW_GAIN2, grad_two * normal)
            add_row(ROW_SHIFT2, grad_two)
            grad_residual = dy.astype(F32) + norm_back(grad_two, normal, spread, vec(ROW_GAIN2))
            res[here, :] = grad_residual
            branch = grad_residual.astype(BF)
            gb[here, :] = branch
            add_row(ROW_OUT, branch.astype(F32))
            grad_att = dot(branch, w_out[...], NT).astype(BF)
            g[here, :] = grad_att
            product = grad_att.astype(F32) * att[here, :].astype(F32)
            high = product.astype(BF)
            delta[here, :] = dot(high, member) + dot((product - high.astype(F32)).astype(BF), member)

        lax.fori_loop(0, L // ROWS, forward, 0)
        home = Homeward(place, out, output_out, home_s.at[0], home_r.at[0], home_l.at[0])
        home.start()
        line.occupy("plane", 16.0)
        tiles = ff // 256
        stored = [pltpu.make_async_copy(stage.at[i % 2], down_part.at[i * 256 : (i + 1) * 256, :], stage_s.at[i % 2])
                  for i in range(tiles)]
        for i in range(tiles):
            if i > 1:
                stored[i - 2].wait()
            stage[i % 2] = dot(act[:, i * 256 : (i + 1) * 256], cot[...], ((0,), (0,))).astype(BF)
            stored[i].start()
        stored[tiles - 2].wait()
        stored[tiles - 1].wait()
        line.worked(6.0)
        line.begin_all(chunks[:SPLIT])
        for b in range(L // ROWS):
            backward(b)
            line.worked(4.3)
        tiles = ff // D
        spread = [pltpu.make_async_copy(w_down.at[i * D : (i + 1) * D, :], up_part.at[:, i * D : (i + 1) * D], stage_s.at[2 + i])
                  for i in range(tiles)]
        for i in range(tiles):
            for j in range(D // 256):
                w_down[i * D : (i + 1) * D, j * 256 : (j + 1) * 256] = dot(n2t[...], gu[:, i * D + j * 256 : i * D + (j + 1) * 256]).astype(BF)
            spread[i].start()
            line.worked(1.6)
        w_out[...] = dot(att[...], gb[...], ((0,), (0,))).astype(BF)
        keep = [pltpu.make_async_copy(w_out, out_part, res_s.at[0]), pltpu.make_async_copy(res, res_part, res_s.at[1])]
        for copy in keep:
            copy.start()
        for copy in spread:
            copy.wait()
        line.worked(1.5)
        line.begin_all(chunks[SPLIT:])
        for copy in keep:
            copy.wait()
        home.wait()

    dma = pltpu.SemaphoreType.DMA
    pl.run_scoped(
        feed_forward, pltpu.VMEM((D, D), BF), pltpu.VMEM((D, ff), BF), pltpu.VMEM((ff, D), BF), pltpu.VMEM((L, ff), BF),
        pltpu.VMEM((L, ff), BF), pltpu.VMEM((D, L), BF), pltpu.VMEM((L, D), BF),
        pltpu.VMEM((L, D), BF), pltpu.VMEM((L, D), BF), pltpu.VMEM((L, D), BF), pltpu.VMEM((L, D), F32),
        pltpu.VMEM((2, 256, D), BF))

    def attention(q_ref, k_ref, v_ref, lse_ref, w_ref, qt, gt, dkt, dvt, dsum, pen, dqkv, side, gtok, gres):
        scale = HDIM**-0.5
        c = scale * LOG2E
        startr_ref = seg_ref.at[1:2]
        loads = [pltpu.make_async_copy(a, b, in_s.at[i]) for i, (a, b) in enumerate((
            (q_hbm, q_ref), (k_hbm, k_ref), (v_hbm, v_ref), (lse_hbm, lse_ref), (w_qkv_hbm, w_ref)))]
        pen_copies = [pltpu.make_async_copy(pen_hbm.at[b * BLOCK : (b + 1) * BLOCK, :], pen.at[b % 2], pen_s.at[b % 2])
                      for b in range(nb)]
        res_copies = [pltpu.make_async_copy(res_part.at[b * BLOCK : (b + 1) * BLOCK, :], gres.at[b % 2], res_s.at[b % 2])
                      for b in range(nb)]
        for copy in loads[:4]:
            copy.start()
        pen_copies[0].start()
        loads[4].start()
        out_copy = pltpu.make_async_copy(out_part, side.at[:, 3 * D : 4 * D], in_s.at[5])
        out_copy.start()
        dkt[...] = jnp.zeros_like(dkt)
        dvt[...] = jnp.zeros_like(dvt)
        for p in range(pairs):
            gt[p * 128 : (p + 1) * 128, :] = g[:, p * 128 : (p + 1) * 128].T
        for copy in loads[:4]:
            copy.wait()
        for p in range(pairs):
            qt[p * 128 : (p + 1) * 128, :] = q_ref[:, p * 128 : (p + 1) * 128].T
        line.worked(3.0)
        lower = tri(BLOCK, False)
        carry = jnp.zeros((1, L), F32)
        for b in range(nb):
            i0 = b * BLOCK
            n = L - i0
            rowsl = slice(i0, i0 + BLOCK)
            carry = carry[:, -n:]
            pen_copies[b].wait()
            if b + 1 < nb:
                pen_copies[b + 1].start()
            pen_b = pen.at[b % 2, :, i0:L]

            def head(p, h):
                off = p * 128 if isinstance(p, int) else pl.multiple_of(p * 128, 128)
                q = q_ref[rowsl, pl.ds(off, 128)]
                gh = g[rowsl, pl.ds(off, 128)]
                k = k_ref[i0:L, pl.ds(off, 128)]
                v = v_ref[i0:L, pl.ds(off, 128)]
                low = lane_low(q.shape)
                mine = low if h == 0 else jnp.logical_not(low)
                lane = lax.broadcasted_iota(jnp.int32, (BLOCK, 128), 1)
                lse = jnp.sum(jnp.where(lane == 2 * p + h, lse_ref[rowsl, :], 0.0), axis=1, keepdims=True)
                shift = jnp.sum(jnp.where(lane == 2 * p + h, delta[rowsl, :], 0.0), axis=1, keepdims=True)
                s = dot(jnp.where(mine, q, jnp.zeros_like(q)), k, NT)
                pr = jnp.exp2(s * c - pen_b[...] - lse)
                dp = dot(jnp.where(mine, gh, jnp.zeros_like(gh)), v, NT)
                return s, pr, pr * (dp - shift), off, k

            def finish(p, h, pr, ds, k):
                base = p * 128 + h * HDIM
                if not isinstance(p, int):
                    base = pl.multiple_of(base, 64)
                dsb = ds.astype(BF)
                dvt[pl.ds(base, HDIM), i0:L] += dot(gt[pl.ds(base, HDIM), rowsl], pr.astype(BF))
                dkt[pl.ds(base, HDIM), i0:L] += dot(qt[pl.ds(base, HDIM), rowsl], dsb)
                return dot(dsb, k)

            def pair(p, carry_):
                dq = []
                for h in range(2):
                    s, pr, ds, off, k = head(p, h)
                    dsum[:, i0:L] += ds
                    dq.append(finish(p, h, pr, ds, k))
                dqkv[rowsl, pl.ds(off, 128)] = (jnp.where(lane_low(dq[0].shape), dq[0], dq[1]) * scale).astype(BF)
                return carry_

            dsum[:, i0:L] = jnp.zeros((BLOCK, n), F32)
            each = 0.42 * (BLOCK // 256) * (n // 256)
            for begin, end in ((1, 3), (3, pairs)) if b < 2 else ((1, pairs),):
                lax.fori_loop(begin, end, pair, 0)
                line.worked(each * (end - begin))
            s, pr, ds, off, k = head(0, 1)
            dsum[:, i0:L] += ds
            dq1 = finish(0, 1, pr, ds, k)
            s, pr, ds, off, k = head(0, 0)
            total = dsum[:, i0:L] + ds
            rows = i0 + lax.broadcasted_iota(jnp.int32, (BLOCK, n), 0)
            cols = i0 + lax.broadcasted_iota(jnp.int32, (BLOCK, n), 1)
            picked = (pen_b[...] < 1e29) & (cols > rows) & (startr_ref[0:1, i0:L] == 0) & (s > 0)
            gsel = (split_sum(lower, total) + carry) * (-8.0 / L)
            carry = carry + jnp.sum(total, axis=0, keepdims=True)
            ds = ds + jnp.where(picked, gsel, 0.0)
            dq0 = finish(0, 0, pr, ds, k)
            dqkv[rowsl, 0:128] = (jnp.where(lane_low(dq0.shape), dq0, dq1) * scale).astype(BF)
            line.worked(each * 1.2)
        for p in range(pairs):
            sl = slice(p * 128, (p + 1) * 128)
            dqkv[:, D + p * 128 : D + (p + 1) * 128] = (dkt[sl, :] * scale).T.astype(BF)
            dqkv[:, 2 * D + p * 128 : 2 * D + (p + 1) * 128] = dvt[sl, :].T.astype(BF)

        def normal_of(b):
            return norm_parts(tok[b * BLOCK : (b + 1) * BLOCK, :].astype(F32))

        for b in range(nb):
            normal, _ = normal_of(b)
            normed = (normal * vec(ROW_GAIN1) + vec(ROW_SHIFT1)).astype(BF)
            for p in range(pairs):
                qt[p * 128 : (p + 1) * 128, b * BLOCK : (b + 1) * BLOCK] = normed[:, p * 128 : (p + 1) * 128].T
        line.worked(3.0)
        out_copy.wait()
        for j in range(SPLIT):
            for panel in range(3):
                at = slice(panel * D + j * width, panel * D + (j + 1) * width)
                side[:, at] = dot(qt[...], dqkv[:, at]).astype(BF)
            line.now += 5.0 / SPLIT
            line.complete(chunks[j])
            line.begin(Chunk(place, 2 * SPLIT + j, side, side_out, False, j * width, buffers, sems))
            line.ready()
        sm_acc[0, 0:1, :] = jnp.sum(dqkv[:, 0:D].astype(F32), axis=0, keepdims=True)
        sm_acc[0, 1:2, :] = jnp.sum(dqkv[:, 2 * D : 3 * D].astype(F32), axis=0, keepdims=True)
        res_copies[0].start()
        loads[4].wait()
        g_gain = jnp.zeros((1, D), F32)
        g_shift = jnp.zeros((1, D), F32)
        for b in range(nb):
            rowsl = slice(b * BLOCK, (b + 1) * BLOCK)
            if b + 1 < nb:
                res_copies[b + 1].start()
            normal, spread = normal_of(b)
            grad = dot(dqkv[rowsl, :], w_ref[...], NT)
            g_gain = g_gain + jnp.sum(grad * normal, axis=0, keepdims=True)
            g_shift = g_shift + jnp.sum(grad, axis=0, keepdims=True)
            back = norm_back(grad, normal, spread, vec(ROW_GAIN1))
            res_copies[b].wait()
            gtok[rowsl, :] = (gres[b % 2] + back).astype(BF)
            line.worked(2.0)
        tokens_home = Homeward(place, gtok, tokens_out, home_s.at[1], home_r.at[1], home_l.at[1])
        tokens_home.start()
        line.occupy("plane", 16.0)
        sm_acc[0, 3:4, :] = g_gain
        sm_acc[0, 4:5, :] = g_shift
        z, col = place.z, place.col
        friends = [place.core, place.across_x, place.across_y, (z + 1 - 2 * (z % 2), col), (lax.rem(z + 2, 4), col)]
        smalls = [remote(sm_acc.at[i], sm_rec.at[i], sm_s.at[i], sm_r.at[i], friends[i]) for i in range(5)]
        smalls[0].start()
        for i in range(5):
            line.worked(4.0)
            smalls[i].wait_recv()
            following = sm_acc[i] + sm_rec[i]
            if i < 4:
                sm_acc[i + 1] = following
                smalls[i + 1].start()
            else:
                small_out[...] = following
        line.finish()
        for copy in smalls:
            copy.wait_send()
        tokens_home.wait()

    pl.run_scoped(
        attention, pltpu.VMEM((L, D), BF), pltpu.VMEM((L, D), BF), pltpu.VMEM((L, D), BF), pltpu.VMEM((L, 128), F32),
        pltpu.VMEM((D, 3 * D), BF), pltpu.VMEM((D, L), BF), pltpu.VMEM((D, L), BF), pltpu.VMEM((D, L), F32),
        pltpu.VMEM((D, L), F32), pltpu.VMEM((BLOCK, L), F32), pltpu.VMEM((2, BLOCK, L), F32), pltpu.VMEM((L, 3 * D), BF),
        pltpu.VMEM((D, 4 * D), BF), pltpu.VMEM((L, D), BF), pltpu.VMEM((2, BLOCK, D), F32))


def rest(attended, tokens, cotangent, q, k, v, lse, pen, vectors, segs, w_qkv, w_out, w_up, w_down):
    L, D = attended.shape
    ff = w_up.shape[1]
    N, W = 3 * SPLIT, PANEL // SPLIT
    hbm = pl.BlockSpec(memory_space=pl.ANY)
    vm = pl.BlockSpec(memory_space=pltpu.VMEM)
    dma = pltpu.SemaphoreType.DMA
    shape = jax.ShapeDtypeStruct
    rows = shape((8, L // 8, D), BF)
    wide, tall = shape((D, ff), BF), shape((ff, D), BF)
    return pl.pallas_call(
        rest_kernel,
        out_shape=(rows, rows, tall, wide, wide, shape((16, D), F32), tall, wide, shape((D, D), BF), shape((L, D), F32)),
        in_specs=[vm] * 9 + [hbm] * 8 + [vm] + [hbm] * 4,
        out_specs=(hbm,) * 5 + (vm,) + (hbm,) * 4,
        scratch_shapes=[
            pltpu.VMEM((2, L), jnp.int32), pltpu.VMEM((L, D), BF), pltpu.VMEM((L, D), BF), pltpu.VMEM((L, 128), F32), pltpu.VMEM((5, 16, D), F32),
            pltpu.VMEM((5, 16, D), F32), pltpu.VMEM((SLOTS, 2, PANEL, W), BF), pltpu.VMEM((SLOTS, 2, PANEL, W), BF),
            pltpu.VMEM((SLOTS, 2, PANEL // 2, W), BF), pltpu.VMEM((SLOTS, 2, PANEL // 4, W), BF),
            pltpu.VMEM((SLOTS, 2, 3, PANEL // 16, W), BF),
            dma((N, 24)), dma((N, 24)), dma((N, 4)), dma((2, 7)), dma((2, 7)), dma((2,)), dma((5,)), dma((5,)),
            dma((6,)), dma((6,)), dma((2,)), dma((2,)),
        ],
        compiler_params=pltpu.CompilerParams(vmem_limit_bytes=VMEM_LIMIT, collective_id=1, has_side_effects=True),
        name="rest",
    )(*vectors, attended, tokens, cotangent, q, k, v, lse, pen, segs, w_qkv, w_out, w_up, w_down)


def widen_kernel(tok_in, down_in, up_in, side_in, small_in, tok_out, down_out, up_out, qkv_out, out_out, *vectors):
    @pl.when(pl.program_id(0) == 0)
    def _():
        row = 0
        for ref in vectors:
            for i in range(ref.shape[0] // PANEL):
                ref[i * PANEL : (i + 1) * PANEL] = small_in[row : row + 1, :].reshape(PANEL)
                row += 1

    tok_out[...] = tok_in[...].astype(F32)
    down_out[...] = down_in[...].astype(F32)
    up_out[...] = up_in[...].astype(F32)
    split = qkv_out.shape[1]
    qkv_out[...] = side_in[:, :split].astype(F32)
    out_out[...] = side_in[:, split:].astype(F32)


def widen(tok, down, up, side, small):
    parts, part, D = tok.shape
    steps = 2 * parts
    block = lambda a: pl.BlockSpec((a[0] // steps, a[1]), lambda i: (i, 0))
    tok_spec = pl.BlockSpec((1, part // 2, D), lambda i: (i // 2, i % 2, 0))
    shapes = [down.shape, up.shape, (D, 3 * D), (D, D)]
    vectors = [(D,)] * 8 + [(4 * D,)]
    return pl.pallas_call(
        widen_kernel,
        grid=(steps,),
        out_shape=[jax.ShapeDtypeStruct(a, F32) for a in [tok.shape] + shapes + vectors],
        in_specs=[tok_spec, block(down.shape), block(up.shape), block(side.shape), pl.BlockSpec(small.shape, lambda i: (0, 0))],
        out_specs=[tok_spec] + [block(a) for a in shapes] + [pl.BlockSpec(a, lambda i: (0,)) for a in vectors],
        compiler_params=pltpu.CompilerParams(vmem_limit_bytes=VMEM_LIMIT),
        name="widen",
    )(tok, down, up, side, small)


def summed_grads(grads, copies):
    grads = [g / copies for g in grads]
    matrices = [i for i, g in enumerate(grads) if g.ndim == 2]
    vectors = [i for i, g in enumerate(grads) if g.ndim == 1]
    big = lax.psum([grads[i].astype(BF) for i in matrices], ("rows", "cols"))
    small = lax.psum(jnp.concatenate([grads[i] for i in vectors]), ("rows", "cols"))
    out = [None] * len(grads)
    for i, g in zip(matrices, big):
        out[i] = g.astype(F32)
    at = 0
    for i in vectors:
        out[i] = small[at : at + grads[i].shape[0]]
        at += grads[i].shape[0]
    return out


def per_device(tokens, segment_ids, cotangent, *weights):
    seqs, part, width = tokens.shape
    cols = lax.axis_size("cols")
    fitting = (lax.axis_size("rows"), cols, seqs) == (4, 8, 8)
    copies = max(1, cols // seqs)
    held = max(1, seqs // cols)
    first = (lax.axis_index("cols") // copies) * held
    segs = lax.dynamic_slice_in_dim(segment_ids, first, held, 0)
    if fitting:
        output, down, up, side, grad_tokens, small = layer(tokens, segment_ids, cotangent, weights, True)
        grad_tokens, g_w_down, g_w_up, g_w_qkv, g_w_out, *vectors = widen(grad_tokens, down, up, side, small)
        return (
            output, grad_tokens, g_w_qkv, vectors[ROW_Q], vectors[ROW_V], g_w_out, vectors[ROW_OUT], vectors[ROW_GAIN1],
            vectors[ROW_SHIFT1], vectors[ROW_GAIN2], vectors[ROW_SHIFT2], g_w_up, vectors[ROW_UP], g_w_down,
            vectors[ROW_DOWN])
    tokens_whole = to_whole(tokens, copies)
    cotangent_whole = to_whole(cotangent, copies)
    results = [
        layer(tokens_whole[s], segs[s], cotangent_whole[s], weights, False) for s in range(held)
    ]
    output = jnp.stack([r[0] for r in results])
    grad_tokens = jnp.stack([r[1] for r in results])
    grads = [sum(parts[1:], parts[0]) for parts in zip(*[r[2] for r in results])]
    return (
        to_parts(output, copies),
        to_parts(grad_tokens.astype(BF), copies).astype(F32),
        *summed_grads(grads, copies),
    )


def solution(mesh):
    placed = (P("rows", "cols", None), P("rows", None), P("rows", "cols", None)) + (P(),) * 13
    return jax.shard_map(
        per_device,
        mesh=mesh,
        in_specs=placed,
        out_specs=(P("rows", "cols", None), P("rows", "cols", None)) + (P(),) * 13,
        check_vma=False,
    )
```
